32 devices in a mesh: row: 4 (over y, x), col: 8 (over z, core).
Axes of the slice: x: 2, y: 2, z: 4, core: 2. Of those that a mesh axis runs over, the one named last changes fastest.
Arguments:
- density: bfloat16 [2048, 2048], P('row', 'col'), as said below
- pattern: int32 [16, 16], replicated, may hold values from 0 to 1, as said below
Outputs:
- square: bfloat16 [2048, 2048], P('row', 'col')
- traces: float32 [2], replicated
The draws below stay inside these ranges and needn't reach their ends.
Inputs may be any that keep to these rules, and one draw needn't show every extreme that they name: Every diagonal block of 128 x 128 entries of density is symmetric. `pattern`: block (0, 15) is always stored.
All inputs are finite; a program needn't handle non-finite values.
Results may differ from the reference program's by a relative error of at most 0.0013.
Values may be sent and summed in bfloat16 or wider, within the bound.
No kernel may reach another device: no remote copies, remote signals or barrier semaphores. Data moves between devices by JAX's collectives and lax.ppermute only.
A program may use at most 64 MiB of HBM per device.

```python
import math
import jax
import jax.numpy as jnp

BLK = 128
NB = 16
N = 2048


def draw_density(key, part):
    key_off, key_diag = jax.random.split(jax.random.fold_in(key, 11), 2)
    base = jax.random.normal(key_off, (N, N), jnp.float32)
    index_ids = jnp.arange(N)
    block_ids = index_ids // BLK
    same_block = block_ids[:, None] == block_ids[None, :]
    sym_part = (base + base.T) * math.sqrt(0.5)
    entries = jnp.where(same_block, sym_part, base) * math.sqrt(2.0 / N)
    on_diag = index_ids[:, None] == index_ids[None, :]
    scaled = entries
    diag_vals = jax.random.uniform(key_diag, (N,), jnp.float32, 0.1, 0.9)
    result = jnp.where(on_diag, diag_vals[:, None] * jnp.ones((1, N), jnp.float32), scaled)
    return result.astype(jnp.bfloat16)


def draw_pattern(key, part):
    key = jax.random.fold_in(key, 23)
    values = jax.random.randint(key, (NB, NB), 0, 2).astype(jnp.int32)
    return values.at[0, NB - 1].set(1)


def setup_inputs(seed: int = 0) -> dict:
    keys = jax.random.split(jax.random.key(seed), 3)
    density = draw_density(jax.random.fold_in(keys[2], 71), 0)
    pattern = draw_pattern(jax.random.fold_in(keys[2], 71), 0)
    return {"density": density, "pattern": pattern}


def expand(block_mask):
    return jnp.repeat(jnp.repeat(block_mask, BLK, axis=0), BLK, axis=1)


def reference(density, pattern):
    block_ids = jnp.arange(NB)
    diagonal_blk = block_ids[:, None] == block_ids[None, :]
    above = block_ids[None, :] >= block_ids[:, None]
    kept_blocks = ((pattern != 0) | diagonal_blk) & above
    strict_blocks = kept_blocks & jnp.logical_not(diagonal_blk)
    zeros_like = jnp.zeros_like(density)
    stored = jnp.where(expand(kept_blocks), density, zeros_like)
    lower_part = jnp.where(expand(strict_blocks), density, zeros_like).T
    full_matrix = stored + lower_part
    product = jnp.dot(full_matrix, full_matrix, preferred_element_type=jnp.float32)
    trace_first = jnp.sum(jnp.diagonal(full_matrix).astype(jnp.float32))
    trace_second = jnp.sum(jnp.diagonal(product))
    square = jnp.where(expand(kept_blocks), product, jnp.zeros_like(product)).astype(jnp.bfloat16)
    traces = jnp.stack([trace_first, trace_second]) / N
    return square, traces
```

```python
import functools
import jax
import jax.numpy as jnp
from jax import lax
from jax.experimental import pallas as pl
from jax.experimental.pallas import tpu as pltpu
from jax.sharding import PartitionSpec as P

BLK = 128
VMEM = pl.BlockSpec(memory_space=pltpu.VMEM)
SMEM = pl.BlockSpec(memory_space=pltpu.SMEM)
PARAMS = pltpu.CompilerParams(vmem_limit_bytes=40 * 2**20)


def symmetric_kernel(sub, place, pattern, density, *rest):
    pieces, full = rest[:sub], rest[sub]
    row, col = place[0], place[1]
    height, width = density.shape
    per_piece = width // BLK
    row_blocks = height // BLK
    own_slot = lax.rem(col, sub)
    on_diagonal = row == col // sub
    for t in range(sub):
        slot = lax.rem(own_slot + sub - t, sub)
        for a in range(per_piece):
            i = slot * per_piece + a
            block_row = row * row_blocks + i
            rows = pl.ds(pl.multiple_of(i * BLK, BLK), BLK)
            for b in range(per_piece):
                block_col = col * per_piece + b
                cols = pl.ds(b * BLK, BLK)
                mirror = pieces[t][b * BLK : (b + 1) * BLK, a * BLK : (a + 1) * BLK]
                if t == 0:
                    start = pl.multiple_of((own_slot * per_piece + b) * BLK, BLK)
                    mine = density[pl.ds(start, BLK), a * BLK : (a + 1) * BLK]
                    mirror = jnp.where(on_diagonal, mine, mirror)
                chosen = pattern[jnp.minimum(block_row, block_col), jnp.maximum(block_row, block_col)] != 0
                upper = (block_row == block_col) | ((block_row < block_col) & chosen)
                lower = (block_row > block_col) & chosen
                zero = jnp.zeros((BLK, BLK), full.dtype)
                value = jnp.where(lower, mirror.T, zero)
                full[rows, cols] = jnp.where(upper, density[rows, cols], value)


def product_kernel(lines, planes, place, pattern, *refs):
    left = refs[: 2 * lines]
    right = refs[2 * lines : 2 * lines + planes]
    out, panel = refs[2 * lines + planes :]
    row, col = place[0], place[1]
    height, width = out.shape
    core, line = lax.rem(col, 2), col // 2
    for d in range(planes):
        start = pl.multiple_of((row ^ d) * height, height)
        panel[pl.ds(start, height), :] = right[d][...]
    total = jnp.zeros((height, width), jnp.float32)
    for e in range(lines):
        for s in range(2):
            start = pl.multiple_of(((line ^ e) * 2 + (core ^ s)) * width, width)
            total += jnp.dot(
                left[2 * e + s][...],
                panel[pl.ds(start, width), :],
                preferred_element_type=jnp.float32,
            )
    for i in range(height // BLK):
        for j in range(width // BLK):
            block_row = row * (height // BLK) + i
            block_col = col * (width // BLK) + j
            kept = (block_row == block_col) | ((block_row < block_col) & (pattern[block_row, block_col] != 0))
            block = total[i * BLK : (i + 1) * BLK, j * BLK : (j + 1) * BLK]
            out[i * BLK : (i + 1) * BLK, j * BLK : (j + 1) * BLK] = jnp.where(
                kept, block, jnp.zeros_like(block)
            ).astype(out.dtype)


def block_weights(pattern, row, col, row_blocks, col_blocks):
    block_rows = row * row_blocks + jnp.arange(row_blocks)
    block_cols = col * col_blocks + jnp.arange(col_blocks)
    chosen = lax.dynamic_slice(pattern, (row * row_blocks, col * col_blocks), (row_blocks, col_blocks))
    diagonal = block_rows[:, None] == block_cols[None, :]
    strict = (block_cols[None, :] > block_rows[:, None]) & (chosen != 0)
    return jnp.where(diagonal, 1.0, jnp.where(strict, 2.0, 0.0)).astype(jnp.float32)


def any_mesh(density, pattern):
    n_row = lax.axis_size("row")
    n_col = lax.axis_size("col")
    sub = n_col // n_row
    row = lax.axis_index("row")
    col = lax.axis_index("col")
    height, width = density.shape
    order_size = width * n_col
    place = jnp.stack([row, col]).astype(jnp.int32)

    pieces = []
    for t in range(sub):
        pairs = []
        for q in range(n_row):
            for c in range(n_col):
                p = (c + t) % sub
                if c > q * sub + p:
                    pairs.append((q * n_col + c, (c // sub) * n_col + q * sub + p))
        start = lax.rem(col + t, sub) * width
        piece = lax.dynamic_slice_in_dim(density, start, width, 0)
        pieces.append(lax.ppermute(piece, ("row", "col"), pairs))
    full = pl.pallas_call(
        functools.partial(symmetric_kernel, sub),
        out_shape=jax.ShapeDtypeStruct(density.shape, density.dtype),
        in_specs=[SMEM, SMEM] + [VMEM] * (sub + 1),
        out_specs=VMEM,
        compiler_params=PARAMS,
    )(place, pattern, density, *pieces)

    weights = block_weights(pattern, row, col, height // BLK, width // BLK)
    values = density.astype(jnp.float32).reshape(height // BLK, BLK, width // BLK, BLK)
    squares = jnp.sum(values * values, axis=(1, 3))
    rows_at = row * height + jnp.arange(height)[:, None]
    cols_at = col * width + jnp.arange(width)[None, :]
    diagonal = jnp.where(rows_at == cols_at, density.astype(jnp.float32), 0.0)
    sums = jnp.stack([jnp.sum(diagonal), jnp.sum(jnp.where(weights > 0, weights * squares, 0.0))])
    step = 1
    while step < n_row:
        sums = sums + lax.ppermute(sums, "row", [(i, i ^ step) for i in range(n_row)])
        step *= 2
    step = 1
    while step < n_col:
        sums = sums + lax.ppermute(sums, "col", [(i, i ^ step) for i in range(n_col)])
        step *= 2
    traces = sums / order_size

    right = [full]
    for d in range(1, n_row):
        right.append(lax.ppermute(full, "row", [(i, i ^ d) for i in range(n_row)]))
    left = []
    for e in range(n_col // 2):
        shard = full
        if e > 0:
            shard = lax.ppermute(full, "col", [(i, i ^ (2 * e)) for i in range(n_col)])
        other = lax.ppermute(shard, "col", [(i, i ^ 1) for i in range(n_col)])
        left += [shard, other]
    square = pl.pallas_call(
        functools.partial(product_kernel, n_col // 2, n_row),
        out_shape=jax.ShapeDtypeStruct(density.shape, density.dtype),
        in_specs=[SMEM, SMEM] + [VMEM] * (len(left) + len(right)),
        out_specs=VMEM,
        scratch_shapes=[pltpu.VMEM((order_size, width), density.dtype)],
        compiler_params=PARAMS,
    )(place, pattern, *left, *right)
    return (square, traces)

GRID_PARAMS = pltpu.CompilerParams(vmem_limit_bytes=14 * 2**20)
USES = 8
FIRST = 5
SECOND = 3
SUMS = 2 + SECOND
BASE = SUMS + 2 * FIRST
SEEN = ((), (0,), (1, 3), (2,))

MESSAGES = (
    (0, (0, 0), 1, (0, 0, 1), (0, 3, 1)),
    (0, (0, 2), 0, (0, 1, 0), (0, 0, 0)),
    (0, (0, 1), 1, (0, 1, 1), (1, 2, 0)),
    (0, (0, 1), 0, (0, 2, 0), (0, 3, 0)),
    (0, (2, 3), 0, (0, 3, 0), (1, 3, 1)),
    (0, (2, 3), 1, (0, 3, 1), (1, 2, 1)),
    (0, (1, 3), 1, (1, 2, 1), (0, 1, 1)),
    (0, (1, 3), 0, (1, 3, 0), (0, 1, 0)),
    (0, (1, 2), 1, (1, 3, 1), (2, 3, 0)),
    (0, (0, 3), 0, (2, 3, 0), (3, 3, 0)),
    (0, (0, 3), 1, (2, 3, 1), (3, 3, 1)),
    (0, (1, 1), 0, (3, 1, 0), (1, 3, 0)),
    (0, (1, 2), 0, (3, 2, 0), (2, 2, 0)),
    (0, (1, 3), 0, (3, 3, 0), (1, 1, 1)),
    (0, (1, 3), 1, (3, 3, 1), (2, 3, 1)),
    (1, (0, 3), 1, (0, 2, 1), (0, 1, 0)),
    (1, (1, 3), 0, (0, 3, 0), (2, 3, 0)),
    (1, (2, 3), 1, (0, 3, 1), (0, 2, 0)),
    (1, (0, 0), 1, (1, 0, 1), (0, 2, 1)),
    (1, (0, 1), 0, (1, 1, 0), (1, 3, 0)),
    (1, (1, 1), 1, (1, 2, 1), (1, 3, 1)),
    (1, (3, 3), 0, (1, 3, 0), (0, 3, 0)),
    (1, (1, 2), 1, (1, 3, 1), (2, 2, 1)),
    (1, (0, 1), 0, (2, 1, 0), (1, 2, 0)),
    (1, (0, 2), 0, (2, 2, 0), (2, 3, 1)),
    (1, (0, 2), 1, (2, 2, 1), (0, 0, 1)),
    (1, (0, 3), 0, (2, 3, 0), (0, 1, 1)),
    (1, (3, 3), 1, (2, 3, 1), (0, 3, 1)),
    (1, (2, 2), 1, (3, 2, 1), (1, 2, 1)),
    (2, (0, 0), 0, (0, 0, 0), (0, 3, 1)),
    (2, (2, 2), 0, (0, 2, 0), (1, 2, 0)),
    (2, (0, 3), 1, (0, 2, 1), (0, 0, 1)),
    (2, (0, 3), 0, (0, 3, 0), (0, 0, 0)),
    (2, (0, 2), 1, (0, 3, 1), (2, 3, 1)),
    (2, (1, 2), 0, (1, 1, 0), (0, 1, 1)),
    (2, (0, 1), 1, (1, 1, 1), (1, 3, 0)),
    (2, (1, 3), 1, (1, 2, 1), (1, 1, 1)),
    (2, (1, 2), 0, (1, 3, 0), (2, 3, 0)),
    (2, (0, 0), 0, (2, 0, 0), (0, 2, 0)),
    (2, (0, 1), 1, (2, 1, 1), (0, 3, 0)),
    (2, (2, 3), 0, (2, 2, 0), (0, 2, 1)),
    (2, (2, 3), 1, (2, 3, 1), (1, 3, 1)),
    (2, (1, 2), 1, (3, 2, 1), (0, 1, 0)),
    (2, (2, 3), 0, (3, 3, 0), (1, 2, 1)),
)


def wanted(r, z):
    if r > z:
        return [None] * USES
    return [(min(r, j), max(r, j)) for j in range(4)] + [(min(z, j), max(z, j)) for j in range(4)]


def first_round(devices):
    def ring(r, z, k, up):
        step = 1 if (k == 0) == up else -1
        return (r, z + step, k) if 0 <= z + step < 4 else (r, z, 1 - k)

    return [[(d, ring(*d, up)) for d in devices] for up in (True, False)] + [
        [((r, z, k), (r ^ bit, z, k)) for r, z, k in devices] for bit in (1, 2)
    ]


def closed(pairs, devices):
    def hops(a, b):
        return abs(a[1] - b[1]) + bin(a[0] ^ b[0]).count("1")

    sends, receives = {a for a, _ in pairs}, {b for _, b in pairs}
    free = sorted((hops(a, b), a, b) for a in devices for b in devices if a not in sends and b not in receives and a != b)
    extra = []
    for _, a, b in free:
        if a not in sends and b not in receives:
            sends.add(a)
            receives.add(b)
            extra.append((a, b))
    return pairs + extra


def schedule():
    devices = [(r, z, k) for r in range(4) for z in range(4) for k in range(2)]
    first = first_round(devices)
    held = {d: [((d[0], d[1]), d[2])] for d in devices}
    for pairs in first:
        for a, b in pairs:
            held[b].append(((a[0], a[1]), a[2]))
    second = [[] for _ in range(SECOND)]
    later = {d: [None] * SECOND for d in devices}
    sends = {d: [-1] * SECOND for d in devices}
    for i, tile, half, a, b in MESSAGES:
        second[i].append((a, b))
        sends[a][i] = held[a].index((tile, half))
        later[b][i] = (tile, half)
    second = [closed(pairs, devices) for pairs in second]
    rows = []
    for r, z, k in devices:
        row = [r, 2 * z + k] + sends[r, z, k]
        added = {(r, z), (r ^ 1, z), (r ^ 2, z)} | {(r, j) for j in SEEN[z]}
        for s, (tile, half) in enumerate(held[r, z, k]):
            ours = tile in added and half == k and (s == 0 or tile != (r, z))
            row += [tile[0], 2 * tile[1] + half] if ours else [-1, -1]
        taken = set()
        for shards in (held, later):
            here = shards[r, z, k] + shards[r, z, 1 - k]
            halves = [[], []]
            for u, tile in enumerate(wanted(r, z)):
                found = tile and u not in taken and (tile, 0) in here and (tile, 1) in here
                if found:
                    taken.add(u)
                for h in range(2):
                    halves[h].append(here.index((tile, h)) if found else -1)
            row += halves[0] + halves[1]
        assert r > z or len(taken) == USES
        rows.append(row)

    def flat(pairs):
        assert len({a for a, _ in pairs}) == len({b for _, b in pairs}) == len(devices)
        return [(8 * a[0] + 2 * a[1] + a[2], 8 * b[0] + 2 * b[1] + b[2]) for a, b in pairs]

    return [flat(p) for p in first], [flat(p) for p in second], rows


class Scalars:
    def __init__(self, info, rows):
        self.info, self.rows, self.width = info, rows, info.shape[1]

    def plan(self, i):
        return self.info[i // self.width, i % self.width] if isinstance(i, int) else self.info[
            lax.div(i, self.width), lax.rem(i, self.width)
        ]

    def kept(self, i, j):
        low, high = jnp.minimum(i, j), jnp.maximum(i, j)
        return (low == high) | (self.info[self.rows + low, high] != 0)


def partial_kernel(rows, info, *refs):
    scalars = Scalars(info, rows)
    shards, out, squares, diagonals = refs[:FIRST], refs[FIRST], refs[FIRST + 1], refs[FIRST + 2]
    squares[...] = jnp.zeros_like(squares)
    diagonals[...] = jnp.zeros_like(diagonals)
    for s, ref in enumerate(shards):
        row, col = scalars.plan(SUMS + 2 * s), scalars.plan(SUMS + 2 * s + 1)
        row_blocks, col_blocks = ref.shape[0] // BLK, ref.shape[1] // BLK

        @pl.when((row >= 0) & (row <= col // 2))
        def _():
            zero = jnp.zeros((BLK, BLK), jnp.float32)
            total = zero
            for a in range(row_blocks):
                for b in range(col_blocks):
                    i, j = row * row_blocks + a, col * col_blocks + b
                    block = ref[a * BLK : (a + 1) * BLK, b * BLK : (b + 1) * BLK].astype(jnp.float32)
                    block = jnp.where((i <= j) & scalars.kept(i, j), block, zero)
                    total += jnp.where(i == j, 1.0, 2.0) * (block * block)
            squares[...] += total

            @pl.when(row == col // 2)
            def _():
                rows_at = lax.broadcasted_iota(jnp.int32, (BLK, BLK), 0)
                cols_at = lax.broadcasted_iota(jnp.int32, (BLK, BLK), 1)
                for b in range(col_blocks):
                    start = pl.multiple_of((lax.rem(col, 2) * col_blocks + b) * BLK, BLK)
                    block = ref[pl.ds(start, BLK), b * BLK : (b + 1) * BLK].astype(jnp.float32)
                    diagonals[...] += jnp.where(rows_at == cols_at, block, zero)

    at_col = lax.broadcasted_iota(jnp.int32, out.shape, 1)
    out[...] = jnp.where(
        at_col == 0, jnp.sum(diagonals[...]), jnp.where(at_col == 1, jnp.sum(squares[...]), 0.0)
    )


def choose_kernel(rows, info, *refs):
    scalars = Scalars(info, rows)
    held, outs = refs[:FIRST], refs[FIRST:]
    for c, out in enumerate(outs):
        for s, ref in enumerate(held):
            @pl.when(scalars.plan(2 + c) == s)
            def _():
                out[...] = ref[...]


def copy_kernel(source, out):
    out[...] = source[...]


def pack_kernel(*refs):
    out = refs[-1]
    for i, ref in enumerate(refs[:-1]):
        out[i] = ref[...]


def copy_kernel(source, out):
    out[...] = source[...]


def pack_kernel(*refs):
    out = refs[-1]
    for i, ref in enumerate(refs[:-1]):
        out[i] = ref[...]


def choose_kernel(rows, info, *refs):
    scalars = Scalars(info, rows)
    held, outs = refs[:FIRST], refs[FIRST:]
    for c, out in enumerate(outs):
        for s, ref in enumerate(held):
            @pl.when(scalars.plan(2 + c) == s)
            def _():
                out[...] = ref[...]


def place_tiles(base, scalars, shards, left, right, raw):
    row, col = scalars.plan(0), scalars.plan(1)
    line, core = col // 2, lax.rem(col, 2)
    tile = left.shape[1]
    width = right.shape[2]
    blocks, half = tile // BLK, width // BLK
    zero = jnp.zeros((BLK, BLK), left.dtype)

    def stored(a, b):
        start = pl.multiple_of((b // 2) * tile + a * BLK, BLK)
        cols = pl.ds(pl.multiple_of(lax.rem(b, 2) * BLK, BLK), BLK) if not isinstance(b, int) else pl.ds((b % 2) * BLK, BLK)
        return raw[pl.ds(start, BLK), cols]

    def fetch(use):
        for half in range(2):
            for s, ref in enumerate(shards):
                @pl.when(scalars.plan(base + half * USES + use) == s)
                def _():
                    raw[half * tile : (half + 1) * tile, :] = ref[...]

    def left_tile(j, carry):
        slot = scalars.plan(base + j)

        @pl.when(slot >= 0)
        def _():
            fetch(j)

            def fill(block_of):
                for a in range(blocks):
                    for b in range(blocks):
                        keep = scalars.kept(row * blocks + a, j * blocks + b)
                        left[j, a * BLK : (a + 1) * BLK, b * BLK : (b + 1) * BLK] = jnp.where(keep, block_of(a, b), zero)

            @pl.when(j > row)
            def _():
                fill(stored)

            @pl.when(j < row)
            def _():
                fill(lambda a, b: stored(b, a).T)

            @pl.when(j == row)
            def _():
                fill(lambda a, b: stored(a, b) if a <= b else stored(b, a).T)

        return carry

    def right_tile(j, carry):
        slot = scalars.plan(base + 4 + j)

        @pl.when(slot >= 0)
        def _():
            fetch(4 + j)

            def fill(block_of):
                for a in range(blocks):
                    for b in range(half):
                        keep = scalars.kept(j * blocks + a, col * half + b)
                        right[j, a * BLK : (a + 1) * BLK, b * BLK : (b + 1) * BLK] = jnp.where(keep, block_of(a, b), zero)

            def direct(a, b):
                start = pl.multiple_of(core * tile + a * BLK, BLK)
                return raw[pl.ds(start, BLK), b * BLK : (b + 1) * BLK]

            def mirrored(a, b):
                start = pl.multiple_of((a // 2) * tile + (core * half + b) * BLK, BLK)
                return raw[pl.ds(start, BLK), (a % 2) * BLK : (a % 2 + 1) * BLK].T

            @pl.when(j < line)
            def _():
                fill(direct)

            @pl.when(j > line)
            def _():
                fill(mirrored)

            @pl.when(j == line)
            def _():
                fill(lambda a, b: jnp.where(a <= core * half + b, direct(a, b), mirrored(a, b)))

        return carry

    lax.fori_loop(0, 4, left_tile, 0)
    lax.fori_loop(0, 4, right_tile, 0)


def panels_kernel(base, count, rows, info, *refs):
    packed, left, right, raw = refs[count:]
    shards = list(refs[:count]) + [packed.at[i] for i in range(count)]
    place_tiles(base, Scalars(info, rows), shards, left, right, raw)


def grid_product_kernel(base, count, rows, info, *refs):
    left, right, out, raw = refs[2 * count + 2 :]
    scalars = Scalars(info, rows)
    place_tiles(base, scalars, refs[: 2 * count], left, right, raw)
    row, col = scalars.plan(0), scalars.plan(1)
    height, width = out.shape
    blocks, half = height // BLK, width // BLK

    @pl.when(row <= col // 2)
    def _():
        total = jnp.zeros((height, width), jnp.float32)
        for j in range(4):
            total += jnp.dot(left[j], right[j], preferred_element_type=jnp.float32)
        for a in range(blocks):
            for b in range(half):
                i, j = row * blocks + a, col * half + b
                keep = (i <= j) & scalars.kept(i, j)
                block = total[a * BLK : (a + 1) * BLK, b * BLK : (b + 1) * BLK]
                out[a * BLK : (a + 1) * BLK, b * BLK : (b + 1) * BLK] = jnp.where(
                    keep, block, jnp.zeros_like(block)
                ).astype(out.dtype)

    @pl.when(row > col // 2)
    def _():
        out[...] = jnp.zeros_like(out)


def chip_grid(density, pattern):
    height, width = density.shape
    n_col = lax.axis_size("col")
    n_devices = lax.axis_size("row") * n_col
    order_size = width * lax.axis_size("col")
    dtype = density.dtype
    axes = ("row", "col")
    first, second, rows = schedule()
    me = lax.axis_index("row") * lax.axis_size("col") + lax.axis_index("col")
    lanes = pattern.shape[1]
    plan_rows = -(-len(rows[0]) // lanes)
    table = jnp.asarray([row + [0] * (plan_rows * lanes - len(row)) for row in rows], jnp.int32)
    plan = lax.dynamic_index_in_dim(table.reshape(n_devices, plan_rows, lanes), me, 0, keepdims=False)
    plan = jnp.concatenate([plan, pattern], axis=0)
    shard = jax.ShapeDtypeStruct(density.shape, dtype)
    raw = pltpu.VMEM((2 * height, width), dtype)
    panels = [
        jax.ShapeDtypeStruct((4, height, height), dtype),
        jax.ShapeDtypeStruct((4, height, width), dtype),
    ]

    def call(kernel, out_shape, smem, args, scratch=(), out_specs=VMEM, aliases=None, flops=0):
        return pl.pallas_call(
            kernel,
            out_shape=out_shape,
            in_specs=[SMEM] * smem + [VMEM] * (len(args) - smem),
            out_specs=out_specs,
            scratch_shapes=list(scratch),
            input_output_aliases=aliases or {},
            compiler_params=GRID_PARAMS,
            cost_estimate=pl.CostEstimate(flops=flops, bytes_accessed=2**23, transcendentals=0) if flops else None,
        )(*args)

    def share(value):
        return lax.ppermute(value, axes, [(d, d ^ 1) for d in range(n_devices)])

    def part_from(parts, row_bits, col_bits):
        return lax.ppermute(parts, axes, [(d, d ^ (row_bits * n_col + col_bits)) for d in range(n_devices)])

    came = [lax.ppermute(density, axes, pairs) for pairs in first]
    came[-1], own = lax.optimization_barrier((came[-1], call(copy_kernel, shard, 0, [density])))
    held = [own] + came
    chosen = call(
        functools.partial(choose_kernel, plan_rows), [shard] * SECOND, 1, [plan] + held, (), [VMEM] * SECOND
    )
    tied = lax.optimization_barrier((*chosen, *held))
    chosen, held = tied[:SECOND], list(tied[SECOND:])
    later = [lax.ppermute(value, axes, pairs) for value, pairs in zip(chosen, second)]
    packed = share(call(pack_kernel, jax.ShapeDtypeStruct((FIRST, height, width), dtype), 0, held))
    parts = call(
        functools.partial(partial_kernel, plan_rows),
        jax.ShapeDtypeStruct((8, 128), jnp.float32),
        1,
        [plan] + held,
        [pltpu.VMEM((BLK, BLK), jnp.float32)] * 2,
    )
    packed, parts = lax.optimization_barrier((packed, parts + part_from(parts, 0, 1)))
    received = part_from(parts, 3, 2)
    left, right = call(
        functools.partial(panels_kernel, BASE, FIRST, plan_rows),
        panels,
        1,
        [plan] + held + [packed],
        [raw],
        [VMEM] * 2,
        flops=2**31,
    )
    *later, left, right, received = lax.optimization_barrier((*later, left, right, received))
    parts = parts + received
    received = part_from(parts, 0, 4)
    inputs = [plan] + later + [share(value) for value in later] + [left, right]
    square = call(
        functools.partial(grid_product_kernel, BASE + 2 * USES, SECOND, plan_rows),
        panels + [shard],
        1,
        inputs,
        [raw],
        [VMEM] * 3,
        {len(inputs) - 2: 0, len(inputs) - 1: 1},
        flops=2**31,
    )[2]
    square, received = lax.optimization_barrier((square, received))
    traces = (parts + received)[0, :2] / order_size
    return (square, traces)


def per_device(density, pattern):
    if lax.axis_size("row") == 4 and lax.axis_size("col") == 8 and density.shape[0] == 2 * density.shape[1]:
        return chip_grid(density, pattern)
    return any_mesh(density, pattern)


def solution(mesh):
    placed = (P("row", "col"), P())
    return jax.shard_map(
        per_device, mesh=mesh, in_specs=placed, out_specs=(P("row", "col"), P()), check_vma=False
    )
```

```python
import functools
import jax
import jax.numpy as jnp
from jax import lax
from jax.experimental import pallas as pl
from jax.experimental.pallas import tpu as pltpu
from jax.sharding import PartitionSpec as P

BLK = 128
VMEM = pl.BlockSpec(memory_space=pltpu.VMEM)
SMEM = pl.BlockSpec(memory_space=pltpu.SMEM)
PARAMS = pltpu.CompilerParams(vmem_limit_bytes=40 * 2**20)


def symmetric_kernel(sub, place, pattern, density, *rest):
    pieces, full = rest[:sub], rest[sub]
    row, col = place[0], place[1]
    height, width = density.shape
    per_piece = width // BLK
    row_blocks = height // BLK
    own_slot = lax.rem(col, sub)
    on_diagonal = row == col // sub
    for t in range(sub):
        slot = lax.rem(own_slot + sub - t, sub)
        for a in range(per_piece):
            i = slot * per_piece + a
            block_row = row * row_blocks + i
            rows = pl.ds(pl.multiple_of(i * BLK, BLK), BLK)
            for b in range(per_piece):
                block_col = col * per_piece + b
                cols = pl.ds(b * BLK, BLK)
                mirror = pieces[t][b * BLK : (b + 1) * BLK, a * BLK : (a + 1) * BLK]
                if t == 0:
                    start = pl.multiple_of((own_slot * per_piece + b) * BLK, BLK)
                    mine = density[pl.ds(start, BLK), a * BLK : (a + 1) * BLK]
                    mirror = jnp.where(on_diagonal, mine, mirror)
                chosen = pattern[jnp.minimum(block_row, block_col), jnp.maximum(block_row, block_col)] != 0
                upper = (block_row == block_col) | ((block_row < block_col) & chosen)
                lower = (block_row > block_col) & chosen
                zero = jnp.zeros((BLK, BLK), full.dtype)
                value = jnp.where(lower, mirror.T, zero)
                full[rows, cols] = jnp.where(upper, density[rows, cols], value)


def product_kernel(lines, planes, place, pattern, *refs):
    left = refs[: 2 * lines]
    right = refs[2 * lines : 2 * lines + planes]
    out, panel = refs[2 * lines + planes :]
    row, col = place[0], place[1]
    height, width = out.shape
    core, line = lax.rem(col, 2), col // 2
    for d in range(planes):
        start = pl.multiple_of((row ^ d) * height, height)
        panel[pl.ds(start, height), :] = right[d][...]
    total = jnp.zeros((height, width), jnp.float32)
    for e in range(lines):
        for s in range(2):
            start = pl.multiple_of(((line ^ e) * 2 + (core ^ s)) * width, width)
            total += jnp.dot(
                left[2 * e + s][...],
                panel[pl.ds(start, width), :],
                preferred_element_type=jnp.float32,
            )
    for i in range(height // BLK):
        for j in range(width // BLK):
            block_row = row * (height // BLK) + i
            block_col = col * (width // BLK) + j
            kept = (block_row == block_col) | ((block_row < block_col) & (pattern[block_row, block_col] != 0))
            block = total[i * BLK : (i + 1) * BLK, j * BLK : (j + 1) * BLK]
            out[i * BLK : (i + 1) * BLK, j * BLK : (j + 1) * BLK] = jnp.where(
                kept, block, jnp.zeros_like(block)
            ).astype(out.dtype)


def block_weights(pattern, row, col, row_blocks, col_blocks):
    block_rows = row * row_blocks + jnp.arange(row_blocks)
    block_cols = col * col_blocks + jnp.arange(col_blocks)
    chosen = lax.dynamic_slice(pattern, (row * row_blocks, col * col_blocks), (row_blocks, col_blocks))
    diagonal = block_rows[:, None] == block_cols[None, :]
    strict = (block_cols[None, :] > block_rows[:, None]) & (chosen != 0)
    return jnp.where(diagonal, 1.0, jnp.where(strict, 2.0, 0.0)).astype(jnp.float32)


def any_mesh(density, pattern):
    n_row = lax.axis_size("row")
    n_col = lax.axis_size("col")
    sub = n_col // n_row
    row = lax.axis_index("row")
    col = lax.axis_index("col")
    height, width = density.shape
    order_size = width * n_col
    place = jnp.stack([row, col]).astype(jnp.int32)

    pieces = []
    for t in range(sub):
        pairs = []
        for q in range(n_row):
            for c in range(n_col):
                p = (c + t) % sub
                if c > q * sub + p:
                    pairs.append((q * n_col + c, (c // sub) * n_col + q * sub + p))
        start = lax.rem(col + t, sub) * width
        piece = lax.dynamic_slice_in_dim(density, start, width, 0)
        pieces.append(lax.ppermute(piece, ("row", "col"), pairs))
    full = pl.pallas_call(
        functools.partial(symmetric_kernel, sub),
        out_shape=jax.ShapeDtypeStruct(density.shape, density.dtype),
        in_specs=[SMEM, SMEM] + [VMEM] * (sub + 1),
        out_specs=VMEM,
        compiler_params=PARAMS,
    )(place, pattern, density, *pieces)

    weights = block_weights(pattern, row, col, height // BLK, width // BLK)
    values = density.astype(jnp.float32).reshape(height // BLK, BLK, width // BLK, BLK)
    squares = jnp.sum(values * values, axis=(1, 3))
    rows_at = row * height + jnp.arange(height)[:, None]
    cols_at = col * width + jnp.arange(width)[None, :]
    diagonal = jnp.where(rows_at == cols_at, density.astype(jnp.float32), 0.0)
    sums = jnp.stack([jnp.sum(diagonal), jnp.sum(jnp.where(weights > 0, weights * squares, 0.0))])
    step = 1
    while step < n_row:
        sums = sums + lax.ppermute(sums, "row", [(i, i ^ step) for i in range(n_row)])
        step *= 2
    step = 1
    while step < n_col:
        sums = sums + lax.ppermute(sums, "col", [(i, i ^ step) for i in range(n_col)])
        step *= 2
    traces = sums / order_size

    right = [full]
    for d in range(1, n_row):
        right.append(lax.ppermute(full, "row", [(i, i ^ d) for i in range(n_row)]))
    left = []
    for e in range(n_col // 2):
        shard = full
        if e > 0:
            shard = lax.ppermute(full, "col", [(i, i ^ (2 * e)) for i in range(n_col)])
        other = lax.ppermute(shard, "col", [(i, i ^ 1) for i in range(n_col)])
        left += [shard, other]
    square = pl.pallas_call(
        functools.partial(product_kernel, n_col // 2, n_row),
        out_shape=jax.ShapeDtypeStruct(density.shape, density.dtype),
        in_specs=[SMEM, SMEM] + [VMEM] * (len(left) + len(right)),
        out_specs=VMEM,
        scratch_shapes=[pltpu.VMEM((order_size, width), density.dtype)],
        compiler_params=PARAMS,
    )(place, pattern, *left, *right)
    return (square, traces)

GRID_PARAMS = pltpu.CompilerParams(vmem_limit_bytes=14 * 2**20)
USES = 8
FIRST = 5
SECOND = 3
SEEN = ((), (0,), (1, 3), (2,))

MESSAGES = (
    (0, (0, 0), 1, (0, 0, 1), (0, 3, 1)),
    (0, (0, 2), 0, (0, 1, 0), (0, 0, 1)),
    (0, (2, 2), 0, (0, 2, 0), (1, 2, 1)),
    (0, (0, 3), 1, (0, 2, 1), (0, 0, 0)),
    (0, (2, 3), 0, (0, 3, 0), (0, 2, 1)),
    (0, (2, 3), 1, (0, 3, 1), (0, 2, 0)),
    (0, (0, 1), 0, (1, 1, 0), (1, 3, 0)),
    (0, (1, 2), 1, (1, 1, 1), (0, 1, 0)),
    (0, (1, 3), 0, (1, 2, 0), (0, 1, 1)),
    (0, (1, 1), 1, (1, 2, 1), (1, 3, 1)),
    (0, (0, 3), 0, (1, 3, 0), (3, 3, 1)),
    (0, (1, 2), 1, (1, 3, 1), (2, 3, 0)),
    (0, (0, 1), 1, (2, 1, 1), (0, 3, 0)),
    (0, (0, 3), 1, (2, 3, 1), (3, 3, 0)),
    (0, (1, 2), 0, (3, 2, 0), (2, 3, 1)),
    (0, (2, 3), 0, (3, 3, 0), (1, 2, 0)),
    (0, (1, 3), 1, (3, 3, 1), (1, 1, 0)),
    (1, (0, 1), 1, (0, 2, 1), (1, 2, 0)),
    (1, (0, 3), 0, (0, 3, 0), (0, 0, 0)),
    (1, (1, 3), 1, (0, 3, 1), (2, 3, 0)),
    (1, (0, 1), 0, (1, 1, 0), (1, 2, 1)),
    (1, (0, 1), 1, (1, 1, 1), (1, 3, 1)),
    (1, (1, 2), 0, (1, 2, 0), (2, 2, 1)),
    (1, (0, 2), 1, (1, 2, 1), (0, 0, 1)),
    (1, (3, 3), 0, (1, 3, 0), (0, 3, 0)),
    (1, (1, 3), 1, (1, 3, 1), (0, 1, 1)),
    (1, (0, 0), 0, (2, 0, 0), (0, 2, 0)),
    (1, (0, 1), 0, (2, 1, 0), (0, 3, 1)),
    (1, (0, 2), 0, (2, 2, 0), (2, 3, 1)),
    (1, (0, 3), 0, (2, 3, 0), (0, 1, 0)),
    (1, (2, 3), 1, (2, 3, 1), (1, 3, 0)),
    (2, (0, 0), 0, (0, 1, 0), (0, 3, 1)),
    (2, (0, 0), 1, (0, 1, 1), (0, 2, 1)),
    (2, (1, 2), 0, (0, 2, 0), (0, 1, 0)),
    (2, (1, 2), 1, (0, 2, 1), (2, 2, 0)),
    (2, (2, 3), 0, (0, 3, 0), (1, 3, 1)),
    (2, (0, 2), 1, (0, 3, 1), (2, 3, 0)),
    (2, (1, 3), 0, (1, 3, 0), (2, 3, 1)),
    (2, (3, 3), 1, (1, 3, 1), (0, 3, 0)),
    (2, (2, 3), 1, (2, 2, 1), (1, 2, 0)),
    (2, (0, 3), 1, (2, 3, 1), (0, 1, 1)),
    (2, (1, 1), 0, (3, 1, 0), (1, 3, 0)),
    (2, (2, 2), 1, (3, 2, 1), (1, 2, 1)),
    (2, (1, 3), 0, (3, 3, 0), (1, 1, 1)),
)


def number(device):
    return 8 * device[0] + 2 * device[1] + device[2]


def wanted(r, z):
    if r > z:
        return [None] * USES
    return [(min(r, j), max(r, j)) for j in range(4)] + [(min(z, j), max(z, j)) for j in range(4)]


def first_round(devices):
    def ring(r, z, k, up):
        step = 1 if (k == 0) == up else -1
        return (r, z + step, k) if 0 <= z + step < 4 else (r, z, 1 - k)

    return [[(d, ring(*d, up)) for d in devices] for up in (True, False)] + [
        [((r, z, k), (r ^ (1 + (k + turn) % 2), z, k)) for r, z, k in devices] for turn in (0, 1)
    ]


def closed(pairs, devices):
    def hops(a, b):
        return abs(a[1] - b[1]) + bin(a[0] ^ b[0]).count("1")

    sends, receives = {a for a, _ in pairs}, {b for _, b in pairs}
    free = sorted((hops(a, b), a, b) for a in devices for b in devices if a not in sends and b not in receives and a != b)
    extra = []
    for _, a, b in free:
        if a not in sends and b not in receives:
            sends.add(a)
            receives.add(b)
            extra.append((a, b))
    return pairs + extra


def schedule():
    devices = [(r, z, k) for r in range(4) for z in range(4) for k in range(2)]
    first = first_round(devices)
    held = {d: [((d[0], d[1]), d[2])] for d in devices}
    for pairs in first:
        for a, b in pairs:
            held[b].append(((a[0], a[1]), a[2]))
    second = [[] for _ in range(SECOND)]
    later = {d: [None] * SECOND for d in devices}
    sends = [{} for _ in range(SECOND)]
    for i, tile, half, a, b in MESSAGES:
        second[i].append((a, b))
        sends[i][number(a)] = held[a].index((tile, half))
        later[b][i] = (tile, half)
    second = [closed(pairs, devices) for pairs in second]
    adds = [set() for _ in range(FIRST)]
    uses = [[{} for _ in range(USES)] for _ in range(2)]
    for d in devices:
        r, z, k = d
        added = {(r, z), (r ^ 1, z), (r ^ 2, z)} | {(r, j) for j in SEEN[z]}
        for s, (tile, half) in enumerate(held[d]):
            if tile in added and half == k and (s == 0 or tile != (r, z)):
                adds[s].add(number(d))
        for u, tile in enumerate(wanted(r, z)):
            for n, shards in enumerate((held, later)):
                here = shards[d] + shards[r, z, 1 - k]
                if tile and (tile, 0) in here and (tile, 1) in here and not any(number(d) in uses[m][u] for m in range(n)):
                    uses[n][u][number(d)] = (here.index((tile, 0)), here.index((tile, 1)))
            assert tile is None or any(number(d) in uses[n][u] for n in range(2))

    def flat(pairs):
        assert len({a for a, _ in pairs}) == len({b for _, b in pairs}) == len(devices)
        return [(number(a), number(b)) for a, b in pairs]

    return [flat(p) for p in first], [flat(p) for p in second], sends, adds, uses


class Place:
    def __init__(self):
        self.row, self.col = lax.axis_index("row"), lax.axis_index("col")
        self.line, self.core = self.col // 2, lax.rem(self.col, 2)
        self.number = self.row * 8 + self.col

    def among(self, devices):
        bits = sum(1 << d for d in devices)
        bits -= (bits >> 31) << 32
        return (lax.shift_right_logical(jnp.int32(bits), self.number) & 1) == 1


def kept(pattern, i, j):
    low, high = jnp.minimum(i, j), jnp.maximum(i, j)
    return (low == high) | (pattern[low, high] != 0)


def partial_kernel(adds, order_size, pattern, *refs):
    me = Place()
    packed, out, squares, diagonals = refs[FIRST:]
    out[...] = jnp.zeros_like(out)
    at_row = lax.broadcasted_iota(jnp.int32, out.shape, 0)
    at_col = lax.broadcasted_iota(jnp.int32, out.shape, 1)
    both = [(refs[s], s, 0) for s in range(FIRST)] + [(packed.at[s], s, 1) for s in range(FIRST)]
    for ref, s, other in both:
        devices = {d ^ other for d in adds[s]}
        core = me.core ^ other
        before, after = me.line - 1 + 2 * core, me.line + 1 - 2 * core
        row = (me.row, me.row, me.row, me.row ^ (1 + core), me.row ^ (2 - core))[s]
        line = (me.line, before, after, me.line, me.line)[s]
        row_blocks, col_blocks = ref.shape[0] // BLK, ref.shape[1] // BLK

        @pl.when(me.among(devices) & (row <= line))
        def _():
            zero = jnp.zeros((BLK, BLK), jnp.float32)
            total = zero
            for a in range(row_blocks):
                for b in range(col_blocks):
                    i, j = row * row_blocks + a, (2 * line + core) * col_blocks + b
                    block = ref[a * BLK : (a + 1) * BLK, b * BLK : (b + 1) * BLK].astype(jnp.float32)
                    block = jnp.where((i <= j) & kept(pattern, i, j), block, zero)
                    total += jnp.where(i == j, 1.0, 2.0) * (block * block)
            squares[...] = total
            diagonals[...] = zero

            @pl.when(row == line)
            def _():
                rows_at = lax.broadcasted_iota(jnp.int32, (BLK, BLK), 0)
                cols_at = lax.broadcasted_iota(jnp.int32, (BLK, BLK), 1)
                for b in range(col_blocks):
                    start = pl.multiple_of((core * col_blocks + b) * BLK, BLK)
                    block = ref[pl.ds(start, BLK), b * BLK : (b + 1) * BLK].astype(jnp.float32)
                    diagonals[...] += jnp.where(rows_at == cols_at, block, zero)

            owner = 8 * row + 2 * line + core
            for i, values in enumerate((diagonals, squares)):
                out[...] += jnp.where((at_row == i) & (at_col == owner), jnp.sum(values[...]) / order_size, 0.0)


def copy_kernel(source, out):
    out[...] = source[...]


def pack_kernel(*refs):
    out = refs[-1]
    for i, ref in enumerate(refs[:-1]):
        out[i] = ref[...]


def copy_kernel(source, out):
    out[...] = source[...]


def pack_kernel(*refs):
    out = refs[-1]
    for i, ref in enumerate(refs[:-1]):
        out[i] = ref[...]


def choose_kernel(sends, *refs):
    me = Place()
    held, outs = refs[:FIRST], refs[FIRST:]
    for out, send in zip(outs, sends):
        for s, ref in enumerate(held):
            devices = [d for d in send if send[d] == s]
            if devices:
                @pl.when(me.among(devices))
                def _():
                    out[...] = ref[...]


def pack_kernel(*refs):
    out = refs[-1]
    for i, ref in enumerate(refs[:-1]):
        out[i] = ref[...]


def place_tiles(uses, me, shards, keep, left, right, raw):
    tile, width = left.shape[0], right.shape[1]
    blocks, half_blocks = tile // BLK, width // BLK
    zero = jnp.zeros((BLK, BLK), left.dtype)

    def stored(a, b):
        return raw[(b // 2) * tile + a * BLK : (b // 2) * tile + (a + 1) * BLK, (b % 2) * BLK : (b % 2 + 1) * BLK]

    def direct(a, b):
        start = pl.multiple_of(me.core * tile + a * BLK, BLK)
        return raw[pl.ds(start, BLK), b * BLK : (b + 1) * BLK]

    def mirrored(a, b):
        start = pl.multiple_of((a // 2) * tile + (me.core * half_blocks + b) * BLK, BLK)
        return raw[pl.ds(start, BLK), (a % 2) * BLK : (a % 2 + 1) * BLK].T

    left_ways = (
        stored,
        lambda a, b: stored(b, a).T,
        lambda a, b: stored(a, b) if a <= b else stored(b, a).T,
    )
    right_ways = (
        direct,
        mirrored,
        lambda a, b: jnp.where(a <= me.core * half_blocks + b, direct(a, b), mirrored(a, b)),
    )

    def fill(panel, at, cols, u, block_of):
        j = u % 4
        for a in range(blocks):
            for b in range(cols):
                rows = slice(at[0] + a * BLK, at[0] + (a + 1) * BLK)
                lanes = slice(at[1] + b * BLK, at[1] + (b + 1) * BLK)
                if u < 4:
                    flag = keep(panel, rows, lanes, me.row * blocks + a, j * blocks + b)
                else:
                    flag = keep(panel, rows, lanes, j * blocks + a, me.col * half_blocks + b)
                panel[rows, lanes] = jnp.where(flag, block_of(a, b), zero)

    for u, here in enumerate(uses):
        j = u % 4
        panel, at, cols, ways = (left, (0, j * tile), blocks, left_ways) if u < 4 else (
            right, (j * tile, 0), half_blocks, right_ways)

        def index(d):
            return d // 8 if u < 4 else (d % 8) // 2

        def above(d):
            return 2 if index(d) == j else int((index(d) > j) == (u < 4))

        if here:
            @pl.when(me.among(here))
            def _():
                for half in range(2):
                    for s in sorted({here[d][half] for d in here}):
                        @pl.when(me.among([d for d in here if here[d][half] == s]))
                        def _():
                            raw[half * tile : (half + 1) * tile, :] = shards[s][...]

                for way in sorted({above(d) for d in here}):
                    @pl.when(me.among([d for d in here if above(d) == way]))
                    def _():
                        fill(panel, at, cols, u, ways[way])


def place_last_tiles(uses, me, shards, left, right, raw):
    tile, width = left.shape[0], right.shape[1]
    blocks, half_blocks = tile // BLK, width // BLK
    part = 16

    def put(panel, row_at, col_at, block):
        lanes = slice(col_at, col_at + BLK)
        flag = panel[row_at : row_at + part, lanes] != 0
        for q in range(0, BLK, part):
            value = block[q : q + part, :]
            panel[row_at + q : row_at + q + part, lanes] = jnp.where(flag, value, jnp.zeros_like(value))

    def square(ref, a, b):
        return ref[a * BLK : (a + 1) * BLK, b * BLK : (b + 1) * BLK]

    diagonal = [{} for _ in range(USES)]
    for u, here in enumerate(uses):
        j = u % 4
        of_left = u < 4

        def index(d):
            return d // 8 if of_left else (d % 8) // 2

        diagonal[u] = {d: here[d] for d in here if index(d) == j}
        for half in range(2):
            for s in sorted({here[d][half] for d in here}):
                ref = shards[s]
                found = [d for d in here if here[d][half] == s]
                stands = [d for d in found if (index(d) < j if of_left else index(d) > j)]
                lies = [d for d in found if (index(d) > j if of_left else index(d) < j)]
                if of_left and stands:
                    @pl.when(me.among(stands))
                    def _():
                        for a in range(blocks):
                            for b in range(half_blocks):
                                put(left, a * BLK, j * tile + (half * half_blocks + b) * BLK, square(ref, a, b))
                if of_left and lies:
                    @pl.when(me.among(lies))
                    def _():
                        for a in range(half_blocks):
                            for b in range(blocks):
                                put(left, (half * half_blocks + a) * BLK, j * tile + b * BLK, square(ref, b, a).T)
                mine = [d for d in stands if d % 2 == half]
                if not of_left and mine:
                    @pl.when(me.among(mine))
                    def _():
                        for a in range(blocks):
                            for b in range(half_blocks):
                                put(right, j * tile + a * BLK, b * BLK, square(ref, a, b))
                if not of_left and lies:
                    @pl.when(me.among(lies))
                    def _():
                        for a in range(half_blocks):
                            for b in range(half_blocks):
                                start = pl.multiple_of((me.core * half_blocks + b) * BLK, BLK)
                                block = ref[pl.ds(start, BLK), a * BLK : (a + 1) * BLK]
                                put(right, j * tile + (half * half_blocks + a) * BLK, b * BLK, block.T)

    def keep(panel, rows, lanes, i, j):
        return panel[rows, lanes] != 0

    place_tiles(diagonal, me, shards, keep, left, right, raw)


def panels_kernel(uses, pattern, *refs):
    packed, left, right, keeps, raw = refs[FIRST:]
    me = Place()
    shards = list(refs[:FIRST]) + [packed.at[i] for i in range(FIRST)]

    def keep(panel, rows, lanes, i, j):
        return kept(pattern, i, j)

    place_tiles(uses[0], me, shards, keep, left, right, raw)
    tile, width = left.shape[0], right.shape[1]
    blocks, half_blocks = tile // BLK, width // BLK

    def flags(ref, row_at, col_at, cols, flag):
        for a in range(blocks):
            for b in range(cols):
                value = jnp.where(flag(a, b), 1.0, 0.0).astype(ref.dtype)
                ref[row_at + a * BLK : row_at + (a + 1) * BLK, col_at + b * BLK : col_at + (b + 1) * BLK] = (
                    jnp.full((BLK, BLK), value, ref.dtype)
                )

    for u, later in enumerate(uses[1]):
        j = u % 4
        if later:
            @pl.when(me.among(later))
            def _():
                if u < 4:
                    flags(left, 0, j * tile, blocks, lambda a, b: kept(pattern, me.row * blocks + a, j * blocks + b))
                else:
                    flags(
                        right, j * tile, 0, half_blocks,
                        lambda a, b: kept(pattern, j * blocks + a, me.col * half_blocks + b),
                    )

    def square_kept(a, b):
        i, j = me.row * blocks + a, me.col * half_blocks + b
        return (i <= j) & kept(pattern, i, j)

    flags(keeps, 0, 0, half_blocks, square_kept)


def grid_product_kernel(uses, *refs):
    shards = refs[: 2 * SECOND]
    keeps, _, _, left, right, out, raw, result, sems = refs[2 * SECOND :]
    me = Place()
    place_last_tiles(uses[1], me, shards, left, right, raw)
    height = out.shape[0]
    part = height // 2
    copies = []
    for c in range(2):
        rows = pl.ds(c * part, part)

        @pl.when(me.row <= me.line)
        def _():
            product = jnp.dot(left[rows, :], right[...], preferred_element_type=jnp.float32)
            result[rows, :] = jnp.where(
                keeps[rows, :].astype(jnp.float32) != 0, product, jnp.zeros_like(product)
            ).astype(result.dtype)

        @pl.when(me.row > me.line)
        def _():
            result[rows, :] = jnp.zeros((part, result.shape[1]), result.dtype)

        copies.append(pltpu.make_async_copy(result.at[rows], out.at[rows], sems.at[c]))
        copies[-1].start()
    for copy in copies:
        copy.wait()


def chip_grid(density, pattern):
    height, width = density.shape
    n_col = lax.axis_size("col")
    n_devices = lax.axis_size("row") * n_col
    order_size = width * lax.axis_size("col")
    dtype = density.dtype
    axes = ("row", "col")
    first, second, sends, adds, uses = schedule()
    shard = jax.ShapeDtypeStruct(density.shape, dtype)
    raw = pltpu.VMEM((2 * height, width), dtype)
    panels = [
        jax.ShapeDtypeStruct((height, order_size), dtype),
        jax.ShapeDtypeStruct((order_size, width), dtype),
    ]

    def call(kernel, out_shape, smem, args, scratch=(), out_specs=VMEM, aliases=None, cost=None):
        return pl.pallas_call(
            kernel,
            out_shape=out_shape,
            in_specs=[SMEM] * smem + [VMEM] * (len(args) - smem),
            out_specs=out_specs,
            scratch_shapes=list(scratch),
            input_output_aliases=aliases or {},
            compiler_params=GRID_PARAMS,
            cost_estimate=cost,
        )(*args)

    def share(value):
        return lax.ppermute(value, axes, [(d, d ^ 1) for d in range(n_devices)])

    def part_from(parts, row_bits, col_bits):
        return lax.ppermute(parts, axes, [(d, d ^ (row_bits * n_col + col_bits)) for d in range(n_devices)])

    came = [lax.ppermute(density, axes, pairs) for pairs in first]
    came[0], own = lax.optimization_barrier((came[0], call(copy_kernel, shard, 0, [density])))
    held = [own] + came
    chosen = call(functools.partial(choose_kernel, sends), [shard] * SECOND, 0, held, (), [VMEM] * SECOND)
    tied = lax.optimization_barrier((*chosen, *held))
    chosen, held = tied[:SECOND], list(tied[SECOND:])
    later = [lax.ppermute(value, axes, pairs) for value, pairs in zip(chosen, second)]
    packed = share(call(pack_kernel, jax.ShapeDtypeStruct((FIRST, height, width), dtype), 0, held))
    parts = call(
        functools.partial(partial_kernel, adds, order_size),
        jax.ShapeDtypeStruct((8, 128), jnp.float32),
        1,
        [pattern] + held + [packed],
        [pltpu.VMEM((BLK, BLK), jnp.float32)] * 2,
    )
    packed, parts = lax.optimization_barrier((packed, parts))
    received = part_from(parts, 3, 2)
    left, right, keeps = call(
        functools.partial(panels_kernel, uses), panels + [shard], 1, [pattern] + held + [packed], [raw], [VMEM] * 3
    )
    left, parts = lax.optimization_barrier((left, parts + received))
    received = part_from(parts, 0, 4)
    left, parts = lax.optimization_barrier((left, parts))
    shared = []
    for i in range(SECOND):
        later[i], left = lax.optimization_barrier((later[i], left))
        shared.append(share(later[i]))
    inputs = later + shared + [keeps, left, right]
    square = call(
        functools.partial(grid_product_kernel, uses),
        panels + [shard],
        0,
        inputs,
        [raw, pltpu.VMEM(density.shape, dtype), pltpu.SemaphoreType.DMA((2,))],
        [VMEM, VMEM, pl.BlockSpec(memory_space=pltpu.HBM)],
        {len(inputs) - 2: 0, len(inputs) - 1: 1},
    )[2]
    square, received = lax.optimization_barrier((square, received))
    traces = jnp.sum(parts[:2] + received[:2], axis=1)
    return (square, traces)


def per_device(density, pattern):
    if lax.axis_size("row") == 4 and lax.axis_size("col") == 8 and density.shape[0] == 2 * density.shape[1]:
        return chip_grid(density, pattern)
    return any_mesh(density, pattern)


def solution(mesh):
    placed = (P("row", "col"), P())
    return jax.shard_map(
        per_device, mesh=mesh, in_specs=placed, out_specs=(P("row", "col"), P()), check_vma=False
    )
```

```python
import functools
import jax
import jax.numpy as jnp
from jax import lax
from jax.experimental import pallas as pl
from jax.experimental.pallas import tpu as pltpu
from jax.sharding import PartitionSpec as P

BLK = 128
VMEM = pl.BlockSpec(memory_space=pltpu.VMEM)
SMEM = pl.BlockSpec(memory_space=pltpu.SMEM)
PARAMS = pltpu.CompilerParams(vmem_limit_bytes=40 * 2**20)


def symmetric_kernel(sub, place, pattern, density, *rest):
    pieces, full = rest[:sub], rest[sub]
    row, col = place[0], place[1]
    height, width = density.shape
    per_piece = width // BLK
    row_blocks = height // BLK
    own_slot = lax.rem(col, sub)
    on_diagonal = row == col // sub
    for t in range(sub):
        slot = lax.rem(own_slot + sub - t, sub)
        for a in range(per_piece):
            i = slot * per_piece + a
            block_row = row * row_blocks + i
            rows = pl.ds(pl.multiple_of(i * BLK, BLK), BLK)
            for b in range(per_piece):
                block_col = col * per_piece + b
                cols = pl.ds(b * BLK, BLK)
                mirror = pieces[t][b * BLK : (b + 1) * BLK, a * BLK : (a + 1) * BLK]
                if t == 0:
                    start = pl.multiple_of((own_slot * per_piece + b) * BLK, BLK)
                    mine = density[pl.ds(start, BLK), a * BLK : (a + 1) * BLK]
                    mirror = jnp.where(on_diagonal, mine, mirror)
                chosen = pattern[jnp.minimum(block_row, block_col), jnp.maximum(block_row, block_col)] != 0
                upper = (block_row == block_col) | ((block_row < block_col) & chosen)
                lower = (block_row > block_col) & chosen
                zero = jnp.zeros((BLK, BLK), full.dtype)
                value = jnp.where(lower, mirror.T, zero)
                full[rows, cols] = jnp.where(upper, density[rows, cols], value)


def product_kernel(lines, planes, place, pattern, *refs):
    left = refs[: 2 * lines]
    right = refs[2 * lines : 2 * lines + planes]
    out, panel = refs[2 * lines + planes :]
    row, col = place[0], place[1]
    height, width = out.shape
    core, line = lax.rem(col, 2), col // 2
    for d in range(planes):
        start = pl.multiple_of((row ^ d) * height, height)
        panel[pl.ds(start, height), :] = right[d][...]
    total = jnp.zeros((height, width), jnp.float32)
    for e in range(lines):
        for s in range(2):
            start = pl.multiple_of(((line ^ e) * 2 + (core ^ s)) * width, width)
            total += jnp.dot(
                left[2 * e + s][...],
                panel[pl.ds(start, width), :],
                preferred_element_type=jnp.float32,
            )
    for i in range(height // BLK):
        for j in range(width // BLK):
            block_row = row * (height // BLK) + i
            block_col = col * (width // BLK) + j
            kept = (block_row == block_col) | ((block_row < block_col) & (pattern[block_row, block_col] != 0))
            block = total[i * BLK : (i + 1) * BLK, j * BLK : (j + 1) * BLK]
            out[i * BLK : (i + 1) * BLK, j * BLK : (j + 1) * BLK] = jnp.where(
                kept, block, jnp.zeros_like(block)
            ).astype(out.dtype)


def block_weights(pattern, row, col, row_blocks, col_blocks):
    block_rows = row * row_blocks + jnp.arange(row_blocks)
    block_cols = col * col_blocks + jnp.arange(col_blocks)
    chosen = lax.dynamic_slice(pattern, (row * row_blocks, col * col_blocks), (row_blocks, col_blocks))
    diagonal = block_rows[:, None] == block_cols[None, :]
    strict = (block_cols[None, :] > block_rows[:, None]) & (chosen != 0)
    return jnp.where(diagonal, 1.0, jnp.where(strict, 2.0, 0.0)).astype(jnp.float32)


def any_mesh(density, pattern):
    n_row = lax.axis_size("row")
    n_col = lax.axis_size("col")
    sub = n_col // n_row
    row = lax.axis_index("row")
    col = lax.axis_index("col")
    height, width = density.shape
    order_size = width * n_col
    place = jnp.stack([row, col]).astype(jnp.int32)

    pieces = []
    for t in range(sub):
        pairs = []
        for q in range(n_row):
            for c in range(n_col):
                p = (c + t) % sub
                if c > q * sub + p:
                    pairs.append((q * n_col + c, (c // sub) * n_col + q * sub + p))
        start = lax.rem(col + t, sub) * width
        piece = lax.dynamic_slice_in_dim(density, start, width, 0)
        pieces.append(lax.ppermute(piece, ("row", "col"), pairs))
    full = pl.pallas_call(
        functools.partial(symmetric_kernel, sub),
        out_shape=jax.ShapeDtypeStruct(density.shape, density.dtype),
        in_specs=[SMEM, SMEM] + [VMEM] * (sub + 1),
        out_specs=VMEM,
        compiler_params=PARAMS,
    )(place, pattern, density, *pieces)

    weights = block_weights(pattern, row, col, height // BLK, width // BLK)
    values = density.astype(jnp.float32).reshape(height // BLK, BLK, width // BLK, BLK)
    squares = jnp.sum(values * values, axis=(1, 3))
    rows_at = row * height + jnp.arange(height)[:, None]
    cols_at = col * width + jnp.arange(width)[None, :]
    diagonal = jnp.where(rows_at == cols_at, density.astype(jnp.float32), 0.0)
    sums = jnp.stack([jnp.sum(diagonal), jnp.sum(jnp.where(weights > 0, weights * squares, 0.0))])
    step = 1
    while step < n_row:
        sums = sums + lax.ppermute(sums, "row", [(i, i ^ step) for i in range(n_row)])
        step *= 2
    step = 1
    while step < n_col:
        sums = sums + lax.ppermute(sums, "col", [(i, i ^ step) for i in range(n_col)])
        step *= 2
    traces = sums / order_size

    right = [full]
    for d in range(1, n_row):
        right.append(lax.ppermute(full, "row", [(i, i ^ d) for i in range(n_row)]))
    left = []
    for e in range(n_col // 2):
        shard = full
        if e > 0:
            shard = lax.ppermute(full, "col", [(i, i ^ (2 * e)) for i in range(n_col)])
        other = lax.ppermute(shard, "col", [(i, i ^ 1) for i in range(n_col)])
        left += [shard, other]
    square = pl.pallas_call(
        functools.partial(product_kernel, n_col // 2, n_row),
        out_shape=jax.ShapeDtypeStruct(density.shape, density.dtype),
        in_specs=[SMEM, SMEM] + [VMEM] * (len(left) + len(right)),
        out_specs=VMEM,
        scratch_shapes=[pltpu.VMEM((order_size, width), density.dtype)],
        compiler_params=PARAMS,
    )(place, pattern, *left, *right)
    return (square, traces)

GRID_PARAMS = pltpu.CompilerParams(vmem_limit_bytes=14 * 2**20)
USES = 8
FIRST = 5
SECOND = 3
SEEN = ((), (0,), (1, 3), (2,))

MESSAGES = (
    (0, (0, 0), 1, (0, 0, 1), (0, 3, 1)),
    (0, (0, 2), 0, (0, 1, 0), (0, 0, 1)),
    (0, (2, 2), 0, (0, 2, 0), (1, 2, 1)),
    (0, (0, 3), 1, (0, 2, 1), (0, 0, 0)),
    (0, (2, 3), 0, (0, 3, 0), (0, 2, 1)),
    (0, (2, 3), 1, (0, 3, 1), (0, 2, 0)),
    (0, (0, 1), 0, (1, 1, 0), (1, 3, 0)),
    (0, (1, 2), 1, (1, 1, 1), (0, 1, 0)),
    (0, (1, 3), 0, (1, 2, 0), (0, 1, 1)),
    (0, (1, 1), 1, (1, 2, 1), (1, 3, 1)),
    (0, (0, 3), 0, (1, 3, 0), (3, 3, 1)),
    (0, (1, 2), 1, (1, 3, 1), (2, 3, 0)),
    (0, (0, 1), 1, (2, 1, 1), (0, 3, 0)),
    (0, (0, 3), 1, (2, 3, 1), (3, 3, 0)),
    (0, (1, 2), 0, (3, 2, 0), (2, 3, 1)),
    (0, (2, 3), 0, (3, 3, 0), (1, 2, 0)),
    (0, (1, 3), 1, (3, 3, 1), (1, 1, 0)),
    (1, (0, 1), 1, (0, 2, 1), (1, 2, 0)),
    (1, (0, 3), 0, (0, 3, 0), (0, 0, 0)),
    (1, (1, 3), 1, (0, 3, 1), (2, 3, 0)),
    (1, (0, 1), 0, (1, 1, 0), (1, 2, 1)),
    (1, (0, 1), 1, (1, 1, 1), (1, 3, 1)),
    (1, (1, 2), 0, (1, 2, 0), (2, 2, 1)),
    (1, (0, 2), 1, (1, 2, 1), (0, 0, 1)),
    (1, (3, 3), 0, (1, 3, 0), (0, 3, 0)),
    (1, (1, 3), 1, (1, 3, 1), (0, 1, 1)),
    (1, (0, 0), 0, (2, 0, 0), (0, 2, 0)),
    (1, (0, 1), 0, (2, 1, 0), (0, 3, 1)),
    (1, (0, 2), 0, (2, 2, 0), (2, 3, 1)),
    (1, (0, 3), 0, (2, 3, 0), (0, 1, 0)),
    (1, (2, 3), 1, (2, 3, 1), (1, 3, 0)),
    (2, (0, 0), 0, (0, 1, 0), (0, 3, 1)),
    (2, (0, 0), 1, (0, 1, 1), (0, 2, 1)),
    (2, (1, 2), 0, (0, 2, 0), (0, 1, 0)),
    (2, (1, 2), 1, (0, 2, 1), (2, 2, 0)),
    (2, (2, 3), 0, (0, 3, 0), (1, 3, 1)),
    (2, (0, 2), 1, (0, 3, 1), (2, 3, 0)),
    (2, (1, 3), 0, (1, 3, 0), (2, 3, 1)),
    (2, (3, 3), 1, (1, 3, 1), (0, 3, 0)),
    (2, (2, 3), 1, (2, 2, 1), (1, 2, 0)),
    (2, (0, 3), 1, (2, 3, 1), (0, 1, 1)),
    (2, (1, 1), 0, (3, 1, 0), (1, 3, 0)),
    (2, (2, 2), 1, (3, 2, 1), (1, 2, 1)),
    (2, (1, 3), 0, (3, 3, 0), (1, 1, 1)),
)


def number(device):
    return 8 * device[0] + 2 * device[1] + device[2]


def wanted(r, z):
    if r > z:
        return [None] * USES
    return [(min(r, j), max(r, j)) for j in range(4)] + [(min(z, j), max(z, j)) for j in range(4)]


def first_round(devices):
    def ring(r, z, k, up):
        step = 1 if (k == 0) == up else -1
        return (r, z + step, k) if 0 <= z + step < 4 else (r, z, 1 - k)

    return [[(d, ring(*d, up)) for d in devices] for up in (True, False)] + [
        [((r, z, k), (r ^ bit, z, k)) for r, z, k in devices] for bit in (1, 2)
    ]


def closed(pairs, devices):
    def hops(a, b):
        return abs(a[1] - b[1]) + bin(a[0] ^ b[0]).count("1")

    sends, receives = {a for a, _ in pairs}, {b for _, b in pairs}
    free = sorted((hops(a, b), a, b) for a in devices for b in devices if a not in sends and b not in receives and a != b)
    extra = []
    for _, a, b in free:
        if a not in sends and b not in receives:
            sends.add(a)
            receives.add(b)
            extra.append((a, b))
    return pairs + extra


def schedule():
    devices = [(r, z, k) for r in range(4) for z in range(4) for k in range(2)]
    first = first_round(devices)
    held = {d: [((d[0], d[1]), d[2])] for d in devices}
    for pairs in first:
        for a, b in pairs:
            held[b].append(((a[0], a[1]), a[2]))
    second = [[] for _ in range(SECOND)]
    later = {d: [None] * SECOND for d in devices}
    sends = [{} for _ in range(SECOND)]
    for i, tile, half, a, b in MESSAGES:
        second[i].append((a, b))
        sends[i][number(a)] = held[a].index((tile, half))
        later[b][i] = (tile, half)
    second = [closed(pairs, devices) for pairs in second]
    adds = [set() for _ in range(FIRST)]
    uses = [[{} for _ in range(USES)] for _ in range(2)]
    for d in devices:
        r, z, k = d
        added = {(r, z), (r ^ 1, z), (r ^ 2, z)} | {(r, j) for j in SEEN[z]}
        for s, (tile, half) in enumerate(held[d]):
            if tile in added and half == k and (s == 0 or tile != (r, z)):
                adds[s].add(number(d))
        for u, tile in enumerate(wanted(r, z)):
            for n, shards in enumerate((held, later)):
                here = shards[d] + shards[r, z, 1 - k]
                if tile and (tile, 0) in here and (tile, 1) in here and not any(number(d) in uses[m][u] for m in range(n)):
                    uses[n][u][number(d)] = (here.index((tile, 0)), here.index((tile, 1)))
            assert tile is None or any(number(d) in uses[n][u] for n in range(2))

    def flat(pairs):
        assert len({a for a, _ in pairs}) == len({b for _, b in pairs}) == len(devices)
        return [(number(a), number(b)) for a, b in pairs]

    return [flat(p) for p in first], [flat(p) for p in second], sends, adds, uses


class Place:
    def __init__(self):
        self.row, self.col = lax.axis_index("row"), lax.axis_index("col")
        self.line, self.core = self.col // 2, lax.rem(self.col, 2)
        self.number = self.row * 8 + self.col

    def among(self, devices):
        bits = sum(1 << d for d in devices)
        bits -= (bits >> 31) << 32
        return (lax.shift_right_logical(jnp.int32(bits), self.number) & 1) == 1


def kept(pattern, i, j):
    low, high = jnp.minimum(i, j), jnp.maximum(i, j)
    return (low == high) | (pattern[low, high] != 0)


def partial_kernel(adds, order_size, pattern, *refs):
    me = Place()
    packed, out, squares, diagonals = refs[FIRST:]
    out[...] = jnp.zeros_like(out)
    at_row = lax.broadcasted_iota(jnp.int32, out.shape, 0)
    at_col = lax.broadcasted_iota(jnp.int32, out.shape, 1)
    both = [(refs[s], s, 0) for s in range(FIRST)] + [(packed.at[s], s, 1) for s in range(FIRST)]
    for ref, s, other in both:
        devices = {d ^ other for d in adds[s]}
        core = me.core ^ other
        before, after = me.line - 1 + 2 * core, me.line + 1 - 2 * core
        row = (me.row, me.row, me.row, me.row ^ 1, me.row ^ 2)[s]
        line = (me.line, before, after, me.line, me.line)[s]
        row_blocks, col_blocks = ref.shape[0] // BLK, ref.shape[1] // BLK

        @pl.when(me.among(devices) & (row <= line))
        def _():
            zero = jnp.zeros((BLK, BLK), jnp.float32)
            total = zero
            for a in range(row_blocks):
                for b in range(col_blocks):
                    i, j = row * row_blocks + a, (2 * line + core) * col_blocks + b
                    block = ref[a * BLK : (a + 1) * BLK, b * BLK : (b + 1) * BLK].astype(jnp.float32)
                    block = jnp.where((i <= j) & kept(pattern, i, j), block, zero)
                    total += jnp.where(i == j, 1.0, 2.0) * (block * block)
            squares[...] = total
            diagonals[...] = zero

            @pl.when(row == line)
            def _():
                rows_at = lax.broadcasted_iota(jnp.int32, (BLK, BLK), 0)
                cols_at = lax.broadcasted_iota(jnp.int32, (BLK, BLK), 1)
                for b in range(col_blocks):
                    start = pl.multiple_of((core * col_blocks + b) * BLK, BLK)
                    block = ref[pl.ds(start, BLK), b * BLK : (b + 1) * BLK].astype(jnp.float32)
                    diagonals[...] += jnp.where(rows_at == cols_at, block, zero)

            owner = 8 * row + 2 * line + core
            for i, values in enumerate((diagonals, squares)):
                out[...] += jnp.where((at_row == i) & (at_col == owner), jnp.sum(values[...]) / order_size, 0.0)


def copy_kernel(source, out):
    out[...] = source[...]


def pack_kernel(*refs):
    out = refs[-1]
    for i, ref in enumerate(refs[:-1]):
        out[i] = ref[...]


def copy_kernel(source, out):
    out[...] = source[...]


def pack_kernel(*refs):
    out = refs[-1]
    for i, ref in enumerate(refs[:-1]):
        out[i] = ref[...]


def choose_kernel(sends, *refs):
    me = Place()
    held, outs = refs[:FIRST], refs[FIRST:]
    for out, send in zip(outs, sends):
        for s, ref in enumerate(held):
            devices = [d for d in send if send[d] == s]
            if devices:
                @pl.when(me.among(devices))
                def _():
                    out[...] = ref[...]


def pack_kernel(*refs):
    out = refs[-1]
    for i, ref in enumerate(refs[:-1]):
        out[i] = ref[...]


def place_tiles(uses, me, shards, keep, left, right, raw):
    tile, width = left.shape[0], right.shape[1]
    blocks, half_blocks = tile // BLK, width // BLK
    zero = jnp.zeros((BLK, BLK), left.dtype)

    def at_block(start):
        return pl.ds(start if isinstance(start, int) else pl.multiple_of(start, BLK), BLK)

    def stored(a, b):
        return raw[at_block((b // 2) * tile + a * BLK), at_block((b % 2) * BLK)]

    def direct(a, b):
        return raw[at_block(me.core * tile + a * BLK), at_block(b * BLK)]

    def mirrored(a, b):
        return raw[at_block((a // 2) * tile + (me.core * half_blocks + b) * BLK), at_block((a % 2) * BLK)].T

    left_ways = (
        stored,
        lambda a, b: stored(b, a).T,
        lambda a, b: jnp.where(a <= b, stored(a, b), stored(b, a).T),
    )
    right_ways = (
        direct,
        mirrored,
        lambda a, b: jnp.where(a <= me.core * half_blocks + b, direct(a, b), mirrored(a, b)),
    )

    def fill(panel, at, cols, u, block_of):
        j = u % 4

        def block_row(a, carry):
            for b in range(cols):
                rows, lanes = at_block(at[0] + a * BLK), at_block(at[1] + b * BLK)
                if u < 4:
                    flag = keep(panel, rows, lanes, me.row * blocks + a, j * blocks + b)
                else:
                    flag = keep(panel, rows, lanes, j * blocks + a, me.col * half_blocks + b)
                panel[rows, lanes] = jnp.where(flag, block_of(a, b), zero)
            return carry

        lax.fori_loop(0, blocks, block_row, 0)

    def fetch(half, ref):
        def block_row(a, carry):
            raw[at_block(half * tile + a * BLK), :] = ref[at_block(a * BLK), :]
            return carry

        lax.fori_loop(0, blocks, block_row, 0)

    for u, here in enumerate(uses):
        j = u % 4
        panel, at, cols, ways = (left, (0, j * tile), blocks, left_ways) if u < 4 else (
            right, (j * tile, 0), half_blocks, right_ways)

        def index(d):
            return d // 8 if u < 4 else (d % 8) // 2

        def above(d):
            return 2 if index(d) == j else int((index(d) > j) == (u < 4))

        if here:
            @pl.when(me.among(here))
            def _():
                for half in range(2):
                    for s in sorted({here[d][half] for d in here}):
                        @pl.when(me.among([d for d in here if here[d][half] == s]))
                        def _():
                            fetch(half, shards[s])

                for way in sorted({above(d) for d in here}):
                    @pl.when(me.among([d for d in here if above(d) == way]))
                    def _():
                        fill(panel, at, cols, u, ways[way])


def panels_kernel(uses, pattern, *refs):
    packed, left, right, keeps, raw = refs[FIRST:]
    me = Place()
    shards = list(refs[:FIRST]) + [packed.at[i] for i in range(FIRST)]

    def keep(panel, rows, lanes, i, j):
        return kept(pattern, i, j)

    place_tiles(uses[0], me, shards, keep, left, right, raw)
    tile, width = left.shape[0], right.shape[1]
    blocks, half_blocks = tile // BLK, width // BLK

    def flags(ref, row_at, col_at, cols, flag):
        def block_row(a, carry):
            for b in range(cols):
                value = jnp.where(flag(a, b), 1.0, 0.0).astype(ref.dtype)
                rows = pl.ds(pl.multiple_of(row_at + a * BLK, BLK), BLK)
                ref[rows, col_at + b * BLK : col_at + (b + 1) * BLK] = jnp.full((BLK, BLK), value, ref.dtype)
            return carry

        lax.fori_loop(0, blocks, block_row, 0)

    for u, later in enumerate(uses[1]):
        j = u % 4
        if later:
            @pl.when(me.among(later))
            def _():
                if u < 4:
                    flags(left, 0, j * tile, blocks, lambda a, b: kept(pattern, me.row * blocks + a, j * blocks + b))
                else:
                    flags(
                        right, j * tile, 0, half_blocks,
                        lambda a, b: kept(pattern, j * blocks + a, me.col * half_blocks + b),
                    )

    def square_kept(a, b):
        i, j = me.row * blocks + a, me.col * half_blocks + b
        return (i <= j) & kept(pattern, i, j)

    flags(keeps, 0, 0, half_blocks, square_kept)


def grid_product_kernel(uses, *refs):
    shards = refs[: 2 * SECOND]
    keeps, _, _, left, right, out, raw, result, sems = refs[2 * SECOND :]
    me = Place()

    def keep(panel, rows, lanes, i, j):
        return panel[rows, lanes] != 0

    place_tiles(uses[1], me, shards, keep, left, right, raw)
    height = out.shape[0]
    part = height // 2
    copies = []
    for c in range(2):
        rows = pl.ds(c * part, part)

        @pl.when(me.row <= me.line)
        def _():
            product = jnp.dot(left[rows, :], right[...], preferred_element_type=jnp.float32)
            result[rows, :] = jnp.where(
                keeps[rows, :].astype(jnp.float32) != 0, product, jnp.zeros_like(product)
            ).astype(result.dtype)

        @pl.when(me.row > me.line)
        def _():
            result[rows, :] = jnp.zeros((part, result.shape[1]), result.dtype)

        copies.append(pltpu.make_async_copy(result.at[rows], out.at[rows], sems.at[c]))
        copies[-1].start()
    for copy in copies:
        copy.wait()


def chip_grid(density, pattern):
    height, width = density.shape
    n_col = lax.axis_size("col")
    n_devices = lax.axis_size("row") * n_col
    order_size = width * lax.axis_size("col")
    dtype = density.dtype
    axes = ("row", "col")
    first, second, sends, adds, uses = schedule()
    shard = jax.ShapeDtypeStruct(density.shape, dtype)
    raw = pltpu.VMEM((2 * height, width), dtype)
    panels = [
        jax.ShapeDtypeStruct((height, order_size), dtype),
        jax.ShapeDtypeStruct((order_size, width), dtype),
    ]

    def call(kernel, out_shape, smem, args, scratch=(), out_specs=VMEM, aliases=None, cost=None):
        return pl.pallas_call(
            kernel,
            out_shape=out_shape,
            in_specs=[SMEM] * smem + [VMEM] * (len(args) - smem),
            out_specs=out_specs,
            scratch_shapes=list(scratch),
            input_output_aliases=aliases or {},
            compiler_params=GRID_PARAMS,
            cost_estimate=cost,
        )(*args)

    def share(value):
        return lax.ppermute(value, axes, [(d, d ^ 1) for d in range(n_devices)])

    def part_from(parts, row_bits, col_bits):
        return lax.ppermute(parts, axes, [(d, d ^ (row_bits * n_col + col_bits)) for d in range(n_devices)])

    came = [lax.ppermute(density, axes, pairs) for pairs in first]
    came[0], own = lax.optimization_barrier((came[0], call(copy_kernel, shard, 0, [density])))
    held = [own] + came
    chosen = call(functools.partial(choose_kernel, sends), [shard] * SECOND, 0, held, (), [VMEM] * SECOND)
    tied = lax.optimization_barrier((*chosen, *held))
    chosen, held = tied[:SECOND], list(tied[SECOND:])
    later = [lax.ppermute(value, axes, pairs) for value, pairs in zip(chosen, second)]
    packed = share(call(pack_kernel, jax.ShapeDtypeStruct((FIRST, height, width), dtype), 0, held))
    parts = call(
        functools.partial(partial_kernel, adds, order_size),
        jax.ShapeDtypeStruct((8, 128), jnp.float32),
        1,
        [pattern] + held + [packed],
        [pltpu.VMEM((BLK, BLK), jnp.float32)] * 2,
    )
    packed, parts = lax.optimization_barrier((packed, parts))
    received = part_from(parts, 3, 2)
    left, right, keeps = call(
        functools.partial(panels_kernel, uses), panels + [shard], 1, [pattern] + held + [packed], [raw], [VMEM] * 3
    )
    left, parts = lax.optimization_barrier((left, parts + received))
    received = part_from(parts, 0, 4)
    left, parts = lax.optimization_barrier((left, parts))
    shared = []
    for i in range(SECOND):
        later[i], left = lax.optimization_barrier((later[i], left))
        shared.append(share(later[i]))
    inputs = later + shared + [keeps, left, right]
    square = call(
        functools.partial(grid_product_kernel, uses),
        panels + [shard],
        0,
        inputs,
        [raw, pltpu.VMEM(density.shape, dtype), pltpu.SemaphoreType.DMA((2,))],
        [VMEM, VMEM, pl.BlockSpec(memory_space=pltpu.HBM)],
        {len(inputs) - 2: 0, len(inputs) - 1: 1},
    )[2]
    square, received = lax.optimization_barrier((square, received))
    traces = jnp.sum(parts[:2] + received[:2], axis=1)
    return (square, traces)


def per_device(density, pattern):
    if lax.axis_size("row") == 4 and lax.axis_size("col") == 8 and density.shape[0] == 2 * density.shape[1]:
        return chip_grid(density, pattern)
    return any_mesh(density, pattern)


def solution(mesh):
    placed = (P("row", "col"), P())
    return jax.shard_map(
        per_device, mesh=mesh, in_specs=placed, out_specs=(P("row", "col"), P()), check_vma=False
    )
```

```python
import functools
import jax
import jax.numpy as jnp
from jax import lax
from jax.experimental import pallas as pl
from jax.experimental.pallas import tpu as pltpu
from jax.sharding import PartitionSpec as P

BLK = 128
VMEM = pl.BlockSpec(memory_space=pltpu.VMEM)
SMEM = pl.BlockSpec(memory_space=pltpu.SMEM)
PARAMS = pltpu.CompilerParams(vmem_limit_bytes=40 * 2**20)


def symmetric_kernel(sub, place, pattern, density, *rest):
    pieces, full = rest[:sub], rest[sub]
    row, col = place[0], place[1]
    height, width = density.shape
    per_piece = width // BLK
    row_blocks = height // BLK
    own_slot = lax.rem(col, sub)
    on_diagonal = row == col // sub
    for t in range(sub):
        slot = lax.rem(own_slot + sub - t, sub)
        for a in range(per_piece):
            i = slot * per_piece + a
            block_row = row * row_blocks + i
            rows = pl.ds(pl.multiple_of(i * BLK, BLK), BLK)
            for b in range(per_piece):
                block_col = col * per_piece + b
                cols = pl.ds(b * BLK, BLK)
                mirror = pieces[t][b * BLK : (b + 1) * BLK, a * BLK : (a + 1) * BLK]
                if t == 0:
                    start = pl.multiple_of((own_slot * per_piece + b) * BLK, BLK)
                    mine = density[pl.ds(start, BLK), a * BLK : (a + 1) * BLK]
                    mirror = jnp.where(on_diagonal, mine, mirror)
                chosen = pattern[jnp.minimum(block_row, block_col), jnp.maximum(block_row, block_col)] != 0
                upper = (block_row == block_col) | ((block_row < block_col) & chosen)
                lower = (block_row > block_col) & chosen
                zero = jnp.zeros((BLK, BLK), full.dtype)
                value = jnp.where(lower, mirror.T, zero)
                full[rows, cols] = jnp.where(upper, density[rows, cols], value)


def product_kernel(lines, planes, place, pattern, *refs):
    left = refs[: 2 * lines]
    right = refs[2 * lines : 2 * lines + planes]
    out, panel = refs[2 * lines + planes :]
    row, col = place[0], place[1]
    height, width = out.shape
    core, line = lax.rem(col, 2), col // 2
    for d in range(planes):
        start = pl.multiple_of((row ^ d) * height, height)
        panel[pl.ds(start, height), :] = right[d][...]
    total = jnp.zeros((height, width), jnp.float32)
    for e in range(lines):
        for s in range(2):
            start = pl.multiple_of(((line ^ e) * 2 + (core ^ s)) * width, width)
            total += jnp.dot(
                left[2 * e + s][...],
                panel[pl.ds(start, width), :],
                preferred_element_type=jnp.float32,
            )
    for i in range(height // BLK):
        for j in range(width // BLK):
            block_row = row * (height // BLK) + i
            block_col = col * (width // BLK) + j
            kept = (block_row == block_col) | ((block_row < block_col) & (pattern[block_row, block_col] != 0))
            block = total[i * BLK : (i + 1) * BLK, j * BLK : (j + 1) * BLK]
            out[i * BLK : (i + 1) * BLK, j * BLK : (j + 1) * BLK] = jnp.where(
                kept, block, jnp.zeros_like(block)
            ).astype(out.dtype)


def block_weights(pattern, row, col, row_blocks, col_blocks):
    block_rows = row * row_blocks + jnp.arange(row_blocks)
    block_cols = col * col_blocks + jnp.arange(col_blocks)
    chosen = lax.dynamic_slice(pattern, (row * row_blocks, col * col_blocks), (row_blocks, col_blocks))
    diagonal = block_rows[:, None] == block_cols[None, :]
    strict = (block_cols[None, :] > block_rows[:, None]) & (chosen != 0)
    return jnp.where(diagonal, 1.0, jnp.where(strict, 2.0, 0.0)).astype(jnp.float32)


def any_mesh(density, pattern):
    n_row = lax.axis_size("row")
    n_col = lax.axis_size("col")
    sub = n_col // n_row
    row = lax.axis_index("row")
    col = lax.axis_index("col")
    height, width = density.shape
    order_size = width * n_col
    place = jnp.stack([row, col]).astype(jnp.int32)

    pieces = []
    for t in range(sub):
        pairs = []
        for q in range(n_row):
            for c in range(n_col):
                p = (c + t) % sub
                if c > q * sub + p:
                    pairs.append((q * n_col + c, (c // sub) * n_col + q * sub + p))
        start = lax.rem(col + t, sub) * width
        piece = lax.dynamic_slice_in_dim(density, start, width, 0)
        pieces.append(lax.ppermute(piece, ("row", "col"), pairs))
    full = pl.pallas_call(
        functools.partial(symmetric_kernel, sub),
        out_shape=jax.ShapeDtypeStruct(density.shape, density.dtype),
        in_specs=[SMEM, SMEM] + [VMEM] * (sub + 1),
        out_specs=VMEM,
        compiler_params=PARAMS,
    )(place, pattern, density, *pieces)

    weights = block_weights(pattern, row, col, height // BLK, width // BLK)
    values = density.astype(jnp.float32).reshape(height // BLK, BLK, width // BLK, BLK)
    squares = jnp.sum(values * values, axis=(1, 3))
    rows_at = row * height + jnp.arange(height)[:, None]
    cols_at = col * width + jnp.arange(width)[None, :]
    diagonal = jnp.where(rows_at == cols_at, density.astype(jnp.float32), 0.0)
    sums = jnp.stack([jnp.sum(diagonal), jnp.sum(jnp.where(weights > 0, weights * squares, 0.0))])
    step = 1
    while step < n_row:
        sums = sums + lax.ppermute(sums, "row", [(i, i ^ step) for i in range(n_row)])
        step *= 2
    step = 1
    while step < n_col:
        sums = sums + lax.ppermute(sums, "col", [(i, i ^ step) for i in range(n_col)])
        step *= 2
    traces = sums / order_size

    right = [full]
    for d in range(1, n_row):
        right.append(lax.ppermute(full, "row", [(i, i ^ d) for i in range(n_row)]))
    left = []
    for e in range(n_col // 2):
        shard = full
        if e > 0:
            shard = lax.ppermute(full, "col", [(i, i ^ (2 * e)) for i in range(n_col)])
        other = lax.ppermute(shard, "col", [(i, i ^ 1) for i in range(n_col)])
        left += [shard, other]
    square = pl.pallas_call(
        functools.partial(product_kernel, n_col // 2, n_row),
        out_shape=jax.ShapeDtypeStruct(density.shape, density.dtype),
        in_specs=[SMEM, SMEM] + [VMEM] * (len(left) + len(right)),
        out_specs=VMEM,
        scratch_shapes=[pltpu.VMEM((order_size, width), density.dtype)],
        compiler_params=PARAMS,
    )(place, pattern, *left, *right)
    return (square, traces)

GRID_PARAMS = pltpu.CompilerParams(vmem_limit_bytes=14 * 2**20)
USES = 8
FIRST = 5
SECOND = 3
SEEN = ((), (0,), (1, 3), (2,))

MESSAGES = (
    (0, (0, 0), 0, (0, 0, 0), (0, 3, 1)),
    (0, (0, 2), 0, (0, 1, 0), (0, 0, 0)),
    (0, (2, 2), 0, (0, 2, 0), (1, 2, 1)),
    (0, (0, 3), 1, (0, 2, 1), (0, 0, 1)),
    (0, (2, 3), 0, (0, 3, 0), (0, 2, 0)),
    (0, (0, 2), 1, (0, 3, 1), (2, 3, 1)),
    (0, (0, 0), 1, (1, 0, 1), (0, 2, 1)),
    (0, (1, 1), 0, (1, 2, 0), (1, 3, 0)),
    (0, (1, 3), 1, (1, 2, 1), (0, 1, 0)),
    (0, (1, 2), 0, (1, 3, 0), (2, 2, 0)),
    (0, (0, 1), 1, (2, 1, 1), (0, 3, 0)),
    (0, (0, 2), 0, (2, 2, 0), (2, 3, 0)),
    (0, (0, 3), 0, (2, 3, 0), (0, 1, 1)),
    (0, (1, 1), 1, (3, 1, 1), (1, 3, 1)),
    (0, (2, 2), 1, (3, 2, 1), (1, 2, 0)),
    (0, (1, 3), 1, (3, 3, 1), (1, 1, 1)),
    (1, (0, 0), 1, (0, 0, 1), (0, 3, 1)),
    (1, (0, 3), 0, (0, 2, 0), (0, 0, 0)),
    (1, (2, 3), 1, (0, 3, 1), (1, 3, 0)),
    (1, (0, 1), 1, (1, 1, 1), (1, 3, 1)),
    (1, (1, 3), 0, (1, 2, 0), (0, 1, 1)),
    (1, (1, 2), 0, (1, 3, 0), (2, 3, 0)),
    (1, (0, 0), 0, (2, 0, 0), (0, 2, 0)),
    (1, (0, 1), 0, (2, 1, 0), (0, 3, 0)),
    (1, (0, 2), 1, (2, 2, 1), (0, 0, 1)),
    (1, (0, 3), 0, (2, 3, 0), (3, 3, 1)),
    (1, (1, 2), 0, (3, 2, 0), (0, 1, 0)),
    (1, (1, 2), 1, (3, 2, 1), (2, 3, 1)),
    (1, (2, 3), 0, (3, 3, 0), (1, 2, 0)),
    (1, (2, 3), 1, (3, 3, 1), (1, 2, 1)),
    (2, (0, 1), 1, (0, 1, 1), (1, 2, 1)),
    (2, (0, 1), 0, (0, 2, 0), (1, 2, 0)),
    (2, (1, 3), 0, (0, 3, 0), (2, 3, 0)),
    (2, (0, 3), 1, (0, 3, 1), (0, 1, 0)),
    (2, (0, 1), 0, (1, 1, 0), (1, 3, 0)),
    (2, (1, 2), 1, (1, 1, 1), (0, 1, 1)),
    (2, (1, 3), 0, (1, 2, 0), (1, 1, 1)),
    (2, (3, 3), 0, (1, 3, 0), (0, 3, 0)),
    (2, (3, 3), 1, (1, 3, 1), (0, 3, 1)),
    (2, (2, 3), 1, (2, 2, 1), (0, 2, 1)),
    (2, (2, 3), 0, (2, 3, 0), (1, 3, 1)),
    (2, (0, 3), 1, (2, 3, 1), (3, 3, 0)),
    (2, (1, 2), 1, (3, 2, 1), (2, 2, 0)),
    (2, (1, 3), 1, (3, 3, 1), (2, 3, 1)),
)


def number(device):
    return 8 * device[0] + 2 * device[1] + device[2]


def wanted(r, z):
    if r > z:
        return [None] * USES
    return [(min(r, j), max(r, j)) for j in range(4)] + [(min(z, j), max(z, j)) for j in range(4)]


def first_round(devices):
    def ring(r, z, k, up):
        step = 1 if (k == 0) == up else -1
        return (r, z + step, k) if 0 <= z + step < 4 else (r, z, 1 - k)

    return [[(d, ring(*d, up)) for d in devices] for up in (True, False)] + [
        [((r, z, k), (r ^ bit, z, k)) for r, z, k in devices] for bit in (1, 2)
    ]


def closed(pairs, devices):
    sends, receives = {a for a, _ in pairs}, {b for _, b in pairs}
    ends = [d for d in devices if d not in sends]
    starts = [d for d in devices if d not in receives]

    def cost(a, b):
        return 1000 if a == b else (abs(a[1] - b[1]) + bin(a[0] ^ b[0]).count("1")) ** 2

    size = len(ends)
    u, v, row_of = [0] * (size + 1), [0] * (size + 1), [0] * (size + 1)
    for i in range(1, size + 1):
        row_of[0], col = i, 0
        least, before, done = [10**6] * (size + 1), [0] * (size + 1), [False] * (size + 1)
        while row_of[col]:
            done[col], row, delta, following = True, row_of[col], 10**6, 0
            for j in range(1, size + 1):
                if not done[j]:
                    slack = cost(ends[row - 1], starts[j - 1]) - u[row] - v[j]
                    if slack < least[j]:
                        least[j], before[j] = slack, col
                    if least[j] < delta:
                        delta, following = least[j], j
            for j in range(size + 1):
                if done[j]:
                    u[row_of[j]] += delta
                    v[j] -= delta
                else:
                    least[j] -= delta
            col = following
        while col:
            row_of[col] = row_of[before[col]]
            col = before[col]
    return pairs + [(ends[row_of[j] - 1], starts[j - 1]) for j in range(1, size + 1)]


def schedule():
    devices = [(r, z, k) for r in range(4) for z in range(4) for k in range(2)]
    first = first_round(devices)
    held = {d: [((d[0], d[1]), d[2])] for d in devices}
    for pairs in first:
        for a, b in pairs:
            held[b].append(((a[0], a[1]), a[2]))
    second = [[] for _ in range(SECOND)]
    later = {d: [None] * SECOND for d in devices}
    sends = [{} for _ in range(SECOND)]
    for i, tile, half, a, b in MESSAGES:
        second[i].append((a, b))
        sends[i][number(a)] = held[a].index((tile, half))
        later[b][i] = (tile, half)
    second = [closed(pairs, devices) for pairs in second]
    adds = [set() for _ in range(FIRST)]
    uses = [[{} for _ in range(USES)] for _ in range(2)]
    for d in devices:
        r, z, k = d
        added = {(r, z), (r ^ 1, z), (r ^ 2, z)} | {(r, j) for j in SEEN[z]}
        for s, (tile, half) in enumerate(held[d]):
            if tile in added and half == k and (s == 0 or tile != (r, z)):
                adds[s].add(number(d))
        for u, tile in enumerate(wanted(r, z)):
            for n, shards in enumerate((held, later)):
                here = shards[d] + shards[r, z, 1 - k]
                if tile and (tile, 0) in here and (tile, 1) in here and not any(number(d) in uses[m][u] for m in range(n)):
                    uses[n][u][number(d)] = (here.index((tile, 0)), here.index((tile, 1)))
            assert tile is None or any(number(d) in uses[n][u] for n in range(2))

    def flat(pairs):
        assert len({a for a, _ in pairs}) == len({b for _, b in pairs}) == len(devices)
        return [(number(a), number(b)) for a, b in pairs]

    return [flat(p) for p in first], [flat(p) for p in second], sends, adds, uses


class Place:
    def __init__(self):
        self.row, self.col = lax.axis_index("row"), lax.axis_index("col")
        self.line, self.core = self.col // 2, lax.rem(self.col, 2)
        self.number = self.row * 8 + self.col

    def among(self, devices):
        bits = sum(1 << d for d in devices)
        bits -= (bits >> 31) << 32
        return (lax.shift_right_logical(jnp.int32(bits), self.number) & 1) == 1


def kept(pattern, i, j):
    low, high = jnp.minimum(i, j), jnp.maximum(i, j)
    return (low == high) | (pattern[low, high] != 0)


def partial_kernel(adds, order_size, pattern, *refs):
    me = Place()
    packed, out = refs[FIRST:]
    out[...] = jnp.zeros_like(out)
    at_row = lax.broadcasted_iota(jnp.int32, out.shape, 0)
    at_col = lax.broadcasted_iota(jnp.int32, out.shape, 1)
    both = [(refs[s], s, 0) for s in range(FIRST)] + [(packed.at[s], s, 1) for s in range(FIRST)]
    for ref, s, other in both:
        devices = {d ^ other for d in adds[s]}
        core = me.core ^ other
        before, after = me.line - 1 + 2 * core, me.line + 1 - 2 * core
        row = (me.row, me.row, me.row, me.row ^ 1, me.row ^ 2)[s]
        line = (me.line, before, after, me.line, me.line)[s]
        row_blocks, col_blocks = ref.shape[0] // BLK, ref.shape[1] // BLK

        @pl.when(me.among(devices) & (row <= line))
        def _():
            zero = jnp.zeros((BLK, BLK), jnp.float32)
            total = zero
            for a in range(row_blocks):
                for b in range(col_blocks):
                    i, j = row * row_blocks + a, (2 * line + core) * col_blocks + b
                    block = ref[a * BLK : (a + 1) * BLK, b * BLK : (b + 1) * BLK].astype(jnp.float32)
                    block = jnp.where((i <= j) & kept(pattern, i, j), block, zero)
                    total += jnp.where(i == j, 1.0, 2.0) * (block * block)
            lane = at_col == 8 * row + 2 * line + core
            out[...] += jnp.where((at_row == 1) & lane, jnp.sum(total) / order_size, 0.0)

            @pl.when(row == line)
            def _():
                rows_at = lax.broadcasted_iota(jnp.int32, (BLK, BLK), 0)
                cols_at = lax.broadcasted_iota(jnp.int32, (BLK, BLK), 1)
                diagonals = zero
                for b in range(col_blocks):
                    start = pl.multiple_of((core * col_blocks + b) * BLK, BLK)
                    block = ref[pl.ds(start, BLK), b * BLK : (b + 1) * BLK].astype(jnp.float32)
                    diagonals += jnp.where(rows_at == cols_at, block, zero)
                out[...] += jnp.where((at_row == 0) & lane, jnp.sum(diagonals) / order_size, 0.0)


def copy_kernel(source, out):
    out[...] = source[...]


def pack_kernel(*refs):
    out = refs[-1]
    for i, ref in enumerate(refs[:-1]):
        out[i] = ref[...]


def copy_kernel(source, out):
    out[...] = source[...]


def pack_kernel(*refs):
    out = refs[-1]
    for i, ref in enumerate(refs[:-1]):
        out[i] = ref[...]


def choose_kernel(sends, *refs):
    me = Place()
    held, outs = refs[:FIRST], refs[FIRST:]
    for out, send in zip(outs, sends):
        for s, ref in enumerate(held):
            devices = [d for d in send if send[d] == s]
            if devices:
                @pl.when(me.among(devices))
                def _():
                    out[...] = ref[...]


def pack_kernel(*refs):
    out = refs[-1]
    for i, ref in enumerate(refs[:-1]):
        out[i] = ref[...]


def place_tiles(uses, me, shards, keep, left, right, raw):
    tile, width = left.shape[0], right.shape[1]
    blocks, half_blocks = tile // BLK, width // BLK
    zero = jnp.zeros((BLK, BLK), left.dtype)

    def stored(a, b):
        return raw[(b // 2) * tile + a * BLK : (b // 2) * tile + (a + 1) * BLK, (b % 2) * BLK : (b % 2 + 1) * BLK]

    def direct(a, b):
        start = pl.multiple_of(me.core * tile + a * BLK, BLK)
        return raw[pl.ds(start, BLK), b * BLK : (b + 1) * BLK]

    def mirrored(a, b):
        start = pl.multiple_of((a // 2) * tile + (me.core * half_blocks + b) * BLK, BLK)
        return raw[pl.ds(start, BLK), (a % 2) * BLK : (a % 2 + 1) * BLK].T

    left_ways = (
        stored,
        lambda a, b: stored(b, a).T,
        lambda a, b: stored(a, b) if a <= b else stored(b, a).T,
    )
    right_ways = (
        direct,
        mirrored,
        lambda a, b: jnp.where(a <= me.core * half_blocks + b, direct(a, b), mirrored(a, b)),
    )

    def fill(panel, at, cols, u, block_of):
        j = u % 4
        for a in range(blocks):
            for b in range(cols):
                rows = slice(at[0] + a * BLK, at[0] + (a + 1) * BLK)
                lanes = slice(at[1] + b * BLK, at[1] + (b + 1) * BLK)
                if u < 4:
                    flag = keep(panel, rows, lanes, me.row * blocks + a, j * blocks + b)
                else:
                    flag = keep(panel, rows, lanes, j * blocks + a, me.col * half_blocks + b)
                panel[rows, lanes] = jnp.where(flag, block_of(a, b), zero)

    for u, here in enumerate(uses):
        j = u % 4
        panel, at, cols, ways = (left, (0, j * tile), blocks, left_ways) if u < 4 else (
            right, (j * tile, 0), half_blocks, right_ways)

        def index(d):
            return d // 8 if u < 4 else (d % 8) // 2

        def above(d):
            return 2 if index(d) == j else int((index(d) > j) == (u < 4))

        if here:
            @pl.when(me.among(here))
            def _():
                for half in range(2):
                    for s in sorted({here[d][half] for d in here}):
                        @pl.when(me.among([d for d in here if here[d][half] == s]))
                        def _():
                            raw[half * tile : (half + 1) * tile, :] = shards[s][...]

                for way in sorted({above(d) for d in here}):
                    @pl.when(me.among([d for d in here if above(d) == way]))
                    def _():
                        fill(panel, at, cols, u, ways[way])


def panels_kernel(uses, pattern, *refs):
    packed, left, right, keeps, raw = refs[FIRST:]
    me = Place()
    shards = list(refs[:FIRST]) + [packed.at[i] for i in range(FIRST)]

    def keep(panel, rows, lanes, i, j):
        return kept(pattern, i, j)

    place_tiles(uses[0], me, shards, keep, left, right, raw)
    tile, width = left.shape[0], right.shape[1]
    blocks, half_blocks = tile // BLK, width // BLK

    def flags(ref, row_at, col_at, cols, flag):
        for a in range(blocks):
            for b in range(cols):
                value = jnp.where(flag(a, b), 1.0, 0.0).astype(ref.dtype)
                ref[row_at + a * BLK : row_at + (a + 1) * BLK, col_at + b * BLK : col_at + (b + 1) * BLK] = (
                    jnp.full((BLK, BLK), value, ref.dtype)
                )

    for u, later in enumerate(uses[1]):
        j = u % 4
        if later:
            @pl.when(me.among(later))
            def _():
                if u < 4:
                    flags(left, 0, j * tile, blocks, lambda a, b: kept(pattern, me.row * blocks + a, j * blocks + b))
                else:
                    flags(
                        right, j * tile, 0, half_blocks,
                        lambda a, b: kept(pattern, j * blocks + a, me.col * half_blocks + b),
                    )

    def square_kept(a, b):
        i, j = me.row * blocks + a, me.col * half_blocks + b
        return (i <= j) & kept(pattern, i, j)

    flags(keeps, 0, 0, half_blocks, square_kept)


def grid_product_kernel(uses, *refs):
    shards = refs[: 2 * SECOND]
    keeps, _, _, left, right, out, raw, result, sems = refs[2 * SECOND :]
    me = Place()

    def keep(panel, rows, lanes, i, j):
        return panel[rows, lanes] != 0

    place_tiles(uses[1], me, shards, keep, left, right, raw)
    height = out.shape[0]
    part = height // 2
    copies = []
    for c in range(2):
        rows = pl.ds(c * part, part)

        @pl.when(me.row <= me.line)
        def _():
            product = jnp.dot(left[rows, :], right[...], preferred_element_type=jnp.float32)
            result[rows, :] = jnp.where(
                keeps[rows, :].astype(jnp.float32) != 0, product, jnp.zeros_like(product)
            ).astype(result.dtype)

        @pl.when(me.row > me.line)
        def _():
            result[rows, :] = jnp.zeros((part, result.shape[1]), result.dtype)

        copies.append(pltpu.make_async_copy(result.at[rows], out.at[rows], sems.at[c]))
        copies[-1].start()
    for copy in copies:
        copy.wait()


def chip_grid(density, pattern):
    height, width = density.shape
    n_col = lax.axis_size("col")
    n_devices = lax.axis_size("row") * n_col
    order_size = width * lax.axis_size("col")
    dtype = density.dtype
    axes = ("row", "col")
    first, second, sends, adds, uses = schedule()
    shard = jax.ShapeDtypeStruct(density.shape, dtype)
    raw = pltpu.VMEM((2 * height, width), dtype)
    panels = [
        jax.ShapeDtypeStruct((height, order_size), dtype),
        jax.ShapeDtypeStruct((order_size, width), dtype),
    ]

    def call(kernel, out_shape, smem, args, scratch=(), out_specs=VMEM, aliases=None, cost=None):
        return pl.pallas_call(
            kernel,
            out_shape=out_shape,
            in_specs=[SMEM] * smem + [VMEM] * (len(args) - smem),
            out_specs=out_specs,
            scratch_shapes=list(scratch),
            input_output_aliases=aliases or {},
            compiler_params=GRID_PARAMS,
            cost_estimate=cost,
        )(*args)

    def share(value):
        return lax.ppermute(value, axes, [(d, d ^ 1) for d in range(n_devices)])

    def part_from(parts, row_bits, col_bits):
        return lax.ppermute(parts, axes, [(d, d ^ (row_bits * n_col + col_bits)) for d in range(n_devices)])

    came = [lax.ppermute(density, axes, pairs) for pairs in first]
    came[0], own = lax.optimization_barrier((came[0], call(copy_kernel, shard, 0, [density])))
    held = [own] + came
    chosen = call(functools.partial(choose_kernel, sends), [shard] * SECOND, 0, held, (), [VMEM] * SECOND)
    tied = lax.optimization_barrier((*chosen, *held))
    chosen, held = tied[:SECOND], list(tied[SECOND:])
    later = [lax.ppermute(value, axes, pairs) for value, pairs in zip(chosen, second)]
    packed = share(call(pack_kernel, jax.ShapeDtypeStruct((FIRST, height, width), dtype), 0, held))
    parts = call(
        functools.partial(partial_kernel, adds, order_size),
        jax.ShapeDtypeStruct((8, 128), jnp.float32),
        1,
        [pattern] + held + [packed],
    )
    packed, parts = lax.optimization_barrier((packed, parts))
    received = part_from(parts, 3, 2)
    left, right, keeps = call(
        functools.partial(panels_kernel, uses), panels + [shard], 1, [pattern] + held + [packed], [raw], [VMEM] * 3
    )
    left, parts = lax.optimization_barrier((left, parts + received))
    received = part_from(parts, 0, 4)
    left, parts = lax.optimization_barrier((left, parts))
    shared = []
    for i in range(SECOND):
        later[i], left = lax.optimization_barrier((later[i], left))
        shared.append(share(later[i]))
    inputs = later + shared + [keeps, left, right]
    square = call(
        functools.partial(grid_product_kernel, uses),
        panels + [shard],
        0,
        inputs,
        [raw, pltpu.VMEM(density.shape, dtype), pltpu.SemaphoreType.DMA((2,))],
        [VMEM, VMEM, pl.BlockSpec(memory_space=pltpu.HBM)],
        {len(inputs) - 2: 0, len(inputs) - 1: 1},
    )[2]
    square, received = lax.optimization_barrier((square, received))
    traces = jnp.sum(parts[:2] + received[:2], axis=1)
    return (square, traces)


def per_device(density, pattern):
    if lax.axis_size("row") == 4 and lax.axis_size("col") == 8 and density.shape[0] == 2 * density.shape[1]:
        return chip_grid(density, pattern)
    return any_mesh(density, pattern)


def solution(mesh):
    placed = (P("row", "col"), P())
    return jax.shard_map(
        per_device, mesh=mesh, in_specs=placed, out_specs=(P("row", "col"), P()), check_vma=False
    )
```

```python
import functools
import jax
import jax.numpy as jnp
from jax import lax
from jax.experimental import pallas as pl
from jax.experimental.pallas import tpu as pltpu
from jax.sharding import PartitionSpec as P

BLK = 128
VMEM = pl.BlockSpec(memory_space=pltpu.VMEM)
SMEM = pl.BlockSpec(memory_space=pltpu.SMEM)
PARAMS = pltpu.CompilerParams(vmem_limit_bytes=40 * 2**20)


def symmetric_kernel(sub, place, pattern, density, *rest):
    pieces, full = rest[:sub], rest[sub]
    row, col = place[0], place[1]
    height, width = density.shape
    per_piece = width // BLK
    row_blocks = height // BLK
    own_slot = lax.rem(col, sub)
    on_diagonal = row == col // sub
    for t in range(sub):
        slot = lax.rem(own_slot + sub - t, sub)
        for a in range(per_piece):
            i = slot * per_piece + a
            block_row = row * row_blocks + i
            rows = pl.ds(pl.multiple_of(i * BLK, BLK), BLK)
            for b in range(per_piece):
                block_col = col * per_piece + b
                cols = pl.ds(b * BLK, BLK)
                mirror = pieces[t][b * BLK : (b + 1) * BLK, a * BLK : (a + 1) * BLK]
                if t == 0:
                    start = pl.multiple_of((own_slot * per_piece + b) * BLK, BLK)
                    mine = density[pl.ds(start, BLK), a * BLK : (a + 1) * BLK]
                    mirror = jnp.where(on_diagonal, mine, mirror)
                chosen = pattern[jnp.minimum(block_row, block_col), jnp.maximum(block_row, block_col)] != 0
                upper = (block_row == block_col) | ((block_row < block_col) & chosen)
                lower = (block_row > block_col) & chosen
                zero = jnp.zeros((BLK, BLK), full.dtype)
                value = jnp.where(lower, mirror.T, zero)
                full[rows, cols] = jnp.where(upper, density[rows, cols], value)


def product_kernel(lines, planes, place, pattern, *refs):
    left = refs[: 2 * lines]
    right = refs[2 * lines : 2 * lines + planes]
    out, panel = refs[2 * lines + planes :]
    row, col = place[0], place[1]
    height, width = out.shape
    core, line = lax.rem(col, 2), col // 2
    for d in range(planes):
        start = pl.multiple_of((row ^ d) * height, height)
        panel[pl.ds(start, height), :] = right[d][...]
    total = jnp.zeros((height, width), jnp.float32)
    for e in range(lines):
        for s in range(2):
            start = pl.multiple_of(((line ^ e) * 2 + (core ^ s)) * width, width)
            total += jnp.dot(
                left[2 * e + s][...],
                panel[pl.ds(start, width), :],
                preferred_element_type=jnp.float32,
            )
    for i in range(height // BLK):
        for j in range(width // BLK):
            block_row = row * (height // BLK) + i
            block_col = col * (width // BLK) + j
            kept = (block_row == block_col) | ((block_row < block_col) & (pattern[block_row, block_col] != 0))
            block = total[i * BLK : (i + 1) * BLK, j * BLK : (j + 1) * BLK]
            out[i * BLK : (i + 1) * BLK, j * BLK : (j + 1) * BLK] = jnp.where(
                kept, block, jnp.zeros_like(block)
            ).astype(out.dtype)


def block_weights(pattern, row, col, row_blocks, col_blocks):
    block_rows = row * row_blocks + jnp.arange(row_blocks)
    block_cols = col * col_blocks + jnp.arange(col_blocks)
    chosen = lax.dynamic_slice(pattern, (row * row_blocks, col * col_blocks), (row_blocks, col_blocks))
    diagonal = block_rows[:, None] == block_cols[None, :]
    strict = (block_cols[None, :] > block_rows[:, None]) & (chosen != 0)
    return jnp.where(diagonal, 1.0, jnp.where(strict, 2.0, 0.0)).astype(jnp.float32)


def any_mesh(density, pattern):
    n_row = lax.axis_size("row")
    n_col = lax.axis_size("col")
    sub = n_col // n_row
    row = lax.axis_index("row")
    col = lax.axis_index("col")
    height, width = density.shape
    order_size = width * n_col
    place = jnp.stack([row, col]).astype(jnp.int32)

    pieces = []
    for t in range(sub):
        pairs = []
        for q in range(n_row):
            for c in range(n_col):
                p = (c + t) % sub
                if c > q * sub + p:
                    pairs.append((q * n_col + c, (c // sub) * n_col + q * sub + p))
        start = lax.rem(col + t, sub) * width
        piece = lax.dynamic_slice_in_dim(density, start, width, 0)
        pieces.append(lax.ppermute(piece, ("row", "col"), pairs))
    full = pl.pallas_call(
        functools.partial(symmetric_kernel, sub),
        out_shape=jax.ShapeDtypeStruct(density.shape, density.dtype),
        in_specs=[SMEM, SMEM] + [VMEM] * (sub + 1),
        out_specs=VMEM,
        compiler_params=PARAMS,
    )(place, pattern, density, *pieces)

    weights = block_weights(pattern, row, col, height // BLK, width // BLK)
    values = density.astype(jnp.float32).reshape(height // BLK, BLK, width // BLK, BLK)
    squares = jnp.sum(values * values, axis=(1, 3))
    rows_at = row * height + jnp.arange(height)[:, None]
    cols_at = col * width + jnp.arange(width)[None, :]
    diagonal = jnp.where(rows_at == cols_at, density.astype(jnp.float32), 0.0)
    sums = jnp.stack([jnp.sum(diagonal), jnp.sum(jnp.where(weights > 0, weights * squares, 0.0))])
    step = 1
    while step < n_row:
        sums = sums + lax.ppermute(sums, "row", [(i, i ^ step) for i in range(n_row)])
        step *= 2
    step = 1
    while step < n_col:
        sums = sums + lax.ppermute(sums, "col", [(i, i ^ step) for i in range(n_col)])
        step *= 2
    traces = sums / order_size

    right = [full]
    for d in range(1, n_row):
        right.append(lax.ppermute(full, "row", [(i, i ^ d) for i in range(n_row)]))
    left = []
    for e in range(n_col // 2):
        shard = full
        if e > 0:
            shard = lax.ppermute(full, "col", [(i, i ^ (2 * e)) for i in range(n_col)])
        other = lax.ppermute(shard, "col", [(i, i ^ 1) for i in range(n_col)])
        left += [shard, other]
    square = pl.pallas_call(
        functools.partial(product_kernel, n_col // 2, n_row),
        out_shape=jax.ShapeDtypeStruct(density.shape, density.dtype),
        in_specs=[SMEM, SMEM] + [VMEM] * (len(left) + len(right)),
        out_specs=VMEM,
        scratch_shapes=[pltpu.VMEM((order_size, width), density.dtype)],
        compiler_params=PARAMS,
    )(place, pattern, *left, *right)
    return (square, traces)

GRID_PARAMS = pltpu.CompilerParams(vmem_limit_bytes=14 * 2**20)
USES = 8
FIRST = 5
SECOND = 3
SEEN = ((), (0,), (1, 3), (2,))

MESSAGES = (
    (0, (0, 0), 1, (0, 0, 1), (0, 3, 1)),
    (0, (0, 3), 0, (0, 2, 0), (0, 0, 0)),
    (0, (0, 3), 1, (0, 2, 1), (0, 0, 1)),
    (0, (2, 3), 0, (0, 3, 0), (0, 2, 0)),
    (0, (0, 2), 1, (0, 3, 1), (2, 3, 1)),
    (0, (0, 1), 0, (1, 1, 0), (1, 3, 1)),
    (0, (1, 2), 0, (1, 2, 0), (2, 2, 0)),
    (0, (1, 3), 1, (1, 3, 1), (0, 1, 1)),
    (0, (0, 0), 0, (2, 0, 0), (0, 2, 1)),
    (0, (0, 1), 0, (2, 1, 0), (0, 3, 0)),
    (0, (0, 2), 0, (2, 2, 0), (2, 3, 0)),
    (0, (0, 3), 0, (2, 3, 0), (0, 1, 0)),
    (0, (1, 1), 1, (3, 1, 1), (1, 3, 0)),
    (0, (2, 2), 0, (3, 2, 0), (1, 2, 0)),
    (0, (2, 2), 1, (3, 2, 1), (1, 2, 1)),
    (0, (1, 3), 1, (3, 3, 1), (1, 1, 0)),
    (1, (0, 0), 0, (0, 0, 0), (0, 3, 1)),
    (1, (0, 2), 0, (0, 1, 0), (0, 0, 0)),
    (1, (0, 1), 1, (0, 2, 1), (1, 3, 1)),
    (1, (2, 3), 0, (0, 3, 0), (1, 2, 0)),
    (1, (2, 3), 1, (0, 3, 1), (1, 3, 0)),
    (1, (0, 0), 1, (1, 0, 1), (0, 2, 0)),
    (1, (1, 3), 0, (1, 2, 0), (0, 1, 0)),
    (1, (1, 2), 0, (1, 3, 0), (2, 3, 1)),
    (1, (1, 2), 1, (1, 3, 1), (2, 3, 0)),
    (1, (0, 1), 1, (2, 1, 1), (0, 3, 0)),
    (1, (0, 2), 1, (2, 2, 1), (0, 0, 1)),
    (1, (0, 3), 0, (2, 3, 0), (3, 3, 0)),
    (1, (1, 2), 0, (3, 2, 0), (0, 1, 1)),
    (1, (2, 3), 1, (3, 3, 1), (1, 2, 1)),
    (2, (0, 1), 1, (0, 1, 1), (1, 2, 1)),
    (2, (0, 1), 0, (0, 2, 0), (1, 2, 0)),
    (2, (1, 3), 0, (0, 3, 0), (2, 3, 0)),
    (2, (0, 3), 1, (0, 3, 1), (0, 1, 1)),
    (2, (1, 1), 0, (1, 1, 0), (1, 3, 1)),
    (2, (1, 2), 1, (1, 1, 1), (0, 1, 0)),
    (2, (1, 3), 0, (1, 2, 0), (1, 1, 1)),
    (2, (1, 2), 1, (1, 2, 1), (2, 2, 0)),
    (2, (3, 3), 1, (1, 3, 1), (0, 3, 1)),
    (2, (2, 3), 1, (2, 2, 1), (0, 2, 1)),
    (2, (3, 3), 0, (2, 3, 0), (0, 3, 0)),
    (2, (0, 3), 1, (2, 3, 1), (3, 3, 0)),
    (2, (2, 3), 0, (3, 3, 0), (1, 3, 0)),
    (2, (1, 3), 1, (3, 3, 1), (2, 3, 1)),
)


def number(device):
    return 8 * device[0] + 2 * device[1] + device[2]


def wanted(r, z):
    if r > z:
        return [None] * USES
    return [(min(r, j), max(r, j)) for j in range(4)] + [(min(z, j), max(z, j)) for j in range(4)]


def first_round(devices):
    def ring(r, z, k, up):
        step = 1 if (k == 0) == up else -1
        return (r, z + step, k) if 0 <= z + step < 4 else (r, z, 1 - k)

    return [[(d, ring(*d, up)) for d in devices] for up in (True, False)] + [
        [((r, z, k), (r ^ bit, z, k)) for r, z, k in devices] for bit in (1, 2)
    ]


def closed(pairs, devices):
    sends, receives = {a for a, _ in pairs}, {b for _, b in pairs}
    ends = [d for d in devices if d not in sends]
    starts = [d for d in devices if d not in receives]

    def cost(a, b):
        return 1000 if a == b else (abs(a[1] - b[1]) + bin(a[0] ^ b[0]).count("1")) ** 2

    size = len(ends)
    u, v, row_of = [0] * (size + 1), [0] * (size + 1), [0] * (size + 1)
    for i in range(1, size + 1):
        row_of[0], col = i, 0
        least, before, done = [10**6] * (size + 1), [0] * (size + 1), [False] * (size + 1)
        while row_of[col]:
            done[col], row, delta, following = True, row_of[col], 10**6, 0
            for j in range(1, size + 1):
                if not done[j]:
                    slack = cost(ends[row - 1], starts[j - 1]) - u[row] - v[j]
                    if slack < least[j]:
                        least[j], before[j] = slack, col
                    if least[j] < delta:
                        delta, following = least[j], j
            for j in range(size + 1):
                if done[j]:
                    u[row_of[j]] += delta
                    v[j] -= delta
                else:
                    least[j] -= delta
            col = following
        while col:
            row_of[col] = row_of[before[col]]
            col = before[col]
    return pairs + [(ends[row_of[j] - 1], starts[j - 1]) for j in range(1, size + 1)]


def schedule():
    devices = [(r, z, k) for r in range(4) for z in range(4) for k in range(2)]
    first = first_round(devices)
    held = {d: [((d[0], d[1]), d[2])] for d in devices}
    for pairs in first:
        for a, b in pairs:
            held[b].append(((a[0], a[1]), a[2]))
    second = [[] for _ in range(SECOND)]
    later = {d: [None] * SECOND for d in devices}
    sends = [{} for _ in range(SECOND)]
    for i, tile, half, a, b in MESSAGES:
        second[i].append((a, b))
        sends[i][number(a)] = held[a].index((tile, half))
        later[b][i] = (tile, half)
    second = [closed(pairs, devices) for pairs in second]
    adds = [set() for _ in range(FIRST)]
    uses = [[{} for _ in range(USES)] for _ in range(2)]
    for d in devices:
        r, z, k = d
        added = {(r, z), (r ^ 1, z), (r ^ 2, z)} | {(r, j) for j in SEEN[z]}
        for s, (tile, half) in enumerate(held[d]):
            if tile in added and half == k and (s == 0 or tile != (r, z)):
                adds[s].add(number(d))
        for u, tile in enumerate(wanted(r, z)):
            for n, shards in enumerate((held, later)):
                here = shards[d] + shards[r, z, 1 - k]
                if tile and (tile, 0) in here and (tile, 1) in here and not any(number(d) in uses[m][u] for m in range(n)):
                    uses[n][u][number(d)] = (here.index((tile, 0)), here.index((tile, 1)))
            assert tile is None or any(number(d) in uses[n][u] for n in range(2))

    def flat(pairs):
        assert len({a for a, _ in pairs}) == len({b for _, b in pairs}) == len(devices)
        return [(number(a), number(b)) for a, b in pairs]

    return [flat(p) for p in first], [flat(p) for p in second], sends, adds, uses


class Place:
    def __init__(self):
        self.row, self.col = lax.axis_index("row"), lax.axis_index("col")
        self.line, self.core = self.col // 2, lax.rem(self.col, 2)
        self.number = self.row * 8 + self.col

    def among(self, devices):
        bits = sum(1 << d for d in devices)
        bits -= (bits >> 31) << 32
        return (lax.shift_right_logical(jnp.int32(bits), self.number) & 1) == 1


def kept(pattern, i, j):
    low, high = jnp.minimum(i, j), jnp.maximum(i, j)
    return (low == high) | (pattern[low, high] != 0)


def partial_kernel(adds, order_size, pattern, *refs):
    me = Place()
    packed, out = refs[FIRST:]
    out[...] = jnp.zeros_like(out)
    at_row = lax.broadcasted_iota(jnp.int32, out.shape, 0)
    at_col = lax.broadcasted_iota(jnp.int32, out.shape, 1)
    both = [(refs[s], s, 0) for s in range(FIRST)] + [(packed.at[s], s, 1) for s in range(FIRST)]
    for ref, s, other in both:
        devices = {d ^ other for d in adds[s]}
        core = me.core ^ other
        before, after = me.line - 1 + 2 * core, me.line + 1 - 2 * core
        row = (me.row, me.row, me.row, me.row ^ 1, me.row ^ 2)[s]
        line = (me.line, before, after, me.line, me.line)[s]
        row_blocks, col_blocks = ref.shape[0] // BLK, ref.shape[1] // BLK

        @pl.when(me.among(devices) & (row <= line))
        def _():
            zero = jnp.zeros((BLK, BLK), jnp.float32)
            total = zero
            for a in range(row_blocks):
                for b in range(col_blocks):
                    i, j = row * row_blocks + a, (2 * line + core) * col_blocks + b
                    block = ref[a * BLK : (a + 1) * BLK, b * BLK : (b + 1) * BLK].astype(jnp.float32)
                    block = jnp.where((i <= j) & kept(pattern, i, j), block, zero)
                    total += jnp.where(i == j, 1.0, 2.0) * (block * block)
            lane = at_col == 8 * row + 2 * line + core
            out[...] += jnp.where((at_row == 1) & lane, jnp.sum(total) / order_size, 0.0)

            @pl.when(row == line)
            def _():
                rows_at = lax.broadcasted_iota(jnp.int32, (BLK, BLK), 0)
                cols_at = lax.broadcasted_iota(jnp.int32, (BLK, BLK), 1)
                diagonals = zero
                for b in range(col_blocks):
                    start = pl.multiple_of((core * col_blocks + b) * BLK, BLK)
                    block = ref[pl.ds(start, BLK), b * BLK : (b + 1) * BLK].astype(jnp.float32)
                    diagonals += jnp.where(rows_at == cols_at, block, zero)
                out[...] += jnp.where((at_row == 0) & lane, jnp.sum(diagonals) / order_size, 0.0)


def copy_kernel(source, out):
    out[...] = source[...]


def pack_kernel(*refs):
    out = refs[-1]
    for i, ref in enumerate(refs[:-1]):
        out[i] = ref[...]


def copy_kernel(source, out):
    out[...] = source[...]


def pack_kernel(*refs):
    out = refs[-1]
    for i, ref in enumerate(refs[:-1]):
        out[i] = ref[...]


def choose_kernel(sends, *refs):
    me = Place()
    held, outs = refs[:FIRST], refs[FIRST:]
    for out, send in zip(outs, sends):
        for s, ref in enumerate(held):
            devices = [d for d in send if send[d] == s]
            if devices:
                @pl.when(me.among(devices))
                def _():
                    out[...] = ref[...]


def pack_kernel(*refs):
    out = refs[-1]
    for i, ref in enumerate(refs[:-1]):
        out[i] = ref[...]


def place_tiles(uses, me, shards, keep, left, right, raw):
    tile, width = left.shape[0], right.shape[1]
    blocks, half_blocks = tile // BLK, width // BLK
    zero = jnp.zeros((BLK, BLK), left.dtype)

    def stored(a, b):
        return raw[(b // 2) * tile + a * BLK : (b // 2) * tile + (a + 1) * BLK, (b % 2) * BLK : (b % 2 + 1) * BLK]

    def direct(a, b):
        start = pl.multiple_of(me.core * tile + a * BLK, BLK)
        return raw[pl.ds(start, BLK), b * BLK : (b + 1) * BLK]

    def mirrored(a, b):
        start = pl.multiple_of((a // 2) * tile + (me.core * half_blocks + b) * BLK, BLK)
        return raw[pl.ds(start, BLK), (a % 2) * BLK : (a % 2 + 1) * BLK].T

    left_ways = (
        stored,
        lambda a, b: stored(b, a).T,
        lambda a, b: stored(a, b) if a <= b else stored(b, a).T,
    )
    right_ways = (
        direct,
        mirrored,
        lambda a, b: jnp.where(a <= me.core * half_blocks + b, direct(a, b), mirrored(a, b)),
    )

    def fill(panel, at, cols, u, block_of):
        j = u % 4
        for a in range(blocks):
            for b in range(cols):
                rows = slice(at[0] + a * BLK, at[0] + (a + 1) * BLK)
                lanes = slice(at[1] + b * BLK, at[1] + (b + 1) * BLK)
                if u < 4:
                    flag = keep(panel, rows, lanes, me.row * blocks + a, j * blocks + b)
                else:
                    flag = keep(panel, rows, lanes, j * blocks + a, me.col * half_blocks + b)
                panel[rows, lanes] = jnp.where(flag, block_of(a, b), zero)

    for u, here in enumerate(uses):
        j = u % 4
        panel, at, cols, ways = (left, (0, j * tile), blocks, left_ways) if u < 4 else (
            right, (j * tile, 0), half_blocks, right_ways)

        def index(d):
            return d // 8 if u < 4 else (d % 8) // 2

        def above(d):
            return 2 if index(d) == j else int((index(d) > j) == (u < 4))

        if here:
            @pl.when(me.among(here))
            def _():
                for half in range(2):
                    for s in sorted({here[d][half] for d in here}):
                        @pl.when(me.among([d for d in here if here[d][half] == s]))
                        def _():
                            raw[half * tile : (half + 1) * tile, :] = shards[s][...]

                for way in sorted({above(d) for d in here}):
                    @pl.when(me.among([d for d in here if above(d) == way]))
                    def _():
                        fill(panel, at, cols, u, ways[way])


def panels_kernel(uses, pattern, *refs):
    packed, left, right, keeps, raw = refs[FIRST:]
    me = Place()
    shards = list(refs[:FIRST]) + [packed.at[i] for i in range(FIRST)]

    def keep(panel, rows, lanes, i, j):
        return kept(pattern, i, j)

    place_tiles(uses[0], me, shards, keep, left, right, raw)
    tile, width = left.shape[0], right.shape[1]
    blocks, half_blocks = tile // BLK, width // BLK

    def flags(ref, row_at, col_at, cols, flag):
        for a in range(blocks):
            for b in range(cols):
                value = jnp.where(flag(a, b), 1.0, 0.0).astype(ref.dtype)
                ref[row_at + a * BLK : row_at + (a + 1) * BLK, col_at + b * BLK : col_at + (b + 1) * BLK] = (
                    jnp.full((BLK, BLK), value, ref.dtype)
                )

    for u, later in enumerate(uses[1]):
        j = u % 4
        if later:
            @pl.when(me.among(later))
            def _():
                if u < 4:
                    flags(left, 0, j * tile, blocks, lambda a, b: kept(pattern, me.row * blocks + a, j * blocks + b))
                else:
                    flags(
                        right, j * tile, 0, half_blocks,
                        lambda a, b: kept(pattern, j * blocks + a, me.col * half_blocks + b),
                    )

    def square_kept(a, b):
        i, j = me.row * blocks + a, me.col * half_blocks + b
        return (i <= j) & kept(pattern, i, j)

    flags(keeps, 0, 0, half_blocks, square_kept)


def grid_product_kernel(uses, *refs):
    shards = refs[: 2 * SECOND]
    keeps, _, _, left, right, out, raw, result, sems = refs[2 * SECOND :]
    me = Place()

    def keep(panel, rows, lanes, i, j):
        return panel[rows, lanes] != 0

    place_tiles(uses[1], me, shards, keep, left, right, raw)
    height = out.shape[0]
    part = height // 2
    copies = []
    for c in range(2):
        rows = pl.ds(c * part, part)

        @pl.when(me.row <= me.line)
        def _():
            product = jnp.dot(left[rows, :], right[...], preferred_element_type=jnp.float32)
            result[rows, :] = jnp.where(
                keeps[rows, :].astype(jnp.float32) != 0, product, jnp.zeros_like(product)
            ).astype(result.dtype)

        @pl.when(me.row > me.line)
        def _():
            result[rows, :] = jnp.zeros((part, result.shape[1]), result.dtype)

        copies.append(pltpu.make_async_copy(result.at[rows], out.at[rows], sems.at[c]))
        copies[-1].start()
    for copy in copies:
        copy.wait()


def chip_grid(density, pattern):
    height, width = density.shape
    n_col = lax.axis_size("col")
    n_devices = lax.axis_size("row") * n_col
    order_size = width * lax.axis_size("col")
    dtype = density.dtype
    axes = ("row", "col")
    first, second, sends, adds, uses = schedule()
    shard = jax.ShapeDtypeStruct(density.shape, dtype)
    raw = pltpu.VMEM((2 * height, width), dtype)
    panels = [
        jax.ShapeDtypeStruct((height, order_size), dtype),
        jax.ShapeDtypeStruct((order_size, width), dtype),
    ]

    def call(kernel, out_shape, smem, args, scratch=(), out_specs=VMEM, aliases=None, cost=None):
        return pl.pallas_call(
            kernel,
            out_shape=out_shape,
            in_specs=[SMEM] * smem + [VMEM] * (len(args) - smem),
            out_specs=out_specs,
            scratch_shapes=list(scratch),
            input_output_aliases=aliases or {},
            compiler_params=GRID_PARAMS,
            cost_estimate=cost,
        )(*args)

    def share(value):
        return lax.ppermute(value, axes, [(d, d ^ 1) for d in range(n_devices)])

    def part_from(parts, row_bits, col_bits):
        return lax.ppermute(parts, axes, [(d, d ^ (row_bits * n_col + col_bits)) for d in range(n_devices)])

    came = [lax.ppermute(density, axes, pairs) for pairs in first]
    came[0], own = lax.optimization_barrier((came[0], call(copy_kernel, shard, 0, [density])))
    held = [own] + came
    chosen = call(functools.partial(choose_kernel, sends), [shard] * SECOND, 0, held, (), [VMEM] * SECOND)
    tied = lax.optimization_barrier((*chosen, *held))
    chosen, held = tied[:SECOND], list(tied[SECOND:])
    later = [lax.ppermute(value, axes, pairs) for value, pairs in zip(chosen, second)]
    packed = share(call(pack_kernel, jax.ShapeDtypeStruct((FIRST, height, width), dtype), 0, held))
    parts = call(
        functools.partial(partial_kernel, adds, order_size),
        jax.ShapeDtypeStruct((8, 128), jnp.float32),
        1,
        [pattern] + held + [packed],
    )
    packed, parts = lax.optimization_barrier((packed, parts))
    received = part_from(parts, 3, 2)
    left, right, keeps = call(
        functools.partial(panels_kernel, uses), panels + [shard], 1, [pattern] + held + [packed], [raw], [VMEM] * 3
    )
    left, parts = lax.optimization_barrier((left, parts + received))
    received = part_from(parts, 0, 4)
    left, parts = lax.optimization_barrier((left, parts))
    shared = []
    for i in range(SECOND):
        later[i], left = lax.optimization_barrier((later[i], left))
        shared.append(share(later[i]))
    inputs = later + shared + [keeps, left, right]
    square = call(
        functools.partial(grid_product_kernel, uses),
        panels + [shard],
        0,
        inputs,
        [raw, pltpu.VMEM(density.shape, dtype), pltpu.SemaphoreType.DMA((2,))],
        [VMEM, VMEM, pl.BlockSpec(memory_space=pltpu.HBM)],
        {len(inputs) - 2: 0, len(inputs) - 1: 1},
    )[2]
    square, received = lax.optimization_barrier((square, received))
    traces = jnp.sum(parts[:2] + received[:2], axis=1)
    return (square, traces)


def per_device(density, pattern):
    if lax.axis_size("row") == 4 and lax.axis_size("col") == 8 and density.shape[0] == 2 * density.shape[1]:
        return chip_grid(density, pattern)
    return any_mesh(density, pattern)


def solution(mesh):
    placed = (P("row", "col"), P())
    return jax.shard_map(
        per_device, mesh=mesh, in_specs=placed, out_specs=(P("row", "col"), P()), check_vma=False
    )
```

```python
import functools
import jax
import jax.numpy as jnp
from jax import lax
from jax.experimental import pallas as pl
from jax.experimental.pallas import tpu as pltpu
from jax.sharding import PartitionSpec as P

BLK = 128
VMEM = pl.BlockSpec(memory_space=pltpu.VMEM)
SMEM = pl.BlockSpec(memory_space=pltpu.SMEM)
PARAMS = pltpu.CompilerParams(vmem_limit_bytes=40 * 2**20)


def symmetric_kernel(sub, place, pattern, density, *rest):
    pieces, full = rest[:sub], rest[sub]
    row, col = place[0], place[1]
    height, width = density.shape
    per_piece = width // BLK
    row_blocks = height // BLK
    own_slot = lax.rem(col, sub)
    on_diagonal = row == col // sub
    for t in range(sub):
        slot = lax.rem(own_slot + sub - t, sub)
        for a in range(per_piece):
            i = slot * per_piece + a
            block_row = row * row_blocks + i
            rows = pl.ds(pl.multiple_of(i * BLK, BLK), BLK)
            for b in range(per_piece):
                block_col = col * per_piece + b
                cols = pl.ds(b * BLK, BLK)
                mirror = pieces[t][b * BLK : (b + 1) * BLK, a * BLK : (a + 1) * BLK]
                if t == 0:
                    start = pl.multiple_of((own_slot * per_piece + b) * BLK, BLK)
                    mine = density[pl.ds(start, BLK), a * BLK : (a + 1) * BLK]
                    mirror = jnp.where(on_diagonal, mine, mirror)
                chosen = pattern[jnp.minimum(block_row, block_col), jnp.maximum(block_row, block_col)] != 0
                upper = (block_row == block_col) | ((block_row < block_col) & chosen)
                lower = (block_row > block_col) & chosen
                zero = jnp.zeros((BLK, BLK), full.dtype)
                value = jnp.where(lower, mirror.T, zero)
                full[rows, cols] = jnp.where(upper, density[rows, cols], value)


def product_kernel(lines, planes, place, pattern, *refs):
    left = refs[: 2 * lines]
    right = refs[2 * lines : 2 * lines + planes]
    out, panel = refs[2 * lines + planes :]
    row, col = place[0], place[1]
    height, width = out.shape
    core, line = lax.rem(col, 2), col // 2
    for d in range(planes):
        start = pl.multiple_of((row ^ d) * height, height)
        panel[pl.ds(start, height), :] = right[d][...]
    total = jnp.zeros((height, width), jnp.float32)
    for e in range(lines):
        for s in range(2):
            start = pl.multiple_of(((line ^ e) * 2 + (core ^ s)) * width, width)
            total += jnp.dot(
                left[2 * e + s][...],
                panel[pl.ds(start, width), :],
                preferred_element_type=jnp.float32,
            )
    for i in range(height // BLK):
        for j in range(width // BLK):
            block_row = row * (height // BLK) + i
            block_col = col * (width // BLK) + j
            kept = (block_row == block_col) | ((block_row < block_col) & (pattern[block_row, block_col] != 0))
            block = total[i * BLK : (i + 1) * BLK, j * BLK : (j + 1) * BLK]
            out[i * BLK : (i + 1) * BLK, j * BLK : (j + 1) * BLK] = jnp.where(
                kept, block, jnp.zeros_like(block)
            ).astype(out.dtype)


def block_weights(pattern, row, col, row_blocks, col_blocks):
    block_rows = row * row_blocks + jnp.arange(row_blocks)
    block_cols = col * col_blocks + jnp.arange(col_blocks)
    chosen = lax.dynamic_slice(pattern, (row * row_blocks, col * col_blocks), (row_blocks, col_blocks))
    diagonal = block_rows[:, None] == block_cols[None, :]
    strict = (block_cols[None, :] > block_rows[:, None]) & (chosen != 0)
    return jnp.where(diagonal, 1.0, jnp.where(strict, 2.0, 0.0)).astype(jnp.float32)


def any_mesh(density, pattern):
    n_row = lax.axis_size("row")
    n_col = lax.axis_size("col")
    sub = n_col // n_row
    row = lax.axis_index("row")
    col = lax.axis_index("col")
    height, width = density.shape
    order_size = width * n_col
    place = jnp.stack([row, col]).astype(jnp.int32)

    pieces = []
    for t in range(sub):
        pairs = []
        for q in range(n_row):
            for c in range(n_col):
                p = (c + t) % sub
                if c > q * sub + p:
                    pairs.append((q * n_col + c, (c // sub) * n_col + q * sub + p))
        start = lax.rem(col + t, sub) * width
        piece = lax.dynamic_slice_in_dim(density, start, width, 0)
        pieces.append(lax.ppermute(piece, ("row", "col"), pairs))
    full = pl.pallas_call(
        functools.partial(symmetric_kernel, sub),
        out_shape=jax.ShapeDtypeStruct(density.shape, density.dtype),
        in_specs=[SMEM, SMEM] + [VMEM] * (sub + 1),
        out_specs=VMEM,
        compiler_params=PARAMS,
    )(place, pattern, density, *pieces)

    weights = block_weights(pattern, row, col, height // BLK, width // BLK)
    values = density.astype(jnp.float32).reshape(height // BLK, BLK, width // BLK, BLK)
    squares = jnp.sum(values * values, axis=(1, 3))
    rows_at = row * height + jnp.arange(height)[:, None]
    cols_at = col * width + jnp.arange(width)[None, :]
    diagonal = jnp.where(rows_at == cols_at, density.astype(jnp.float32), 0.0)
    sums = jnp.stack([jnp.sum(diagonal), jnp.sum(jnp.where(weights > 0, weights * squares, 0.0))])
    step = 1
    while step < n_row:
        sums = sums + lax.ppermute(sums, "row", [(i, i ^ step) for i in range(n_row)])
        step *= 2
    step = 1
    while step < n_col:
        sums = sums + lax.ppermute(sums, "col", [(i, i ^ step) for i in range(n_col)])
        step *= 2
    traces = sums / order_size

    right = [full]
    for d in range(1, n_row):
        right.append(lax.ppermute(full, "row", [(i, i ^ d) for i in range(n_row)]))
    left = []
    for e in range(n_col // 2):
        shard = full
        if e > 0:
            shard = lax.ppermute(full, "col", [(i, i ^ (2 * e)) for i in range(n_col)])
        other = lax.ppermute(shard, "col", [(i, i ^ 1) for i in range(n_col)])
        left += [shard, other]
    square = pl.pallas_call(
        functools.partial(product_kernel, n_col // 2, n_row),
        out_shape=jax.ShapeDtypeStruct(density.shape, density.dtype),
        in_specs=[SMEM, SMEM] + [VMEM] * (len(left) + len(right)),
        out_specs=VMEM,
        scratch_shapes=[pltpu.VMEM((order_size, width), density.dtype)],
        compiler_params=PARAMS,
    )(place, pattern, *left, *right)
    return (square, traces)

GRID_PARAMS = pltpu.CompilerParams(vmem_limit_bytes=14 * 2**20)
USES = 8
FIRST = 5
SECOND = 3
HEARD = (
    ((2, 0), (0, 3), (0, 1), (1, 3), (0, 2), (3, 0), (3, 2), (1, 0), (0, 0), (2, 3), (2, 1), (3, 3), (3, 1), (1, 1), (1, 2), (2, 2)),
    ((3, 0), (3, 2), (2, 2), (1, 3), (0, 0), (1, 0), (0, 3), (1, 1), (2, 1), (1, 2), (0, 1), (0, 2), (3, 3), (2, 0), (2, 3), (3, 1)),
)
LAST_HEARD = ((0, 1), (0, 0), (0, 3), (0, 2), (3, 0), (1, 2), (1, 1), (3, 3), (2, 1), (2, 0), (2, 3), (2, 2), (1, 0), (3, 2), (3, 1), (1, 3))
MESSAGES = (
    (0, (0, 0), 0, (0, 0, 0), (0, 3, 1)),
    (0, (0, 2), 0, (0, 1, 0), (0, 0, 0)),
    (0, (2, 2), 0, (0, 2, 0), (1, 2, 1)),
    (0, (0, 3), 1, (0, 2, 1), (0, 0, 1)),
    (0, (2, 3), 0, (0, 3, 0), (0, 2, 0)),
    (0, (0, 2), 1, (0, 3, 1), (2, 3, 1)),
    (0, (0, 0), 1, (1, 0, 1), (0, 2, 1)),
    (0, (1, 1), 0, (1, 2, 0), (1, 3, 0)),
    (0, (1, 3), 1, (1, 2, 1), (0, 1, 0)),
    (0, (1, 2), 0, (1, 3, 0), (2, 2, 0)),
    (0, (0, 1), 1, (2, 1, 1), (0, 3, 0)),
    (0, (0, 2), 0, (2, 2, 0), (2, 3, 0)),
    (0, (0, 3), 0, (2, 3, 0), (0, 1, 1)),
    (0, (1, 1), 1, (3, 1, 1), (1, 3, 1)),
    (0, (2, 2), 1, (3, 2, 1), (1, 2, 0)),
    (0, (1, 3), 1, (3, 3, 1), (1, 1, 1)),
    (1, (0, 0), 1, (0, 0, 1), (0, 3, 1)),
    (1, (0, 3), 0, (0, 2, 0), (0, 0, 0)),
    (1, (2, 3), 1, (0, 3, 1), (1, 3, 0)),
    (1, (0, 1), 1, (1, 1, 1), (1, 3, 1)),
    (1, (1, 3), 0, (1, 2, 0), (0, 1, 1)),
    (1, (1, 2), 0, (1, 3, 0), (2, 3, 0)),
    (1, (0, 0), 0, (2, 0, 0), (0, 2, 0)),
    (1, (0, 1), 0, (2, 1, 0), (0, 3, 0)),
    (1, (0, 2), 1, (2, 2, 1), (0, 0, 1)),
    (1, (0, 3), 0, (2, 3, 0), (3, 3, 1)),
    (1, (1, 2), 0, (3, 2, 0), (0, 1, 0)),
    (1, (1, 2), 1, (3, 2, 1), (2, 3, 1)),
    (1, (2, 3), 0, (3, 3, 0), (1, 2, 0)),
    (1, (2, 3), 1, (3, 3, 1), (1, 2, 1)),
    (2, (0, 1), 1, (0, 1, 1), (1, 2, 1)),
    (2, (0, 1), 0, (0, 2, 0), (1, 2, 0)),
    (2, (1, 3), 0, (0, 3, 0), (2, 3, 0)),
    (2, (0, 3), 1, (0, 3, 1), (0, 1, 0)),
    (2, (0, 1), 0, (1, 1, 0), (1, 3, 0)),
    (2, (1, 2), 1, (1, 1, 1), (0, 1, 1)),
    (2, (1, 3), 0, (1, 2, 0), (1, 1, 1)),
    (2, (3, 3), 0, (1, 3, 0), (0, 3, 0)),
    (2, (3, 3), 1, (1, 3, 1), (0, 3, 1)),
    (2, (2, 3), 1, (2, 2, 1), (0, 2, 1)),
    (2, (2, 3), 0, (2, 3, 0), (1, 3, 1)),
    (2, (0, 3), 1, (2, 3, 1), (3, 3, 0)),
    (2, (1, 2), 1, (3, 2, 1), (2, 2, 0)),
    (2, (1, 3), 1, (3, 3, 1), (2, 3, 1)),
)


def number(device):
    return 8 * device[0] + 2 * device[1] + device[2]


def wanted(r, z):
    if r > z:
        return [None] * USES
    return [(min(r, j), max(r, j)) for j in range(4)] + [(min(z, j), max(z, j)) for j in range(4)]


def first_round(devices):
    def ring(r, z, k, up):
        step = 1 if (k == 0) == up else -1
        return (r, z + step, k) if 0 <= z + step < 4 else (r, z, 1 - k)

    return [[(d, ring(*d, up)) for d in devices] for up in (True, False)] + [
        [((r, z, k), (r ^ bit, z, k)) for r, z, k in devices] for bit in (1, 2)
    ]


def closed(pairs, devices):
    sends, receives = {a for a, _ in pairs}, {b for _, b in pairs}
    ends = [d for d in devices if d not in sends]
    starts = [d for d in devices if d not in receives]

    def cost(a, b):
        return 1000 if a == b else (abs(a[1] - b[1]) + bin(a[0] ^ b[0]).count("1")) ** 2

    size = len(ends)
    u, v, row_of = [0] * (size + 1), [0] * (size + 1), [0] * (size + 1)
    for i in range(1, size + 1):
        row_of[0], col = i, 0
        least, before, done = [10**6] * (size + 1), [0] * (size + 1), [False] * (size + 1)
        while row_of[col]:
            done[col], row, delta, following = True, row_of[col], 10**6, 0
            for j in range(1, size + 1):
                if not done[j]:
                    slack = cost(ends[row - 1], starts[j - 1]) - u[row] - v[j]
                    if slack < least[j]:
                        least[j], before[j] = slack, col
                    if least[j] < delta:
                        delta, following = least[j], j
            for j in range(size + 1):
                if done[j]:
                    u[row_of[j]] += delta
                    v[j] -= delta
                else:
                    least[j] -= delta
            col = following
        while col:
            row_of[col] = row_of[before[col]]
            col = before[col]
    return pairs + [(ends[row_of[j] - 1], starts[j - 1]) for j in range(1, size + 1)]


def trace_pairs():
    chips = [(r, z) for r in range(4) for z in range(4)]

    def near(c):
        return {d for d in chips if abs(c[1] - d[1]) + bin(c[0] ^ d[0]).count("1") <= 1}

    known = {c: near(c) | near(HEARD[0][i]) | near(HEARD[1][i]) for i, c in enumerate(chips)}
    for i, c in enumerate(chips):
        assert known[c] | known[LAST_HEARD[i]] >= {d for d in chips if d[0] <= d[1]}

    def on_cores(sources):
        return [(number((*sources[i], k)), number((*c, k))) for i, c in enumerate(chips) for k in range(2)]

    return [on_cores(sources) for sources in HEARD], on_cores(LAST_HEARD)


def schedule():
    devices = [(r, z, k) for r in range(4) for z in range(4) for k in range(2)]
    first = first_round(devices)
    held = {d: [((d[0], d[1]), d[2])] for d in devices}
    for pairs in first:
        for a, b in pairs:
            held[b].append(((a[0], a[1]), a[2]))
    second = [[] for _ in range(SECOND)]
    later = {d: [None] * SECOND for d in devices}
    sends = [{} for _ in range(SECOND)]
    for i, tile, half, a, b in MESSAGES:
        second[i].append((a, b))
        sends[i][number(a)] = held[a].index((tile, half))
        later[b][i] = (tile, half)
    second = [closed(pairs, devices) for pairs in second]
    adds = [set() for _ in range(FIRST)]
    uses = [[{} for _ in range(USES)] for _ in range(2)]
    for d in devices:
        r, z, k = d
        for s, (tile, half) in enumerate(held[d]):
            if half == k and (s == 0 or tile != (r, z)):
                adds[s].add(number(d))
        for u, tile in enumerate(wanted(r, z)):
            for n, shards in enumerate((held, later)):
                here = shards[d] + shards[r, z, 1 - k]
                if tile and (tile, 0) in here and (tile, 1) in here and not any(number(d) in uses[m][u] for m in range(n)):
                    uses[n][u][number(d)] = (here.index((tile, 0)), here.index((tile, 1)))
            assert tile is None or any(number(d) in uses[n][u] for n in range(2))

    def flat(pairs):
        assert len({a for a, _ in pairs}) == len({b for _, b in pairs}) == len(devices)
        return [(number(a), number(b)) for a, b in pairs]

    return [flat(p) for p in first], [flat(p) for p in second], sends, adds, uses


class Place:
    def __init__(self):
        self.row, self.col = lax.axis_index("row"), lax.axis_index("col")
        self.line, self.core = self.col // 2, lax.rem(self.col, 2)
        self.number = self.row * 8 + self.col

    def among(self, devices):
        bits = sum(1 << d for d in devices)
        bits -= (bits >> 31) << 32
        return (lax.shift_right_logical(jnp.int32(bits), self.number) & 1) == 1


def kept(pattern, i, j):
    low, high = jnp.minimum(i, j), jnp.maximum(i, j)
    return (low == high) | (pattern[low, high] != 0)


def partial_kernel(adds, order_size, pattern, *refs):
    me = Place()
    packed, out = refs[FIRST:]
    out[...] = jnp.zeros_like(out)
    at_row = lax.broadcasted_iota(jnp.int32, out.shape, 0)
    at_col = lax.broadcasted_iota(jnp.int32, out.shape, 1)
    both = [(refs[s], s, 0) for s in range(FIRST)] + [(packed.at[s], s, 1) for s in range(FIRST)]
    for ref, s, other in both:
        devices = {d ^ other for d in adds[s]}
        core = me.core ^ other
        before, after = me.line - 1 + 2 * core, me.line + 1 - 2 * core
        row = (me.row, me.row, me.row, me.row ^ 1, me.row ^ 2)[s]
        line = (me.line, before, after, me.line, me.line)[s]
        row_blocks, col_blocks = ref.shape[0] // BLK, ref.shape[1] // BLK

        @pl.when(me.among(devices) & (row <= line))
        def _():
            zero = jnp.zeros((BLK, BLK), jnp.float32)
            total = zero
            for a in range(row_blocks):
                for b in range(col_blocks):
                    i, j = row * row_blocks + a, (2 * line + core) * col_blocks + b
                    block = ref[a * BLK : (a + 1) * BLK, b * BLK : (b + 1) * BLK].astype(jnp.float32)
                    block = jnp.where((i <= j) & kept(pattern, i, j), block, zero)
                    total += jnp.where(i == j, 1.0, 2.0) * (block * block)
            lane = at_col == 8 * row + 2 * line + core
            out[...] += jnp.where((at_row == 1) & lane, jnp.sum(total) / order_size, 0.0)

            @pl.when(row == line)
            def _():
                rows_at = lax.broadcasted_iota(jnp.int32, (BLK, BLK), 0)
                cols_at = lax.broadcasted_iota(jnp.int32, (BLK, BLK), 1)
                diagonals = zero
                for b in range(col_blocks):
                    start = pl.multiple_of((core * col_blocks + b) * BLK, BLK)
                    block = ref[pl.ds(start, BLK), b * BLK : (b + 1) * BLK].astype(jnp.float32)
                    diagonals += jnp.where(rows_at == cols_at, block, zero)
                out[...] += jnp.where((at_row == 0) & lane, jnp.sum(diagonals) / order_size, 0.0)


def copy_kernel(source, out):
    out[...] = source[...]


def pack_kernel(*refs):
    out = refs[-1]
    for i, ref in enumerate(refs[:-1]):
        out[i] = ref[...]


def copy_kernel(source, out):
    out[...] = source[...]


def pack_kernel(*refs):
    out = refs[-1]
    for i, ref in enumerate(refs[:-1]):
        out[i] = ref[...]


def choose_kernel(sends, *refs):
    me = Place()
    held, outs = refs[:FIRST], refs[FIRST:]
    for out, send in zip(outs, sends):
        for s, ref in enumerate(held):
            devices = [d for d in send if send[d] == s]
            if devices:
                @pl.when(me.among(devices))
                def _():
                    out[...] = ref[...]


def pack_kernel(*refs):
    out = refs[-1]
    for i, ref in enumerate(refs[:-1]):
        out[i] = ref[...]


def place_tiles(uses, me, shards, keep, left, right, raw):
    tile, width = left.shape[0], right.shape[1]
    blocks, half_blocks = tile // BLK, width // BLK
    zero = jnp.zeros((BLK, BLK), left.dtype)

    def stored(a, b):
        return raw[(b // 2) * tile + a * BLK : (b // 2) * tile + (a + 1) * BLK, (b % 2) * BLK : (b % 2 + 1) * BLK]

    def direct(a, b):
        start = pl.multiple_of(me.core * tile + a * BLK, BLK)
        return raw[pl.ds(start, BLK), b * BLK : (b + 1) * BLK]

    def mirrored(a, b):
        start = pl.multiple_of((a // 2) * tile + (me.core * half_blocks + b) * BLK, BLK)
        return raw[pl.ds(start, BLK), (a % 2) * BLK : (a % 2 + 1) * BLK].T

    left_ways = (
        stored,
        lambda a, b: stored(b, a).T,
        lambda a, b: stored(a, b) if a <= b else stored(b, a).T,
    )
    right_ways = (
        direct,
        mirrored,
        lambda a, b: jnp.where(a <= me.core * half_blocks + b, direct(a, b), mirrored(a, b)),
    )

    def fill(panel, at, cols, u, block_of):
        j = u % 4
        for a in range(blocks):
            for b in range(cols):
                rows = slice(at[0] + a * BLK, at[0] + (a + 1) * BLK)
                lanes = slice(at[1] + b * BLK, at[1] + (b + 1) * BLK)
                if u < 4:
                    flag = keep(panel, rows, lanes, me.row * blocks + a, j * blocks + b)
                else:
                    flag = keep(panel, rows, lanes, j * blocks + a, me.col * half_blocks + b)
                panel[rows, lanes] = jnp.where(flag, block_of(a, b), zero)

    for u, here in enumerate(uses):
        j = u % 4
        panel, at, cols, ways = (left, (0, j * tile), blocks, left_ways) if u < 4 else (
            right, (j * tile, 0), half_blocks, right_ways)

        def index(d):
            return d // 8 if u < 4 else (d % 8) // 2

        def above(d):
            return 2 if index(d) == j else int((index(d) > j) == (u < 4))

        if here:
            @pl.when(me.among(here))
            def _():
                for half in range(2):
                    for s in sorted({here[d][half] for d in here}):
                        @pl.when(me.among([d for d in here if here[d][half] == s]))
                        def _():
                            raw[half * tile : (half + 1) * tile, :] = shards[s][...]

                for way in sorted({above(d) for d in here}):
                    @pl.when(me.among([d for d in here if above(d) == way]))
                    def _():
                        fill(panel, at, cols, u, ways[way])


def panels_kernel(uses, pattern, *refs):
    packed, left, right, keeps, raw = refs[FIRST:]
    me = Place()
    shards = list(refs[:FIRST]) + [packed.at[i] for i in range(FIRST)]

    def keep(panel, rows, lanes, i, j):
        return kept(pattern, i, j)

    place_tiles(uses[0], me, shards, keep, left, right, raw)
    tile, width = left.shape[0], right.shape[1]
    blocks, half_blocks = tile // BLK, width // BLK

    def flags(ref, row_at, col_at, cols, flag):
        for a in range(blocks):
            for b in range(cols):
                value = jnp.where(flag(a, b), 1.0, 0.0).astype(ref.dtype)
                ref[row_at + a * BLK : row_at + (a + 1) * BLK, col_at + b * BLK : col_at + (b + 1) * BLK] = (
                    jnp.full((BLK, BLK), value, ref.dtype)
                )

    for u, later in enumerate(uses[1]):
        j = u % 4
        if later:
            @pl.when(me.among(later))
            def _():
                if u < 4:
                    flags(left, 0, j * tile, blocks, lambda a, b: kept(pattern, me.row * blocks + a, j * blocks + b))
                else:
                    flags(
                        right, j * tile, 0, half_blocks,
                        lambda a, b: kept(pattern, j * blocks + a, me.col * half_blocks + b),
                    )

    def square_kept(a, b):
        i, j = me.row * blocks + a, me.col * half_blocks + b
        return (i <= j) & kept(pattern, i, j)

    flags(keeps, 0, 0, half_blocks, square_kept)


def grid_product_kernel(uses, *refs):
    shards = refs[: 2 * SECOND]
    keeps, _, _, left, right, out, raw, result, sems = refs[2 * SECOND :]
    me = Place()

    def keep(panel, rows, lanes, i, j):
        return panel[rows, lanes] != 0

    place_tiles(uses[1], me, shards, keep, left, right, raw)
    height = out.shape[0]
    part = height // 2
    copies = []
    for c in range(2):
        rows = pl.ds(c * part, part)

        @pl.when(me.row <= me.line)
        def _():
            product = jnp.dot(left[rows, :], right[...], preferred_element_type=jnp.float32)
            result[rows, :] = jnp.where(
                keeps[rows, :].astype(jnp.float32) != 0, product, jnp.zeros_like(product)
            ).astype(result.dtype)

        @pl.when(me.row > me.line)
        def _():
            result[rows, :] = jnp.zeros((part, result.shape[1]), result.dtype)

        copies.append(pltpu.make_async_copy(result.at[rows], out.at[rows], sems.at[c]))
        copies[-1].start()
    for copy in copies:
        copy.wait()


def chip_grid(density, pattern):
    height, width = density.shape
    n_col = lax.axis_size("col")
    n_devices = lax.axis_size("row") * n_col
    order_size = width * lax.axis_size("col")
    dtype = density.dtype
    axes = ("row", "col")
    first, second, sends, adds, uses = schedule()
    shard = jax.ShapeDtypeStruct(density.shape, dtype)
    raw = pltpu.VMEM((2 * height, width), dtype)
    panels = [
        jax.ShapeDtypeStruct((height, order_size), dtype),
        jax.ShapeDtypeStruct((order_size, width), dtype),
    ]

    def call(kernel, out_shape, smem, args, scratch=(), out_specs=VMEM, aliases=None, cost=None):
        return pl.pallas_call(
            kernel,
            out_shape=out_shape,
            in_specs=[SMEM] * smem + [VMEM] * (len(args) - smem),
            out_specs=out_specs,
            scratch_shapes=list(scratch),
            input_output_aliases=aliases or {},
            compiler_params=GRID_PARAMS,
            cost_estimate=cost,
        )(*args)

    def share(value):
        return lax.ppermute(value, axes, [(d, d ^ 1) for d in range(n_devices)])

    def merge(parts, others):
        return jnp.where(parts != 0, parts, others)

    came = [lax.ppermute(density, axes, pairs) for pairs in first]
    came[0], own = lax.optimization_barrier((came[0], call(copy_kernel, shard, 0, [density])))
    held = [own] + came
    chosen = call(functools.partial(choose_kernel, sends), [shard] * SECOND, 0, held, (), [VMEM] * SECOND)
    tied = lax.optimization_barrier((*chosen, *held))
    chosen, held = tied[:SECOND], list(tied[SECOND:])
    later = [lax.ppermute(value, axes, pairs) for value, pairs in zip(chosen, second)]
    packed = share(call(pack_kernel, jax.ShapeDtypeStruct((FIRST, height, width), dtype), 0, held))
    parts = call(
        functools.partial(partial_kernel, adds, order_size),
        jax.ShapeDtypeStruct((8, 128), jnp.float32),
        1,
        [pattern] + held + [packed],
    )
    packed, parts = lax.optimization_barrier((packed, parts))
    early, late = trace_pairs()
    received = [lax.ppermute(parts, axes, pairs) for pairs in early]
    left, right, keeps = call(
        functools.partial(panels_kernel, uses), panels + [shard], 1, [pattern] + held + [packed], [raw], [VMEM] * 3
    )
    left, parts = lax.optimization_barrier((left, merge(parts, merge(*received))))
    received = lax.ppermute(parts, axes, late)
    shared = []
    for i in range(SECOND):
        later[i], left = lax.optimization_barrier((later[i], left))
        shared.append(share(later[i]))
    inputs = later + shared + [keeps, left, right]
    square = call(
        functools.partial(grid_product_kernel, uses),
        panels + [shard],
        0,
        inputs,
        [raw, pltpu.VMEM(density.shape, dtype), pltpu.SemaphoreType.DMA((2,))],
        [VMEM, VMEM, pl.BlockSpec(memory_space=pltpu.HBM)],
        {len(inputs) - 2: 0, len(inputs) - 1: 1},
    )[2]
    square, received = lax.optimization_barrier((square, received))
    traces = jnp.sum(merge(parts[:2], received[:2]), axis=1)
    return (square, traces)


def per_device(density, pattern):
    if lax.axis_size("row") == 4 and lax.axis_size("col") == 8 and density.shape[0] == 2 * density.shape[1]:
        return chip_grid(density, pattern)
    return any_mesh(density, pattern)


def solution(mesh):
    placed = (P("row", "col"), P())
    return jax.shard_map(
        per_device, mesh=mesh, in_specs=placed, out_specs=(P("row", "col"), P()), check_vma=False
    )
```

```python
import functools
import jax
import jax.numpy as jnp
from jax import lax
from jax.experimental import pallas as pl
from jax.experimental.pallas import tpu as pltpu
from jax.sharding import PartitionSpec as P

BLK = 128
VMEM = pl.BlockSpec(memory_space=pltpu.VMEM)
SMEM = pl.BlockSpec(memory_space=pltpu.SMEM)
PARAMS = pltpu.CompilerParams(vmem_limit_bytes=40 * 2**20)


def symmetric_kernel(sub, place, pattern, density, *rest):
    pieces, full = rest[:sub], rest[sub]
    row, col = place[0], place[1]
    height, width = density.shape
    per_piece = width // BLK
    row_blocks = height // BLK
    own_slot = lax.rem(col, sub)
    on_diagonal = row == col // sub
    for t in range(sub):
        slot = lax.rem(own_slot + sub - t, sub)
        for a in range(per_piece):
            i = slot * per_piece + a
            block_row = row * row_blocks + i
            rows = pl.ds(pl.multiple_of(i * BLK, BLK), BLK)
            for b in range(per_piece):
                block_col = col * per_piece + b
                cols = pl.ds(b * BLK, BLK)
                mirror = pieces[t][b * BLK : (b + 1) * BLK, a * BLK : (a + 1) * BLK]
                if t == 0:
                    start = pl.multiple_of((own_slot * per_piece + b) * BLK, BLK)
                    mine = density[pl.ds(start, BLK), a * BLK : (a + 1) * BLK]
                    mirror = jnp.where(on_diagonal, mine, mirror)
                chosen = pattern[jnp.minimum(block_row, block_col), jnp.maximum(block_row, block_col)] != 0
                upper = (block_row == block_col) | ((block_row < block_col) & chosen)
                lower = (block_row > block_col) & chosen
                zero = jnp.zeros((BLK, BLK), full.dtype)
                value = jnp.where(lower, mirror.T, zero)
                full[rows, cols] = jnp.where(upper, density[rows, cols], value)


def product_kernel(lines, planes, place, pattern, *refs):
    left = refs[: 2 * lines]
    right = refs[2 * lines : 2 * lines + planes]
    out, panel = refs[2 * lines + planes :]
    row, col = place[0], place[1]
    height, width = out.shape
    core, line = lax.rem(col, 2), col // 2
    for d in range(planes):
        start = pl.multiple_of((row ^ d) * height, height)
        panel[pl.ds(start, height), :] = right[d][...]
    total = jnp.zeros((height, width), jnp.float32)
    for e in range(lines):
        for s in range(2):
            start = pl.multiple_of(((line ^ e) * 2 + (core ^ s)) * width, width)
            total += jnp.dot(
                left[2 * e + s][...],
                panel[pl.ds(start, width), :],
                preferred_element_type=jnp.float32,
            )
    for i in range(height // BLK):
        for j in range(width // BLK):
            block_row = row * (height // BLK) + i
            block_col = col * (width // BLK) + j
            kept = (block_row == block_col) | ((block_row < block_col) & (pattern[block_row, block_col] != 0))
            block = total[i * BLK : (i + 1) * BLK, j * BLK : (j + 1) * BLK]
            out[i * BLK : (i + 1) * BLK, j * BLK : (j + 1) * BLK] = jnp.where(
                kept, block, jnp.zeros_like(block)
            ).astype(out.dtype)


def block_weights(pattern, row, col, row_blocks, col_blocks):
    block_rows = row * row_blocks + jnp.arange(row_blocks)
    block_cols = col * col_blocks + jnp.arange(col_blocks)
    chosen = lax.dynamic_slice(pattern, (row * row_blocks, col * col_blocks), (row_blocks, col_blocks))
    diagonal = block_rows[:, None] == block_cols[None, :]
    strict = (block_cols[None, :] > block_rows[:, None]) & (chosen != 0)
    return jnp.where(diagonal, 1.0, jnp.where(strict, 2.0, 0.0)).astype(jnp.float32)


def any_mesh(density, pattern):
    n_row = lax.axis_size("row")
    n_col = lax.axis_size("col")
    sub = n_col // n_row
    row = lax.axis_index("row")
    col = lax.axis_index("col")
    height, width = density.shape
    order_size = width * n_col
    place = jnp.stack([row, col]).astype(jnp.int32)

    pieces = []
    for t in range(sub):
        pairs = []
        for q in range(n_row):
            for c in range(n_col):
                p = (c + t) % sub
                if c > q * sub + p:
                    pairs.append((q * n_col + c, (c // sub) * n_col + q * sub + p))
        start = lax.rem(col + t, sub) * width
        piece = lax.dynamic_slice_in_dim(density, start, width, 0)
        pieces.append(lax.ppermute(piece, ("row", "col"), pairs))
    full = pl.pallas_call(
        functools.partial(symmetric_kernel, sub),
        out_shape=jax.ShapeDtypeStruct(density.shape, density.dtype),
        in_specs=[SMEM, SMEM] + [VMEM] * (sub + 1),
        out_specs=VMEM,
        compiler_params=PARAMS,
    )(place, pattern, density, *pieces)

    weights = block_weights(pattern, row, col, height // BLK, width // BLK)
    values = density.astype(jnp.float32).reshape(height // BLK, BLK, width // BLK, BLK)
    squares = jnp.sum(values * values, axis=(1, 3))
    rows_at = row * height + jnp.arange(height)[:, None]
    cols_at = col * width + jnp.arange(width)[None, :]
    diagonal = jnp.where(rows_at == cols_at, density.astype(jnp.float32), 0.0)
    sums = jnp.stack([jnp.sum(diagonal), jnp.sum(jnp.where(weights > 0, weights * squares, 0.0))])
    step = 1
    while step < n_row:
        sums = sums + lax.ppermute(sums, "row", [(i, i ^ step) for i in range(n_row)])
        step *= 2
    step = 1
    while step < n_col:
        sums = sums + lax.ppermute(sums, "col", [(i, i ^ step) for i in range(n_col)])
        step *= 2
    traces = sums / order_size

    right = [full]
    for d in range(1, n_row):
        right.append(lax.ppermute(full, "row", [(i, i ^ d) for i in range(n_row)]))
    left = []
    for e in range(n_col // 2):
        shard = full
        if e > 0:
            shard = lax.ppermute(full, "col", [(i, i ^ (2 * e)) for i in range(n_col)])
        other = lax.ppermute(shard, "col", [(i, i ^ 1) for i in range(n_col)])
        left += [shard, other]
    square = pl.pallas_call(
        functools.partial(product_kernel, n_col // 2, n_row),
        out_shape=jax.ShapeDtypeStruct(density.shape, density.dtype),
        in_specs=[SMEM, SMEM] + [VMEM] * (len(left) + len(right)),
        out_specs=VMEM,
        scratch_shapes=[pltpu.VMEM((order_size, width), density.dtype)],
        compiler_params=PARAMS,
    )(place, pattern, *left, *right)
    return (square, traces)

GRID_PARAMS = pltpu.CompilerParams(vmem_limit_bytes=14 * 2**20)
USES = 8
FIRST = 5
SECOND = 3
SEEN = ((), (0,), (1, 3), (2,))

MESSAGES = (
    (0, (0, 0), 0, (2, 0, 0), (0, 2, 0)),
    (0, (0, 0), 1, (0, 0, 1), (0, 3, 1)),
    (0, (0, 1), 0, (2, 1, 0), (0, 3, 0)),
    (0, (0, 1), 1, (1, 1, 1), (1, 3, 1)),
    (0, (0, 2), 1, (2, 2, 1), (0, 0, 1)),
    (0, (0, 3), 0, (0, 2, 0), (0, 0, 0)),
    (0, (0, 3), 0, (2, 3, 0), (3, 3, 1)),
    (0, (1, 2), 0, (1, 3, 0), (2, 3, 0)),
    (0, (1, 2), 0, (3, 2, 0), (0, 1, 0)),
    (0, (1, 2), 1, (3, 2, 1), (2, 3, 1)),
    (0, (1, 3), 0, (1, 2, 0), (0, 1, 1)),
    (0, (2, 3), 0, (3, 3, 0), (1, 2, 0)),
    (0, (2, 3), 1, (0, 3, 1), (1, 3, 0)),
    (0, (2, 3), 1, (3, 3, 1), (1, 2, 1)),
    (1, (0, 0), 0, (0, 0, 0), (0, 3, 1)),
    (1, (0, 0), 1, (1, 0, 1), (0, 2, 1)),
    (1, (0, 1), 1, (2, 1, 1), (0, 3, 0)),
    (1, (0, 2), 0, (0, 1, 0), (0, 0, 0)),
    (1, (0, 2), 0, (2, 2, 0), (2, 3, 0)),
    (1, (0, 2), 1, (0, 3, 1), (2, 3, 1)),
    (1, (0, 3), 0, (2, 3, 0), (0, 1, 1)),
    (1, (0, 3), 1, (0, 2, 1), (0, 0, 1)),
    (1, (1, 1), 0, (1, 2, 0), (1, 3, 0)),
    (1, (1, 1), 1, (3, 1, 1), (1, 3, 1)),
    (1, (1, 2), 0, (1, 3, 0), (2, 2, 0)),
    (1, (1, 3), 1, (1, 2, 1), (0, 1, 0)),
    (1, (1, 3), 1, (3, 3, 1), (1, 1, 1)),
    (1, (2, 2), 0, (0, 2, 0), (1, 2, 1)),
    (1, (2, 2), 1, (3, 2, 1), (1, 2, 0)),
    (1, (2, 3), 0, (0, 3, 0), (0, 2, 0)),
    (2, (0, 1), 0, (0, 2, 0), (1, 2, 0)),
    (2, (0, 1), 0, (1, 1, 0), (1, 3, 0)),
    (2, (0, 1), 1, (0, 1, 1), (1, 2, 1)),
    (2, (0, 3), 1, (0, 3, 1), (0, 1, 0)),
    (2, (0, 3), 1, (2, 3, 1), (3, 3, 0)),
    (2, (1, 2), 1, (1, 1, 1), (0, 1, 1)),
    (2, (1, 2), 1, (3, 2, 1), (2, 2, 0)),
    (2, (1, 3), 0, (0, 3, 0), (2, 3, 0)),
    (2, (1, 3), 0, (1, 2, 0), (1, 1, 1)),
    (2, (1, 3), 1, (3, 3, 1), (2, 3, 1)),
    (2, (2, 3), 0, (2, 3, 0), (1, 3, 1)),
    (2, (2, 3), 1, (2, 2, 1), (0, 2, 1)),
    (2, (3, 3), 0, (1, 3, 0), (0, 3, 0)),
    (2, (3, 3), 1, (1, 3, 1), (0, 3, 1)),
)


def number(device):
    return 8 * device[0] + 2 * device[1] + device[2]


def wanted(r, z):
    if r > z:
        return [None] * USES
    return [(min(r, j), max(r, j)) for j in range(4)] + [(min(z, j), max(z, j)) for j in range(4)]


def first_round(devices):
    def ring(r, z, k, up):
        step = 1 if (k == 0) == up else -1
        return (r, z + step, k) if 0 <= z + step < 4 else (r, z, 1 - k)

    return [[(d, ring(*d, up)) for d in devices] for up in (True, False)] + [
        [((r, z, k), (r ^ bit, z, k)) for r, z, k in devices] for bit in (1, 2)
    ]


def closed(pairs, devices):
    sends, receives = {a for a, _ in pairs}, {b for _, b in pairs}
    ends = [d for d in devices if d not in sends]
    starts = [d for d in devices if d not in receives]

    def cost(a, b):
        return 1000 if a == b else (abs(a[1] - b[1]) + bin(a[0] ^ b[0]).count("1")) ** 2

    size = len(ends)
    u, v, row_of = [0] * (size + 1), [0] * (size + 1), [0] * (size + 1)
    for i in range(1, size + 1):
        row_of[0], col = i, 0
        least, before, done = [10**6] * (size + 1), [0] * (size + 1), [False] * (size + 1)
        while row_of[col]:
            done[col], row, delta, following = True, row_of[col], 10**6, 0
            for j in range(1, size + 1):
                if not done[j]:
                    slack = cost(ends[row - 1], starts[j - 1]) - u[row] - v[j]
                    if slack < least[j]:
                        least[j], before[j] = slack, col
                    if least[j] < delta:
                        delta, following = least[j], j
            for j in range(size + 1):
                if done[j]:
                    u[row_of[j]] += delta
                    v[j] -= delta
                else:
                    least[j] -= delta
            col = following
        while col:
            row_of[col] = row_of[before[col]]
            col = before[col]
    return pairs + [(ends[row_of[j] - 1], starts[j - 1]) for j in range(1, size + 1)]


def schedule():
    devices = [(r, z, k) for r in range(4) for z in range(4) for k in range(2)]
    first = first_round(devices)
    held = {d: [((d[0], d[1]), d[2])] for d in devices}
    for pairs in first:
        for a, b in pairs:
            held[b].append(((a[0], a[1]), a[2]))
    second = [[] for _ in range(SECOND)]
    later = {d: [None] * SECOND for d in devices}
    sends = [{} for _ in range(SECOND)]
    for i, tile, half, a, b in MESSAGES:
        second[i].append((a, b))
        sends[i][number(a)] = held[a].index((tile, half))
        later[b][i] = (tile, half)
    second = [closed(pairs, devices) for pairs in second]
    adds = [set() for _ in range(FIRST)]
    uses = [[{} for _ in range(USES)] for _ in range(2)]
    for d in devices:
        r, z, k = d
        added = {(r, z), (r ^ 1, z), (r ^ 2, z)} | {(r, j) for j in SEEN[z]}
        for s, (tile, half) in enumerate(held[d]):
            if tile in added and half == k and (s == 0 or tile != (r, z)):
                adds[s].add(number(d))
        for u, tile in enumerate(wanted(r, z)):
            for n, shards in enumerate((held, later)):
                here = shards[d] + shards[r, z, 1 - k]
                if tile and (tile, 0) in here and (tile, 1) in here and not any(number(d) in uses[m][u] for m in range(n)):
                    uses[n][u][number(d)] = (here.index((tile, 0)), here.index((tile, 1)))
            assert tile is None or any(number(d) in uses[n][u] for n in range(2))

    def flat(pairs):
        assert len({a for a, _ in pairs}) == len({b for _, b in pairs}) == len(devices)
        return [(number(a), number(b)) for a, b in pairs]

    return [flat(p) for p in first], [flat(p) for p in second], sends, adds, uses


class Place:
    def __init__(self):
        self.row, self.col = lax.axis_index("row"), lax.axis_index("col")
        self.line, self.core = self.col // 2, lax.rem(self.col, 2)
        self.number = self.row * 8 + self.col

    def among(self, devices):
        bits = sum(1 << d for d in devices)
        bits -= (bits >> 31) << 32
        return (lax.shift_right_logical(jnp.int32(bits), self.number) & 1) == 1


def kept(pattern, i, j):
    low, high = jnp.minimum(i, j), jnp.maximum(i, j)
    return (low == high) | (pattern[low, high] != 0)


def partial_kernel(adds, order_size, pattern, *refs):
    me = Place()
    packed, out = refs[FIRST:]
    out[...] = jnp.zeros_like(out)
    at_row = lax.broadcasted_iota(jnp.int32, out.shape, 0)
    at_col = lax.broadcasted_iota(jnp.int32, out.shape, 1)
    both = [(refs[s], s, 0) for s in range(FIRST)] + [(packed.at[s], s, 1) for s in range(FIRST)]
    for ref, s, other in both:
        devices = {d ^ other for d in adds[s]}
        core = me.core ^ other
        before, after = me.line - 1 + 2 * core, me.line + 1 - 2 * core
        row = (me.row, me.row, me.row, me.row ^ 1, me.row ^ 2)[s]
        line = (me.line, before, after, me.line, me.line)[s]
        row_blocks, col_blocks = ref.shape[0] // BLK, ref.shape[1] // BLK

        @pl.when(me.among(devices) & (row <= line))
        def _():
            zero = jnp.zeros((BLK, BLK), jnp.float32)
            total = zero
            for a in range(row_blocks):
                for b in range(col_blocks):
                    i, j = row * row_blocks + a, (2 * line + core) * col_blocks + b
                    block = ref[a * BLK : (a + 1) * BLK, b * BLK : (b + 1) * BLK].astype(jnp.float32)
                    block = jnp.where((i <= j) & kept(pattern, i, j), block, zero)
                    total += jnp.where(i == j, 1.0, 2.0) * (block * block)
            lane = at_col == 8 * row + 2 * line + core
            out[...] += jnp.where((at_row == 1) & lane, jnp.sum(total) / order_size, 0.0)

            @pl.when(row == line)
            def _():
                rows_at = lax.broadcasted_iota(jnp.int32, (BLK, BLK), 0)
                cols_at = lax.broadcasted_iota(jnp.int32, (BLK, BLK), 1)
                diagonals = zero
                for b in range(col_blocks):
                    start = pl.multiple_of((core * col_blocks + b) * BLK, BLK)
                    block = ref[pl.ds(start, BLK), b * BLK : (b + 1) * BLK].astype(jnp.float32)
                    diagonals += jnp.where(rows_at == cols_at, block, zero)
                out[...] += jnp.where((at_row == 0) & lane, jnp.sum(diagonals) / order_size, 0.0)


def copy_kernel(source, out):
    out[...] = source[...]


def pack_kernel(*refs):
    out = refs[-1]
    for i, ref in enumerate(refs[:-1]):
        out[i] = ref[...]


def copy_kernel(source, out):
    out[...] = source[...]


def pack_kernel(*refs):
    out = refs[-1]
    for i, ref in enumerate(refs[:-1]):
        out[i] = ref[...]


def choose_kernel(sends, *refs):
    me = Place()
    held, outs = refs[:FIRST], refs[FIRST:]
    for out, send in zip(outs, sends):
        for s, ref in enumerate(held):
            devices = [d for d in send if send[d] == s]
            if devices:
                @pl.when(me.among(devices))
                def _():
                    out[...] = ref[...]


def pack_kernel(*refs):
    out = refs[-1]
    for i, ref in enumerate(refs[:-1]):
        out[i] = ref[...]


def place_tiles(uses, me, shards, keep, left, right, raw):
    tile, width = left.shape[0], right.shape[1]
    blocks, half_blocks = tile // BLK, width // BLK
    zero = jnp.zeros((BLK, BLK), left.dtype)

    def stored(a, b):
        return raw[(b // 2) * tile + a * BLK : (b // 2) * tile + (a + 1) * BLK, (b % 2) * BLK : (b % 2 + 1) * BLK]

    def direct(a, b):
        start = pl.multiple_of(me.core * tile + a * BLK, BLK)
        return raw[pl.ds(start, BLK), b * BLK : (b + 1) * BLK]

    def mirrored(a, b):
        start = pl.multiple_of((a // 2) * tile + (me.core * half_blocks + b) * BLK, BLK)
        return raw[pl.ds(start, BLK), (a % 2) * BLK : (a % 2 + 1) * BLK].T

    left_ways = (
        stored,
        lambda a, b: stored(b, a).T,
        lambda a, b: stored(a, b) if a <= b else stored(b, a).T,
    )
    right_ways = (
        direct,
        mirrored,
        lambda a, b: jnp.where(a <= me.core * half_blocks + b, direct(a, b), mirrored(a, b)),
    )

    def fill(panel, at, cols, u, block_of):
        j = u % 4
        for a in range(blocks):
            for b in range(cols):
                rows = slice(at[0] + a * BLK, at[0] + (a + 1) * BLK)
                lanes = slice(at[1] + b * BLK, at[1] + (b + 1) * BLK)
                if u < 4:
                    flag = keep(panel, rows, lanes, me.row * blocks + a, j * blocks + b)
                else:
                    flag = keep(panel, rows, lanes, j * blocks + a, me.col * half_blocks + b)
                panel[rows, lanes] = jnp.where(flag, block_of(a, b), zero)

    for u, here in enumerate(uses):
        j = u % 4
        panel, at, cols, ways = (left, (0, j * tile), blocks, left_ways) if u < 4 else (
            right, (j * tile, 0), half_blocks, right_ways)

        def index(d):
            return d // 8 if u < 4 else (d % 8) // 2

        def above(d):
            return 2 if index(d) == j else int((index(d) > j) == (u < 4))

        if here:
            @pl.when(me.among(here))
            def _():
                for half in range(2):
                    for s in sorted({here[d][half] for d in here}):
                        @pl.when(me.among([d for d in here if here[d][half] == s]))
                        def _():
                            raw[half * tile : (half + 1) * tile, :] = shards[s][...]

                for way in sorted({above(d) for d in here}):
                    @pl.when(me.among([d for d in here if above(d) == way]))
                    def _():
                        fill(panel, at, cols, u, ways[way])


def panels_kernel(uses, pattern, *refs):
    packed, left, right, keeps, raw = refs[FIRST:]
    me = Place()
    shards = list(refs[:FIRST]) + [packed.at[i] for i in range(FIRST)]

    def keep(panel, rows, lanes, i, j):
        return kept(pattern, i, j)

    place_tiles(uses[0], me, shards, keep, left, right, raw)
    tile, width = left.shape[0], right.shape[1]
    blocks, half_blocks = tile // BLK, width // BLK

    def flags(ref, row_at, col_at, cols, flag):
        for a in range(blocks):
            for b in range(cols):
                value = jnp.where(flag(a, b), 1.0, 0.0).astype(ref.dtype)
                ref[row_at + a * BLK : row_at + (a + 1) * BLK, col_at + b * BLK : col_at + (b + 1) * BLK] = (
                    jnp.full((BLK, BLK), value, ref.dtype)
                )

    for u, later in enumerate(uses[1]):
        j = u % 4
        if later:
            @pl.when(me.among(later))
            def _():
                if u < 4:
                    flags(left, 0, j * tile, blocks, lambda a, b: kept(pattern, me.row * blocks + a, j * blocks + b))
                else:
                    flags(
                        right, j * tile, 0, half_blocks,
                        lambda a, b: kept(pattern, j * blocks + a, me.col * half_blocks + b),
                    )

    def square_kept(a, b):
        i, j = me.row * blocks + a, me.col * half_blocks + b
        return (i <= j) & kept(pattern, i, j)

    flags(keeps, 0, 0, half_blocks, square_kept)


def grid_product_kernel(uses, *refs):
    shards = refs[: 2 * SECOND]
    keeps, _, _, left, right, out, raw, result, sems = refs[2 * SECOND :]
    me = Place()

    def keep(panel, rows, lanes, i, j):
        return panel[rows, lanes] != 0

    place_tiles(uses[1], me, shards, keep, left, right, raw)
    height = out.shape[0]
    part = height // 2
    copies = []
    for c in range(2):
        rows = pl.ds(c * part, part)

        @pl.when(me.row <= me.line)
        def _():
            product = jnp.dot(left[rows, :], right[...], preferred_element_type=jnp.float32)
            result[rows, :] = jnp.where(
                keeps[rows, :].astype(jnp.float32) != 0, product, jnp.zeros_like(product)
            ).astype(result.dtype)

        @pl.when(me.row > me.line)
        def _():
            result[rows, :] = jnp.zeros((part, result.shape[1]), result.dtype)

        copies.append(pltpu.make_async_copy(result.at[rows], out.at[rows], sems.at[c]))
        copies[-1].start()
    for copy in copies:
        copy.wait()


def chip_grid(density, pattern):
    height, width = density.shape
    n_col = lax.axis_size("col")
    n_devices = lax.axis_size("row") * n_col
    order_size = width * lax.axis_size("col")
    dtype = density.dtype
    axes = ("row", "col")
    first, second, sends, adds, uses = schedule()
    shard = jax.ShapeDtypeStruct(density.shape, dtype)
    raw = pltpu.VMEM((2 * height, width), dtype)
    panels = [
        jax.ShapeDtypeStruct((height, order_size), dtype),
        jax.ShapeDtypeStruct((order_size, width), dtype),
    ]

    def call(kernel, out_shape, smem, args, scratch=(), out_specs=VMEM, aliases=None, cost=None):
        return pl.pallas_call(
            kernel,
            out_shape=out_shape,
            in_specs=[SMEM] * smem + [VMEM] * (len(args) - smem),
            out_specs=out_specs,
            scratch_shapes=list(scratch),
            input_output_aliases=aliases or {},
            compiler_params=GRID_PARAMS,
            cost_estimate=cost,
        )(*args)

    def share(value):
        return lax.ppermute(value, axes, [(d, d ^ 1) for d in range(n_devices)])

    def part_from(parts, row_bits, col_bits):
        return lax.ppermute(parts, axes, [(d, d ^ (row_bits * n_col + col_bits)) for d in range(n_devices)])

    came = [lax.ppermute(density, axes, pairs) for pairs in first]
    came[0], own = lax.optimization_barrier((came[0], call(copy_kernel, shard, 0, [density])))
    held = [own] + came
    chosen = call(functools.partial(choose_kernel, sends), [shard] * SECOND, 0, held, (), [VMEM] * SECOND)
    tied = lax.optimization_barrier((*chosen, *held))
    chosen, held = tied[:SECOND], list(tied[SECOND:])
    later = [lax.ppermute(value, axes, pairs) for value, pairs in zip(chosen, second)]
    packed = share(call(pack_kernel, jax.ShapeDtypeStruct((FIRST, height, width), dtype), 0, held))
    parts = call(
        functools.partial(partial_kernel, adds, order_size),
        jax.ShapeDtypeStruct((8, 128), jnp.float32),
        1,
        [pattern] + held + [packed],
    )
    packed, parts = lax.optimization_barrier((packed, parts))
    received = part_from(parts, 3, 2)
    left, right, keeps = call(
        functools.partial(panels_kernel, uses), panels + [shard], 1, [pattern] + held + [packed], [raw], [VMEM] * 3
    )
    left, parts = lax.optimization_barrier((left, parts + received))
    received = part_from(parts, 0, 4)
    left, parts = lax.optimization_barrier((left, parts))
    shared = []
    for i in range(SECOND):
        later[i], left = lax.optimization_barrier((later[i], left))
        shared.append(share(later[i]))
    inputs = later + shared + [keeps, left, right]
    square = call(
        functools.partial(grid_product_kernel, uses),
        panels + [shard],
        0,
        inputs,
        [raw, pltpu.VMEM(density.shape, dtype), pltpu.SemaphoreType.DMA((2,))],
        [VMEM, VMEM, pl.BlockSpec(memory_space=pltpu.HBM)],
        {len(inputs) - 2: 0, len(inputs) - 1: 1},
    )[2]
    square, received = lax.optimization_barrier((square, received))
    traces = jnp.sum(parts[:2] + received[:2], axis=1)
    return (square, traces)


def per_device(density, pattern):
    if lax.axis_size("row") == 4 and lax.axis_size("col") == 8 and density.shape[0] == 2 * density.shape[1]:
        return chip_grid(density, pattern)
    return any_mesh(density, pattern)


def solution(mesh):
    placed = (P("row", "col"), P())
    return jax.shard_map(
        per_device, mesh=mesh, in_specs=placed, out_specs=(P("row", "col"), P()), check_vma=False
    )
```

```python
import functools
import jax
import jax.numpy as jnp
from jax import lax
from jax.experimental import pallas as pl
from jax.experimental.pallas import tpu as pltpu
from jax.sharding import PartitionSpec as P

BLK = 128
VMEM = pl.BlockSpec(memory_space=pltpu.VMEM)
SMEM = pl.BlockSpec(memory_space=pltpu.SMEM)
PARAMS = pltpu.CompilerParams(vmem_limit_bytes=40 * 2**20)


def symmetric_kernel(sub, place, pattern, density, *rest):
    pieces, full = rest[:sub], rest[sub]
    row, col = place[0], place[1]
    height, width = density.shape
    per_piece = width // BLK
    row_blocks = height // BLK
    own_slot = lax.rem(col, sub)
    on_diagonal = row == col // sub
    for t in range(sub):
        slot = lax.rem(own_slot + sub - t, sub)
        for a in range(per_piece):
            i = slot * per_piece + a
            block_row = row * row_blocks + i
            rows = pl.ds(pl.multiple_of(i * BLK, BLK), BLK)
            for b in range(per_piece):
                block_col = col * per_piece + b
                cols = pl.ds(b * BLK, BLK)
                mirror = pieces[t][b * BLK : (b + 1) * BLK, a * BLK : (a + 1) * BLK]
                if t == 0:
                    start = pl.multiple_of((own_slot * per_piece + b) * BLK, BLK)
                    mine = density[pl.ds(start, BLK), a * BLK : (a + 1) * BLK]
                    mirror = jnp.where(on_diagonal, mine, mirror)
                chosen = pattern[jnp.minimum(block_row, block_col), jnp.maximum(block_row, block_col)] != 0
                upper = (block_row == block_col) | ((block_row < block_col) & chosen)
                lower = (block_row > block_col) & chosen
                zero = jnp.zeros((BLK, BLK), full.dtype)
                value = jnp.where(lower, mirror.T, zero)
                full[rows, cols] = jnp.where(upper, density[rows, cols], value)


def product_kernel(lines, planes, place, pattern, *refs):
    left = refs[: 2 * lines]
    right = refs[2 * lines : 2 * lines + planes]
    out, panel = refs[2 * lines + planes :]
    row, col = place[0], place[1]
    height, width = out.shape
    core, line = lax.rem(col, 2), col // 2
    for d in range(planes):
        start = pl.multiple_of((row ^ d) * height, height)
        panel[pl.ds(start, height), :] = right[d][...]
    total = jnp.zeros((height, width), jnp.float32)
    for e in range(lines):
        for s in range(2):
            start = pl.multiple_of(((line ^ e) * 2 + (core ^ s)) * width, width)
            total += jnp.dot(
                left[2 * e + s][...],
                panel[pl.ds(start, width), :],
                preferred_element_type=jnp.float32,
            )
    for i in range(height // BLK):
        for j in range(width // BLK):
            block_row = row * (height // BLK) + i
            block_col = col * (width // BLK) + j
            kept = (block_row == block_col) | ((block_row < block_col) & (pattern[block_row, block_col] != 0))
            block = total[i * BLK : (i + 1) * BLK, j * BLK : (j + 1) * BLK]
            out[i * BLK : (i + 1) * BLK, j * BLK : (j + 1) * BLK] = jnp.where(
                kept, block, jnp.zeros_like(block)
            ).astype(out.dtype)


def block_weights(pattern, row, col, row_blocks, col_blocks):
    block_rows = row * row_blocks + jnp.arange(row_blocks)
    block_cols = col * col_blocks + jnp.arange(col_blocks)
    chosen = lax.dynamic_slice(pattern, (row * row_blocks, col * col_blocks), (row_blocks, col_blocks))
    diagonal = block_rows[:, None] == block_cols[None, :]
    strict = (block_cols[None, :] > block_rows[:, None]) & (chosen != 0)
    return jnp.where(diagonal, 1.0, jnp.where(strict, 2.0, 0.0)).astype(jnp.float32)


def any_mesh(density, pattern):
    n_row = lax.axis_size("row")
    n_col = lax.axis_size("col")
    sub = n_col // n_row
    row = lax.axis_index("row")
    col = lax.axis_index("col")
    height, width = density.shape
    order_size = width * n_col
    place = jnp.stack([row, col]).astype(jnp.int32)

    pieces = []
    for t in range(sub):
        pairs = []
        for q in range(n_row):
            for c in range(n_col):
                p = (c + t) % sub
                if c > q * sub + p:
                    pairs.append((q * n_col + c, (c // sub) * n_col + q * sub + p))
        start = lax.rem(col + t, sub) * width
        piece = lax.dynamic_slice_in_dim(density, start, width, 0)
        pieces.append(lax.ppermute(piece, ("row", "col"), pairs))
    full = pl.pallas_call(
        functools.partial(symmetric_kernel, sub),
        out_shape=jax.ShapeDtypeStruct(density.shape, density.dtype),
        in_specs=[SMEM, SMEM] + [VMEM] * (sub + 1),
        out_specs=VMEM,
        compiler_params=PARAMS,
    )(place, pattern, density, *pieces)

    weights = block_weights(pattern, row, col, height // BLK, width // BLK)
    values = density.astype(jnp.float32).reshape(height // BLK, BLK, width // BLK, BLK)
    squares = jnp.sum(values * values, axis=(1, 3))
    rows_at = row * height + jnp.arange(height)[:, None]
    cols_at = col * width + jnp.arange(width)[None, :]
    diagonal = jnp.where(rows_at == cols_at, density.astype(jnp.float32), 0.0)
    sums = jnp.stack([jnp.sum(diagonal), jnp.sum(jnp.where(weights > 0, weights * squares, 0.0))])
    step = 1
    while step < n_row:
        sums = sums + lax.ppermute(sums, "row", [(i, i ^ step) for i in range(n_row)])
        step *= 2
    step = 1
    while step < n_col:
        sums = sums + lax.ppermute(sums, "col", [(i, i ^ step) for i in range(n_col)])
        step *= 2
    traces = sums / order_size

    right = [full]
    for d in range(1, n_row):
        right.append(lax.ppermute(full, "row", [(i, i ^ d) for i in range(n_row)]))
    left = []
    for e in range(n_col // 2):
        shard = full
        if e > 0:
            shard = lax.ppermute(full, "col", [(i, i ^ (2 * e)) for i in range(n_col)])
        other = lax.ppermute(shard, "col", [(i, i ^ 1) for i in range(n_col)])
        left += [shard, other]
    square = pl.pallas_call(
        functools.partial(product_kernel, n_col // 2, n_row),
        out_shape=jax.ShapeDtypeStruct(density.shape, density.dtype),
        in_specs=[SMEM, SMEM] + [VMEM] * (len(left) + len(right)),
        out_specs=VMEM,
        scratch_shapes=[pltpu.VMEM((order_size, width), density.dtype)],
        compiler_params=PARAMS,
    )(place, pattern, *left, *right)
    return (square, traces)

GRID_PARAMS = pltpu.CompilerParams(vmem_limit_bytes=14 * 2**20)
USES = 8
FIRST = 5
SECOND = 3
SEEN = ((), (0,), (1, 3), (2,))

MESSAGES = (
    (0, (0, 0), 1, (0, 0, 1), (0, 3, 1)),
    (0, (0, 2), 0, (0, 1, 0), (0, 0, 0)),
    (0, (2, 2), 0, (0, 2, 0), (1, 2, 1)),
    (0, (0, 3), 1, (0, 2, 1), (0, 0, 1)),
    (0, (2, 3), 0, (0, 3, 0), (0, 2, 0)),
    (0, (0, 2), 1, (0, 3, 1), (2, 3, 1)),
    (0, (0, 0), 1, (1, 0, 1), (0, 2, 1)),
    (0, (1, 1), 0, (1, 2, 0), (1, 3, 0)),
    (0, (1, 3), 1, (1, 2, 1), (0, 1, 0)),
    (0, (1, 2), 0, (1, 3, 0), (2, 2, 0)),
    (0, (0, 1), 1, (2, 1, 1), (0, 3, 0)),
    (0, (0, 2), 0, (2, 2, 0), (2, 3, 0)),
    (0, (0, 3), 0, (2, 3, 0), (0, 1, 1)),
    (0, (1, 1), 1, (3, 1, 1), (1, 3, 1)),
    (0, (2, 2), 1, (3, 2, 1), (1, 2, 0)),
    (0, (1, 3), 1, (3, 3, 1), (1, 1, 1)),
    (1, (0, 0), 0, (0, 1, 0), (0, 3, 1)),
    (1, (0, 3), 0, (0, 2, 0), (0, 0, 0)),
    (1, (2, 3), 1, (0, 3, 1), (1, 3, 0)),
    (1, (0, 1), 1, (1, 1, 1), (1, 3, 1)),
    (1, (1, 3), 0, (1, 2, 0), (0, 1, 1)),
    (1, (1, 2), 0, (1, 3, 0), (2, 3, 0)),
    (1, (0, 0), 0, (2, 0, 0), (0, 2, 0)),
    (1, (0, 1), 0, (2, 1, 0), (0, 3, 0)),
    (1, (0, 2), 1, (2, 2, 1), (0, 0, 1)),
    (1, (0, 3), 0, (2, 3, 0), (3, 3, 1)),
    (1, (1, 2), 0, (3, 2, 0), (0, 1, 0)),
    (1, (1, 2), 1, (3, 2, 1), (2, 3, 1)),
    (1, (2, 3), 0, (3, 3, 0), (1, 2, 0)),
    (1, (2, 3), 1, (3, 3, 1), (1, 2, 1)),
    (2, (0, 1), 1, (0, 1, 1), (1, 2, 1)),
    (2, (0, 1), 0, (0, 2, 0), (1, 2, 0)),
    (2, (1, 3), 0, (0, 3, 0), (2, 3, 0)),
    (2, (0, 3), 1, (0, 3, 1), (0, 1, 0)),
    (2, (0, 1), 0, (1, 1, 0), (1, 3, 0)),
    (2, (1, 2), 1, (1, 1, 1), (0, 1, 1)),
    (2, (1, 3), 0, (1, 2, 0), (1, 1, 1)),
    (2, (3, 3), 0, (1, 3, 0), (0, 3, 0)),
    (2, (3, 3), 1, (1, 3, 1), (0, 3, 1)),
    (2, (2, 3), 1, (2, 2, 1), (0, 2, 1)),
    (2, (2, 3), 0, (2, 3, 0), (1, 3, 1)),
    (2, (0, 3), 1, (2, 3, 1), (3, 3, 0)),
    (2, (1, 2), 1, (3, 2, 1), (2, 2, 0)),
    (2, (1, 3), 1, (3, 3, 1), (2, 3, 1)),
)


def number(device):
    return 8 * device[0] + 2 * device[1] + device[2]


def wanted(r, z):
    if r > z:
        return [None] * USES
    return [(min(r, j), max(r, j)) for j in range(4)] + [(min(z, j), max(z, j)) for j in range(4)]


def first_round(devices):
    def ring(r, z, k, up):
        step = 1 if (k == 0) == up else -1
        return (r, z + step, k) if 0 <= z + step < 4 else (r, z, 1 - k)

    return [[(d, ring(*d, up)) for d in devices] for up in (True, False)] + [
        [((r, z, k), (r ^ bit, z, k)) for r, z, k in devices] for bit in (1, 2)
    ]


def closed(pairs, devices):
    sends, receives = {a for a, _ in pairs}, {b for _, b in pairs}
    ends = [d for d in devices if d not in sends]
    starts = [d for d in devices if d not in receives]

    def cost(a, b):
        return 1000 if a == b else (abs(a[1] - b[1]) + bin(a[0] ^ b[0]).count("1")) ** 2

    size = len(ends)
    u, v, row_of = [0] * (size + 1), [0] * (size + 1), [0] * (size + 1)
    for i in range(1, size + 1):
        row_of[0], col = i, 0
        least, before, done = [10**6] * (size + 1), [0] * (size + 1), [False] * (size + 1)
        while row_of[col]:
            done[col], row, delta, following = True, row_of[col], 10**6, 0
            for j in range(1, size + 1):
                if not done[j]:
                    slack = cost(ends[row - 1], starts[j - 1]) - u[row] - v[j]
                    if slack < least[j]:
                        least[j], before[j] = slack, col
                    if least[j] < delta:
                        delta, following = least[j], j
            for j in range(size + 1):
                if done[j]:
                    u[row_of[j]] += delta
                    v[j] -= delta
                else:
                    least[j] -= delta
            col = following
        while col:
            row_of[col] = row_of[before[col]]
            col = before[col]
    return pairs + [(ends[row_of[j] - 1], starts[j - 1]) for j in range(1, size + 1)]


def schedule():
    devices = [(r, z, k) for r in range(4) for z in range(4) for k in range(2)]
    first = first_round(devices)
    held = {d: [((d[0], d[1]), d[2])] for d in devices}
    for pairs in first:
        for a, b in pairs:
            held[b].append(((a[0], a[1]), a[2]))
    second = [[] for _ in range(SECOND)]
    later = {d: [None] * SECOND for d in devices}
    sends = [{} for _ in range(SECOND)]
    for i, tile, half, a, b in MESSAGES:
        second[i].append((a, b))
        sends[i][number(a)] = held[a].index((tile, half))
        later[b][i] = (tile, half)
    second = [closed(pairs, devices) for pairs in second]
    adds = [set() for _ in range(FIRST)]
    uses = [[{} for _ in range(USES)] for _ in range(2)]
    for d in devices:
        r, z, k = d
        added = {(r, z), (r ^ 1, z), (r ^ 2, z)} | {(r, j) for j in SEEN[z]}
        for s, (tile, half) in enumerate(held[d]):
            if tile in added and half == k and (s == 0 or tile != (r, z)):
                adds[s].add(number(d))
        for u, tile in enumerate(wanted(r, z)):
            for n, shards in enumerate((held, later)):
                here = shards[d] + shards[r, z, 1 - k]
                if tile and (tile, 0) in here and (tile, 1) in here and not any(number(d) in uses[m][u] for m in range(n)):
                    uses[n][u][number(d)] = (here.index((tile, 0)), here.index((tile, 1)))
            assert tile is None or any(number(d) in uses[n][u] for n in range(2))

    def flat(pairs):
        assert len({a for a, _ in pairs}) == len({b for _, b in pairs}) == len(devices)
        return [(number(a), number(b)) for a, b in pairs]

    return [flat(p) for p in first], [flat(p) for p in second], sends, adds, uses


class Place:
    def __init__(self):
        self.row, self.col = lax.axis_index("row"), lax.axis_index("col")
        self.line, self.core = self.col // 2, lax.rem(self.col, 2)
        self.number = self.row * 8 + self.col

    def among(self, devices):
        bits = sum(1 << d for d in devices)
        bits -= (bits >> 31) << 32
        return (lax.shift_right_logical(jnp.int32(bits), self.number) & 1) == 1


def kept(pattern, i, j):
    low, high = jnp.minimum(i, j), jnp.maximum(i, j)
    return (low == high) | (pattern[low, high] != 0)


def partial_kernel(adds, order_size, pattern, *refs):
    me = Place()
    packed, out = refs[FIRST:]
    out[...] = jnp.zeros_like(out)
    at_row = lax.broadcasted_iota(jnp.int32, out.shape, 0)
    at_col = lax.broadcasted_iota(jnp.int32, out.shape, 1)
    both = [(refs[s], s, 0) for s in range(FIRST)] + [(packed.at[s], s, 1) for s in range(FIRST)]
    for ref, s, other in both:
        devices = {d ^ other for d in adds[s]}
        core = me.core ^ other
        before, after = me.line - 1 + 2 * core, me.line + 1 - 2 * core
        row = (me.row, me.row, me.row, me.row ^ 1, me.row ^ 2)[s]
        line = (me.line, before, after, me.line, me.line)[s]
        row_blocks, col_blocks = ref.shape[0] // BLK, ref.shape[1] // BLK

        @pl.when(me.among(devices) & (row <= line))
        def _():
            zero = jnp.zeros((BLK, BLK), jnp.float32)
            total = zero
            for a in range(row_blocks):
                for b in range(col_blocks):
                    i, j = row * row_blocks + a, (2 * line + core) * col_blocks + b
                    block = ref[a * BLK : (a + 1) * BLK, b * BLK : (b + 1) * BLK].astype(jnp.float32)
                    block = jnp.where((i <= j) & kept(pattern, i, j), block, zero)
                    total += jnp.where(i == j, 1.0, 2.0) * (block * block)
            lane = at_col == 8 * row + 2 * line + core
            out[...] += jnp.where((at_row == 1) & lane, jnp.sum(total) / order_size, 0.0)

            @pl.when(row == line)
            def _():
                rows_at = lax.broadcasted_iota(jnp.int32, (BLK, BLK), 0)
                cols_at = lax.broadcasted_iota(jnp.int32, (BLK, BLK), 1)
                diagonals = zero
                for b in range(col_blocks):
                    start = pl.multiple_of((core * col_blocks + b) * BLK, BLK)
                    block = ref[pl.ds(start, BLK), b * BLK : (b + 1) * BLK].astype(jnp.float32)
                    diagonals += jnp.where(rows_at == cols_at, block, zero)
                out[...] += jnp.where((at_row == 0) & lane, jnp.sum(diagonals) / order_size, 0.0)


def copy_kernel(source, out):
    out[...] = source[...]


def pack_kernel(*refs):
    out = refs[-1]
    for i, ref in enumerate(refs[:-1]):
        out[i] = ref[...]


def copy_kernel(source, out):
    out[...] = source[...]


def pack_kernel(*refs):
    out = refs[-1]
    for i, ref in enumerate(refs[:-1]):
        out[i] = ref[...]


def choose_kernel(sends, *refs):
    me = Place()
    held, outs = refs[:FIRST], refs[FIRST:]
    for out, send in zip(outs, sends):
        for s, ref in enumerate(held):
            devices = [d for d in send if send[d] == s]
            if devices:
                @pl.when(me.among(devices))
                def _():
                    out[...] = ref[...]


def pack_kernel(*refs):
    out = refs[-1]
    for i, ref in enumerate(refs[:-1]):
        out[i] = ref[...]


def place_tiles(uses, me, shards, keep, left, right, raw):
    tile, width = left.shape[0], right.shape[1]
    blocks, half_blocks = tile // BLK, width // BLK
    zero = jnp.zeros((BLK, BLK), left.dtype)

    def stored(a, b):
        return raw[(b // 2) * tile + a * BLK : (b // 2) * tile + (a + 1) * BLK, (b % 2) * BLK : (b % 2 + 1) * BLK]

    def direct(a, b):
        start = pl.multiple_of(me.core * tile + a * BLK, BLK)
        return raw[pl.ds(start, BLK), b * BLK : (b + 1) * BLK]

    def mirrored(a, b):
        start = pl.multiple_of((a // 2) * tile + (me.core * half_blocks + b) * BLK, BLK)
        return raw[pl.ds(start, BLK), (a % 2) * BLK : (a % 2 + 1) * BLK].T

    left_ways = (
        stored,
        lambda a, b: stored(b, a).T,
        lambda a, b: stored(a, b) if a <= b else stored(b, a).T,
    )
    right_ways = (
        direct,
        mirrored,
        lambda a, b: jnp.where(a <= me.core * half_blocks + b, direct(a, b), mirrored(a, b)),
    )

    def fill(panel, at, cols, u, block_of):
        j = u % 4
        for a in range(blocks):
            for b in range(cols):
                rows = slice(at[0] + a * BLK, at[0] + (a + 1) * BLK)
                lanes = slice(at[1] + b * BLK, at[1] + (b + 1) * BLK)
                if u < 4:
                    flag = keep(panel, rows, lanes, me.row * blocks + a, j * blocks + b)
                else:
                    flag = keep(panel, rows, lanes, j * blocks + a, me.col * half_blocks + b)
                panel[rows, lanes] = jnp.where(flag, block_of(a, b), zero)

    for u, here in enumerate(uses):
        j = u % 4
        panel, at, cols, ways = (left, (0, j * tile), blocks, left_ways) if u < 4 else (
            right, (j * tile, 0), half_blocks, right_ways)

        def index(d):
            return d // 8 if u < 4 else (d % 8) // 2

        def above(d):
            return 2 if index(d) == j else int((index(d) > j) == (u < 4))

        if here:
            @pl.when(me.among(here))
            def _():
                for half in range(2):
                    for s in sorted({here[d][half] for d in here}):
                        @pl.when(me.among([d for d in here if here[d][half] == s]))
                        def _():
                            raw[half * tile : (half + 1) * tile, :] = shards[s][...]

                for way in sorted({above(d) for d in here}):
                    @pl.when(me.among([d for d in here if above(d) == way]))
                    def _():
                        fill(panel, at, cols, u, ways[way])


def panels_kernel(uses, pattern, *refs):
    packed, left, right, keeps, raw = refs[FIRST:]
    me = Place()
    shards = list(refs[:FIRST]) + [packed.at[i] for i in range(FIRST)]

    def keep(panel, rows, lanes, i, j):
        return kept(pattern, i, j)

    place_tiles(uses[0], me, shards, keep, left, right, raw)
    tile, width = left.shape[0], right.shape[1]
    blocks, half_blocks = tile // BLK, width // BLK

    def flags(ref, row_at, col_at, cols, flag):
        for a in range(blocks):
            for b in range(cols):
                value = jnp.where(flag(a, b), 1.0, 0.0).astype(ref.dtype)
                ref[row_at + a * BLK : row_at + (a + 1) * BLK, col_at + b * BLK : col_at + (b + 1) * BLK] = (
                    jnp.full((BLK, BLK), value, ref.dtype)
                )

    for u, later in enumerate(uses[1]):
        j = u % 4
        if later:
            @pl.when(me.among(later))
            def _():
                if u < 4:
                    flags(left, 0, j * tile, blocks, lambda a, b: kept(pattern, me.row * blocks + a, j * blocks + b))
                else:
                    flags(
                        right, j * tile, 0, half_blocks,
                        lambda a, b: kept(pattern, j * blocks + a, me.col * half_blocks + b),
                    )

    def square_kept(a, b):
        i, j = me.row * blocks + a, me.col * half_blocks + b
        return (i <= j) & kept(pattern, i, j)

    flags(keeps, 0, 0, half_blocks, square_kept)


def grid_product_kernel(uses, *refs):
    shards = refs[: 2 * SECOND]
    keeps, _, _, left, right, out, raw, result, sems = refs[2 * SECOND :]
    me = Place()

    def keep(panel, rows, lanes, i, j):
        return panel[rows, lanes] != 0

    place_tiles(uses[1], me, shards, keep, left, right, raw)
    height = out.shape[0]
    part = height // 2
    copies = []
    for c in range(2):
        rows = pl.ds(c * part, part)

        @pl.when(me.row <= me.line)
        def _():
            product = jnp.dot(left[rows, :], right[...], preferred_element_type=jnp.float32)
            result[rows, :] = jnp.where(
                keeps[rows, :].astype(jnp.float32) != 0, product, jnp.zeros_like(product)
            ).astype(result.dtype)

        @pl.when(me.row > me.line)
        def _():
            result[rows, :] = jnp.zeros((part, result.shape[1]), result.dtype)

        copies.append(pltpu.make_async_copy(result.at[rows], out.at[rows], sems.at[c]))
        copies[-1].start()
    for copy in copies:
        copy.wait()


def chip_grid(density, pattern):
    height, width = density.shape
    n_col = lax.axis_size("col")
    n_devices = lax.axis_size("row") * n_col
    order_size = width * lax.axis_size("col")
    dtype = density.dtype
    axes = ("row", "col")
    first, second, sends, adds, uses = schedule()
    shard = jax.ShapeDtypeStruct(density.shape, dtype)
    raw = pltpu.VMEM((2 * height, width), dtype)
    panels = [
        jax.ShapeDtypeStruct((height, order_size), dtype),
        jax.ShapeDtypeStruct((order_size, width), dtype),
    ]

    def call(kernel, out_shape, smem, args, scratch=(), out_specs=VMEM, aliases=None, cost=None):
        return pl.pallas_call(
            kernel,
            out_shape=out_shape,
            in_specs=[SMEM] * smem + [VMEM] * (len(args) - smem),
            out_specs=out_specs,
            scratch_shapes=list(scratch),
            input_output_aliases=aliases or {},
            compiler_params=GRID_PARAMS,
            cost_estimate=cost,
        )(*args)

    def share(value):
        return lax.ppermute(value, axes, [(d, d ^ 1) for d in range(n_devices)])

    def part_from(parts, row_bits, col_bits):
        return lax.ppermute(parts, axes, [(d, d ^ (row_bits * n_col + col_bits)) for d in range(n_devices)])

    came = [lax.ppermute(density, axes, pairs) for pairs in first]
    came[0], own = lax.optimization_barrier((came[0], call(copy_kernel, shard, 0, [density])))
    held = [own] + came
    chosen = call(functools.partial(choose_kernel, sends), [shard] * SECOND, 0, held, (), [VMEM] * SECOND)
    tied = lax.optimization_barrier((*chosen, *held))
    chosen, held = tied[:SECOND], list(tied[SECOND:])
    later = [lax.ppermute(value, axes, pairs) for value, pairs in zip(chosen, second)]
    packed = share(call(pack_kernel, jax.ShapeDtypeStruct((FIRST, height, width), dtype), 0, held))
    parts = call(
        functools.partial(partial_kernel, adds, order_size),
        jax.ShapeDtypeStruct((8, 128), jnp.float32),
        1,
        [pattern] + held + [packed],
    )
    packed, parts = lax.optimization_barrier((packed, parts))
    received = part_from(parts, 3, 2)
    left, right, keeps = call(
        functools.partial(panels_kernel, uses), panels + [shard], 1, [pattern] + held + [packed], [raw], [VMEM] * 3
    )
    left, parts = lax.optimization_barrier((left, parts + received))
    received = part_from(parts, 0, 4)
    left, parts = lax.optimization_barrier((left, parts))
    shared = []
    for i in range(SECOND):
        later[i], left = lax.optimization_barrier((later[i], left))
        shared.append(share(later[i]))
    inputs = later + shared + [keeps, left, right]
    square = call(
        functools.partial(grid_product_kernel, uses),
        panels + [shard],
        0,
        inputs,
        [raw, pltpu.VMEM(density.shape, dtype), pltpu.SemaphoreType.DMA((2,))],
        [VMEM, VMEM, pl.BlockSpec(memory_space=pltpu.HBM)],
        {len(inputs) - 2: 0, len(inputs) - 1: 1},
    )[2]
    square, received = lax.optimization_barrier((square, received))
    traces = jnp.sum(parts[:2] + received[:2], axis=1)
    return (square, traces)


def per_device(density, pattern):
    if lax.axis_size("row") == 4 and lax.axis_size("col") == 8 and density.shape[0] == 2 * density.shape[1]:
        return chip_grid(density, pattern)
    return any_mesh(density, pattern)


def solution(mesh):
    placed = (P("row", "col"), P())
    return jax.shard_map(
        per_device, mesh=mesh, in_specs=placed, out_specs=(P("row", "col"), P()), check_vma=False
    )
```

```python
import functools
import jax
import jax.numpy as jnp
from jax import lax
from jax.experimental import pallas as pl
from jax.experimental.pallas import tpu as pltpu
from jax.sharding import PartitionSpec as P

BLK = 128
VMEM = pl.BlockSpec(memory_space=pltpu.VMEM)
SMEM = pl.BlockSpec(memory_space=pltpu.SMEM)
PARAMS = pltpu.CompilerParams(vmem_limit_bytes=40 * 2**20)


def symmetric_kernel(sub, place, pattern, density, *rest):
    pieces, full = rest[:sub], rest[sub]
    row, col = place[0], place[1]
    height, width = density.shape
    per_piece = width // BLK
    row_blocks = height // BLK
    own_slot = lax.rem(col, sub)
    on_diagonal = row == col // sub
    for t in range(sub):
        slot = lax.rem(own_slot + sub - t, sub)
        for a in range(per_piece):
            i = slot * per_piece + a
            block_row = row * row_blocks + i
            rows = pl.ds(pl.multiple_of(i * BLK, BLK), BLK)
            for b in range(per_piece):
                block_col = col * per_piece + b
                cols = pl.ds(b * BLK, BLK)
                mirror = pieces[t][b * BLK : (b + 1) * BLK, a * BLK : (a + 1) * BLK]
                if t == 0:
                    start = pl.multiple_of((own_slot * per_piece + b) * BLK, BLK)
                    mine = density[pl.ds(start, BLK), a * BLK : (a + 1) * BLK]
                    mirror = jnp.where(on_diagonal, mine, mirror)
                chosen = pattern[jnp.minimum(block_row, block_col), jnp.maximum(block_row, block_col)] != 0
                upper = (block_row == block_col) | ((block_row < block_col) & chosen)
                lower = (block_row > block_col) & chosen
                zero = jnp.zeros((BLK, BLK), full.dtype)
                value = jnp.where(lower, mirror.T, zero)
                full[rows, cols] = jnp.where(upper, density[rows, cols], value)


def product_kernel(lines, planes, place, pattern, *refs):
    left = refs[: 2 * lines]
    right = refs[2 * lines : 2 * lines + planes]
    out, panel = refs[2 * lines + planes :]
    row, col = place[0], place[1]
    height, width = out.shape
    core, line = lax.rem(col, 2), col // 2
    for d in range(planes):
        start = pl.multiple_of((row ^ d) * height, height)
        panel[pl.ds(start, height), :] = right[d][...]
    total = jnp.zeros((height, width), jnp.float32)
    for e in range(lines):
        for s in range(2):
            start = pl.multiple_of(((line ^ e) * 2 + (core ^ s)) * width, width)
            total += jnp.dot(
                left[2 * e + s][...],
                panel[pl.ds(start, width), :],
                preferred_element_type=jnp.float32,
            )
    for i in range(height // BLK):
        for j in range(width // BLK):
            block_row = row * (height // BLK) + i
            block_col = col * (width // BLK) + j
            kept = (block_row == block_col) | ((block_row < block_col) & (pattern[block_row, block_col] != 0))
            block = total[i * BLK : (i + 1) * BLK, j * BLK : (j + 1) * BLK]
            out[i * BLK : (i + 1) * BLK, j * BLK : (j + 1) * BLK] = jnp.where(
                kept, block, jnp.zeros_like(block)
            ).astype(out.dtype)


def block_weights(pattern, row, col, row_blocks, col_blocks):
    block_rows = row * row_blocks + jnp.arange(row_blocks)
    block_cols = col * col_blocks + jnp.arange(col_blocks)
    chosen = lax.dynamic_slice(pattern, (row * row_blocks, col * col_blocks), (row_blocks, col_blocks))
    diagonal = block_rows[:, None] == block_cols[None, :]
    strict = (block_cols[None, :] > block_rows[:, None]) & (chosen != 0)
    return jnp.where(diagonal, 1.0, jnp.where(strict, 2.0, 0.0)).astype(jnp.float32)


def any_mesh(density, pattern):
    n_row = lax.axis_size("row")
    n_col = lax.axis_size("col")
    sub = n_col // n_row
    row = lax.axis_index("row")
    col = lax.axis_index("col")
    height, width = density.shape
    order_size = width * n_col
    place = jnp.stack([row, col]).astype(jnp.int32)

    pieces = []
    for t in range(sub):
        pairs = []
        for q in range(n_row):
            for c in range(n_col):
                p = (c + t) % sub
                if c > q * sub + p:
                    pairs.append((q * n_col + c, (c // sub) * n_col + q * sub + p))
        start = lax.rem(col + t, sub) * width
        piece = lax.dynamic_slice_in_dim(density, start, width, 0)
        pieces.append(lax.ppermute(piece, ("row", "col"), pairs))
    full = pl.pallas_call(
        functools.partial(symmetric_kernel, sub),
        out_shape=jax.ShapeDtypeStruct(density.shape, density.dtype),
        in_specs=[SMEM, SMEM] + [VMEM] * (sub + 1),
        out_specs=VMEM,
        compiler_params=PARAMS,
    )(place, pattern, density, *pieces)

    weights = block_weights(pattern, row, col, height // BLK, width // BLK)
    values = density.astype(jnp.float32).reshape(height // BLK, BLK, width // BLK, BLK)
    squares = jnp.sum(values * values, axis=(1, 3))
    rows_at = row * height + jnp.arange(height)[:, None]
    cols_at = col * width + jnp.arange(width)[None, :]
    diagonal = jnp.where(rows_at == cols_at, density.astype(jnp.float32), 0.0)
    sums = jnp.stack([jnp.sum(diagonal), jnp.sum(jnp.where(weights > 0, weights * squares, 0.0))])
    step = 1
    while step < n_row:
        sums = sums + lax.ppermute(sums, "row", [(i, i ^ step) for i in range(n_row)])
        step *= 2
    step = 1
    while step < n_col:
        sums = sums + lax.ppermute(sums, "col", [(i, i ^ step) for i in range(n_col)])
        step *= 2
    traces = sums / order_size

    right = [full]
    for d in range(1, n_row):
        right.append(lax.ppermute(full, "row", [(i, i ^ d) for i in range(n_row)]))
    left = []
    for e in range(n_col // 2):
        shard = full
        if e > 0:
            shard = lax.ppermute(full, "col", [(i, i ^ (2 * e)) for i in range(n_col)])
        other = lax.ppermute(shard, "col", [(i, i ^ 1) for i in range(n_col)])
        left += [shard, other]
    square = pl.pallas_call(
        functools.partial(product_kernel, n_col // 2, n_row),
        out_shape=jax.ShapeDtypeStruct(density.shape, density.dtype),
        in_specs=[SMEM, SMEM] + [VMEM] * (len(left) + len(right)),
        out_specs=VMEM,
        scratch_shapes=[pltpu.VMEM((order_size, width), density.dtype)],
        compiler_params=PARAMS,
    )(place, pattern, *left, *right)
    return (square, traces)

GRID_PARAMS = pltpu.CompilerParams(vmem_limit_bytes=14 * 2**20)
USES = 8
FIRST = 5
SECOND = 3
HEARD = (
    ((2, 0), (0, 3), (0, 1), (1, 3), (0, 2), (3, 0), (3, 2), (1, 0), (0, 0), (2, 3), (2, 1), (3, 3), (3, 1), (1, 1), (1, 2), (2, 2)),
    ((3, 0), (3, 2), (2, 2), (1, 3), (0, 0), (1, 0), (0, 3), (1, 1), (2, 1), (1, 2), (0, 1), (0, 2), (3, 3), (2, 0), (2, 3), (3, 1)),
)
LAST_HEARD = ((0, 1), (0, 0), (0, 3), (0, 2), (3, 0), (1, 2), (1, 1), (3, 3), (2, 1), (2, 0), (2, 3), (2, 2), (1, 0), (3, 2), (3, 1), (1, 3))
MESSAGES = (
    (0, (0, 0), 1, (0, 0, 1), (0, 3, 1)),
    (0, (0, 2), 0, (0, 1, 0), (0, 0, 0)),
    (0, (2, 2), 0, (0, 2, 0), (1, 2, 1)),
    (0, (0, 3), 1, (0, 2, 1), (0, 0, 1)),
    (0, (2, 3), 0, (0, 3, 0), (0, 2, 0)),
    (0, (0, 2), 1, (0, 3, 1), (2, 3, 1)),
    (0, (0, 0), 1, (1, 0, 1), (0, 2, 1)),
    (0, (1, 1), 0, (1, 2, 0), (1, 3, 0)),
    (0, (1, 3), 1, (1, 2, 1), (0, 1, 0)),
    (0, (1, 2), 0, (1, 3, 0), (2, 2, 0)),
    (0, (0, 1), 1, (2, 1, 1), (0, 3, 0)),
    (0, (0, 2), 0, (2, 2, 0), (2, 3, 0)),
    (0, (0, 3), 0, (2, 3, 0), (0, 1, 1)),
    (0, (1, 1), 1, (3, 1, 1), (1, 3, 1)),
    (0, (2, 2), 1, (3, 2, 1), (1, 2, 0)),
    (0, (1, 3), 1, (3, 3, 1), (1, 1, 1)),
    (1, (0, 0), 0, (0, 1, 0), (0, 3, 1)),
    (1, (0, 3), 0, (0, 2, 0), (0, 0, 0)),
    (1, (2, 3), 1, (0, 3, 1), (1, 3, 0)),
    (1, (0, 1), 1, (1, 1, 1), (1, 3, 1)),
    (1, (1, 3), 0, (1, 2, 0), (0, 1, 1)),
    (1, (1, 2), 0, (1, 3, 0), (2, 3, 0)),
    (1, (0, 0), 0, (2, 0, 0), (0, 2, 0)),
    (1, (0, 1), 0, (2, 1, 0), (0, 3, 0)),
    (1, (0, 2), 1, (2, 2, 1), (0, 0, 1)),
    (1, (0, 3), 0, (2, 3, 0), (3, 3, 1)),
    (1, (1, 2), 0, (3, 2, 0), (0, 1, 0)),
    (1, (1, 2), 1, (3, 2, 1), (2, 3, 1)),
    (1, (2, 3), 0, (3, 3, 0), (1, 2, 0)),
    (1, (2, 3), 1, (3, 3, 1), (1, 2, 1)),
    (2, (0, 1), 1, (0, 1, 1), (1, 2, 1)),
    (2, (0, 1), 0, (0, 2, 0), (1, 2, 0)),
    (2, (1, 3), 0, (0, 3, 0), (2, 3, 0)),
    (2, (0, 3), 1, (0, 3, 1), (0, 1, 0)),
    (2, (0, 1), 0, (1, 1, 0), (1, 3, 0)),
    (2, (1, 2), 1, (1, 1, 1), (0, 1, 1)),
    (2, (1, 3), 0, (1, 2, 0), (1, 1, 1)),
    (2, (3, 3), 0, (1, 3, 0), (0, 3, 0)),
    (2, (3, 3), 1, (1, 3, 1), (0, 3, 1)),
    (2, (2, 3), 1, (2, 2, 1), (0, 2, 1)),
    (2, (2, 3), 0, (2, 3, 0), (1, 3, 1)),
    (2, (0, 3), 1, (2, 3, 1), (3, 3, 0)),
    (2, (1, 2), 1, (3, 2, 1), (2, 2, 0)),
    (2, (1, 3), 1, (3, 3, 1), (2, 3, 1)),
)


def number(device):
    return 8 * device[0] + 2 * device[1] + device[2]


def wanted(r, z):
    if r > z:
        return [None] * USES
    return [(min(r, j), max(r, j)) for j in range(4)] + [(min(z, j), max(z, j)) for j in range(4)]


def first_round(devices):
    def ring(r, z, k, up):
        step = 1 if (k == 0) == up else -1
        return (r, z + step, k) if 0 <= z + step < 4 else (r, z, 1 - k)

    return [[(d, ring(*d, up)) for d in devices] for up in (True, False)] + [
        [((r, z, k), (r ^ bit, z, k)) for r, z, k in devices] for bit in (1, 2)
    ]


def closed(pairs, devices):
    sends, receives = {a for a, _ in pairs}, {b for _, b in pairs}
    ends = [d for d in devices if d not in sends]
    starts = [d for d in devices if d not in receives]

    def cost(a, b):
        return 1000 if a == b else (abs(a[1] - b[1]) + bin(a[0] ^ b[0]).count("1")) ** 2

    size = len(ends)
    u, v, row_of = [0] * (size + 1), [0] * (size + 1), [0] * (size + 1)
    for i in range(1, size + 1):
        row_of[0], col = i, 0
        least, before, done = [10**6] * (size + 1), [0] * (size + 1), [False] * (size + 1)
        while row_of[col]:
            done[col], row, delta, following = True, row_of[col], 10**6, 0
            for j in range(1, size + 1):
                if not done[j]:
                    slack = cost(ends[row - 1], starts[j - 1]) - u[row] - v[j]
                    if slack < least[j]:
                        least[j], before[j] = slack, col
                    if least[j] < delta:
                        delta, following = least[j], j
            for j in range(size + 1):
                if done[j]:
                    u[row_of[j]] += delta
                    v[j] -= delta
                else:
                    least[j] -= delta
            col = following
        while col:
            row_of[col] = row_of[before[col]]
            col = before[col]
    return pairs + [(ends[row_of[j] - 1], starts[j - 1]) for j in range(1, size + 1)]


def trace_pairs():
    chips = [(r, z) for r in range(4) for z in range(4)]

    def near(c):
        return {d for d in chips if abs(c[1] - d[1]) + bin(c[0] ^ d[0]).count("1") <= 1}

    known = {c: near(c) | near(HEARD[0][i]) | near(HEARD[1][i]) for i, c in enumerate(chips)}
    for i, c in enumerate(chips):
        assert known[c] | known[LAST_HEARD[i]] >= {d for d in chips if d[0] <= d[1]}

    def on_cores(sources):
        return [(number((*sources[i], k)), number((*c, k))) for i, c in enumerate(chips) for k in range(2)]

    return [on_cores(sources) for sources in HEARD], on_cores(LAST_HEARD)


def schedule():
    devices = [(r, z, k) for r in range(4) for z in range(4) for k in range(2)]
    first = first_round(devices)
    held = {d: [((d[0], d[1]), d[2])] for d in devices}
    for pairs in first:
        for a, b in pairs:
            held[b].append(((a[0], a[1]), a[2]))
    second = [[] for _ in range(SECOND)]
    later = {d: [None] * SECOND for d in devices}
    sends = [{} for _ in range(SECOND)]
    for i, tile, half, a, b in MESSAGES:
        second[i].append((a, b))
        sends[i][number(a)] = held[a].index((tile, half))
        later[b][i] = (tile, half)
    second = [closed(pairs, devices) for pairs in second]
    adds = [set() for _ in range(FIRST)]
    uses = [[{} for _ in range(USES)] for _ in range(2)]
    for d in devices:
        r, z, k = d
        for s, (tile, half) in enumerate(held[d]):
            if half == k and (s == 0 or tile != (r, z)):
                adds[s].add(number(d))
        for u, tile in enumerate(wanted(r, z)):
            for n, shards in enumerate((held, later)):
                here = shards[d] + shards[r, z, 1 - k]
                if tile and (tile, 0) in here and (tile, 1) in here and not any(number(d) in uses[m][u] for m in range(n)):
                    uses[n][u][number(d)] = (here.index((tile, 0)), here.index((tile, 1)))
            assert tile is None or any(number(d) in uses[n][u] for n in range(2))

    def flat(pairs):
        assert len({a for a, _ in pairs}) == len({b for _, b in pairs}) == len(devices)
        return [(number(a), number(b)) for a, b in pairs]

    return [flat(p) for p in first], [flat(p) for p in second], sends, adds, uses


class Place:
    def __init__(self):
        self.row, self.col = lax.axis_index("row"), lax.axis_index("col")
        self.line, self.core = self.col // 2, lax.rem(self.col, 2)
        self.number = self.row * 8 + self.col

    def among(self, devices):
        bits = sum(1 << d for d in devices)
        bits -= (bits >> 31) << 32
        return (lax.shift_right_logical(jnp.int32(bits), self.number) & 1) == 1


def kept(pattern, i, j):
    low, high = jnp.minimum(i, j), jnp.maximum(i, j)
    return (low == high) | (pattern[low, high] != 0)


def partial_kernel(adds, order_size, pattern, *refs):
    me = Place()
    packed, out = refs[FIRST:]
    out[...] = jnp.zeros_like(out)
    at_row = lax.broadcasted_iota(jnp.int32, out.shape, 0)
    at_col = lax.broadcasted_iota(jnp.int32, out.shape, 1)
    both = [(refs[s], s, 0) for s in range(FIRST)] + [(packed.at[s], s, 1) for s in range(FIRST)]
    for ref, s, other in both:
        devices = {d ^ other for d in adds[s]}
        core = me.core ^ other
        before, after = me.line - 1 + 2 * core, me.line + 1 - 2 * core
        row = (me.row, me.row, me.row, me.row ^ 1, me.row ^ 2)[s]
        line = (me.line, before, after, me.line, me.line)[s]
        row_blocks, col_blocks = ref.shape[0] // BLK, ref.shape[1] // BLK

        @pl.when(me.among(devices) & (row <= line))
        def _():
            zero = jnp.zeros((BLK, BLK), jnp.float32)
            total = zero
            for a in range(row_blocks):
                for b in range(col_blocks):
                    i, j = row * row_blocks + a, (2 * line + core) * col_blocks + b
                    block = ref[a * BLK : (a + 1) * BLK, b * BLK : (b + 1) * BLK].astype(jnp.float32)
                    block = jnp.where((i <= j) & kept(pattern, i, j), block, zero)
                    total += jnp.where(i == j, 1.0, 2.0) * (block * block)
            lane = at_col == 8 * row + 2 * line + core
            out[...] += jnp.where((at_row == 1) & lane, jnp.sum(total) / order_size, 0.0)

            @pl.when(row == line)
            def _():
                rows_at = lax.broadcasted_iota(jnp.int32, (BLK, BLK), 0)
                cols_at = lax.broadcasted_iota(jnp.int32, (BLK, BLK), 1)
                diagonals = zero
                for b in range(col_blocks):
                    start = pl.multiple_of((core * col_blocks + b) * BLK, BLK)
                    block = ref[pl.ds(start, BLK), b * BLK : (b + 1) * BLK].astype(jnp.float32)
                    diagonals += jnp.where(rows_at == cols_at, block, zero)
                out[...] += jnp.where((at_row == 0) & lane, jnp.sum(diagonals) / order_size, 0.0)


def copy_kernel(source, out):
    out[...] = source[...]


def pack_kernel(*refs):
    out = refs[-1]
    for i, ref in enumerate(refs[:-1]):
        out[i] = ref[...]


def copy_kernel(source, out):
    out[...] = source[...]


def pack_kernel(*refs):
    out = refs[-1]
    for i, ref in enumerate(refs[:-1]):
        out[i] = ref[...]


def choose_kernel(sends, *refs):
    me = Place()
    held, outs = refs[:FIRST], refs[FIRST:]
    for out, send in zip(outs, sends):
        for s, ref in enumerate(held):
            devices = [d for d in send if send[d] == s]
            if devices:
                @pl.when(me.among(devices))
                def _():
                    out[...] = ref[...]


def pack_kernel(*refs):
    out = refs[-1]
    for i, ref in enumerate(refs[:-1]):
        out[i] = ref[...]


def place_tiles(uses, me, shards, keep, left, right, raw):
    tile, width = left.shape[0], right.shape[1]
    blocks, half_blocks = tile // BLK, width // BLK
    zero = jnp.zeros((BLK, BLK), left.dtype)

    def stored(a, b):
        return raw[(b // 2) * tile + a * BLK : (b // 2) * tile + (a + 1) * BLK, (b % 2) * BLK : (b % 2 + 1) * BLK]

    def direct(a, b):
        start = pl.multiple_of(me.core * tile + a * BLK, BLK)
        return raw[pl.ds(start, BLK), b * BLK : (b + 1) * BLK]

    def mirrored(a, b):
        start = pl.multiple_of((a // 2) * tile + (me.core * half_blocks + b) * BLK, BLK)
        return raw[pl.ds(start, BLK), (a % 2) * BLK : (a % 2 + 1) * BLK].T

    left_ways = (
        stored,
        lambda a, b: stored(b, a).T,
        lambda a, b: stored(a, b) if a <= b else stored(b, a).T,
    )
    right_ways = (
        direct,
        mirrored,
        lambda a, b: jnp.where(a <= me.core * half_blocks + b, direct(a, b), mirrored(a, b)),
    )

    def fill(panel, at, cols, u, block_of):
        j = u % 4
        for a in range(blocks):
            for b in range(cols):
                rows = slice(at[0] + a * BLK, at[0] + (a + 1) * BLK)
                lanes = slice(at[1] + b * BLK, at[1] + (b + 1) * BLK)
                if u < 4:
                    flag = keep(panel, rows, lanes, me.row * blocks + a, j * blocks + b)
                else:
                    flag = keep(panel, rows, lanes, j * blocks + a, me.col * half_blocks + b)
                panel[rows, lanes] = jnp.where(flag, block_of(a, b), zero)

    for u, here in enumerate(uses):
        j = u % 4
        panel, at, cols, ways = (left, (0, j * tile), blocks, left_ways) if u < 4 else (
            right, (j * tile, 0), half_blocks, right_ways)

        def index(d):
            return d // 8 if u < 4 else (d % 8) // 2

        def above(d):
            return 2 if index(d) == j else int((index(d) > j) == (u < 4))

        if here:
            @pl.when(me.among(here))
            def _():
                for half in range(2):
                    for s in sorted({here[d][half] for d in here}):
                        @pl.when(me.among([d for d in here if here[d][half] == s]))
                        def _():
                            raw[half * tile : (half + 1) * tile, :] = shards[s][...]

                for way in sorted({above(d) for d in here}):
                    @pl.when(me.among([d for d in here if above(d) == way]))
                    def _():
                        fill(panel, at, cols, u, ways[way])


def panels_kernel(uses, pattern, *refs):
    packed, left, right, keeps, raw = refs[FIRST:]
    me = Place()
    shards = list(refs[:FIRST]) + [packed.at[i] for i in range(FIRST)]

    def keep(panel, rows, lanes, i, j):
        return kept(pattern, i, j)

    place_tiles(uses[0], me, shards, keep, left, right, raw)
    tile, width = left.shape[0], right.shape[1]
    blocks, half_blocks = tile // BLK, width // BLK

    def flags(ref, row_at, col_at, cols, flag):
        for a in range(blocks):
            for b in range(cols):
                value = jnp.where(flag(a, b), 1.0, 0.0).astype(ref.dtype)
                ref[row_at + a * BLK : row_at + (a + 1) * BLK, col_at + b * BLK : col_at + (b + 1) * BLK] = (
                    jnp.full((BLK, BLK), value, ref.dtype)
                )

    for u, later in enumerate(uses[1]):
        j = u % 4
        if later:
            @pl.when(me.among(later))
            def _():
                if u < 4:
                    flags(left, 0, j * tile, blocks, lambda a, b: kept(pattern, me.row * blocks + a, j * blocks + b))
                else:
                    flags(
                        right, j * tile, 0, half_blocks,
                        lambda a, b: kept(pattern, j * blocks + a, me.col * half_blocks + b),
                    )

    def square_kept(a, b):
        i, j = me.row * blocks + a, me.col * half_blocks + b
        return (i <= j) & kept(pattern, i, j)

    flags(keeps, 0, 0, half_blocks, square_kept)


def grid_product_kernel(uses, *refs):
    shards = refs[: 2 * SECOND]
    keeps, _, _, left, right, out, raw, result, sems = refs[2 * SECOND :]
    me = Place()

    def keep(panel, rows, lanes, i, j):
        return panel[rows, lanes] != 0

    place_tiles(uses[1], me, shards, keep, left, right, raw)
    height = out.shape[0]
    part = height // 2
    copies = []
    for c in range(2):
        rows = pl.ds(c * part, part)

        @pl.when(me.row <= me.line)
        def _():
            product = jnp.dot(left[rows, :], right[...], preferred_element_type=jnp.float32)
            result[rows, :] = jnp.where(
                keeps[rows, :].astype(jnp.float32) != 0, product, jnp.zeros_like(product)
            ).astype(result.dtype)

        @pl.when(me.row > me.line)
        def _():
            result[rows, :] = jnp.zeros((part, result.shape[1]), result.dtype)

        copies.append(pltpu.make_async_copy(result.at[rows], out.at[rows], sems.at[c]))
        copies[-1].start()
    for copy in copies:
        copy.wait()


def chip_grid(density, pattern):
    height, width = density.shape
    n_col = lax.axis_size("col")
    n_devices = lax.axis_size("row") * n_col
    order_size = width * lax.axis_size("col")
    dtype = density.dtype
    axes = ("row", "col")
    first, second, sends, adds, uses = schedule()
    shard = jax.ShapeDtypeStruct(density.shape, dtype)
    raw = pltpu.VMEM((2 * height, width), dtype)
    panels = [
        jax.ShapeDtypeStruct((height, order_size), dtype),
        jax.ShapeDtypeStruct((order_size, width), dtype),
    ]

    def call(kernel, out_shape, smem, args, scratch=(), out_specs=VMEM, aliases=None, cost=None):
        return pl.pallas_call(
            kernel,
            out_shape=out_shape,
            in_specs=[SMEM] * smem + [VMEM] * (len(args) - smem),
            out_specs=out_specs,
            scratch_shapes=list(scratch),
            input_output_aliases=aliases or {},
            compiler_params=GRID_PARAMS,
            cost_estimate=cost,
        )(*args)

    def share(value):
        return lax.ppermute(value, axes, [(d, d ^ 1) for d in range(n_devices)])

    def merge(parts, others):
        return jnp.where(parts != 0, parts, others)

    came = [lax.ppermute(density, axes, pairs) for pairs in first]
    came[0], own = lax.optimization_barrier((came[0], call(copy_kernel, shard, 0, [density])))
    held = [own] + came
    chosen = call(functools.partial(choose_kernel, sends), [shard] * SECOND, 0, held, (), [VMEM] * SECOND)
    tied = lax.optimization_barrier((*chosen, *held))
    chosen, held = tied[:SECOND], list(tied[SECOND:])
    later = [lax.ppermute(value, axes, pairs) for value, pairs in zip(chosen, second)]
    packed = share(call(pack_kernel, jax.ShapeDtypeStruct((FIRST, height, width), dtype), 0, held))
    parts = call(
        functools.partial(partial_kernel, adds, order_size),
        jax.ShapeDtypeStruct((8, 128), jnp.float32),
        1,
        [pattern] + held + [packed],
    )
    packed, parts = lax.optimization_barrier((packed, parts))
    early, late = trace_pairs()
    received = [lax.ppermute(parts, axes, pairs) for pairs in early]
    left, right, keeps = call(
        functools.partial(panels_kernel, uses), panels + [shard], 1, [pattern] + held + [packed], [raw], [VMEM] * 3
    )
    left, parts = lax.optimization_barrier((left, merge(parts, merge(*received))))
    received = lax.ppermute(parts, axes, late)
    shared = []
    for i in range(SECOND):
        later[i], left = lax.optimization_barrier((later[i], left))
        shared.append(share(later[i]))
    inputs = later + shared + [keeps, left, right]
    square = call(
        functools.partial(grid_product_kernel, uses),
        panels + [shard],
        0,
        inputs,
        [raw, pltpu.VMEM(density.shape, dtype), pltpu.SemaphoreType.DMA((2,))],
        [VMEM, VMEM, pl.BlockSpec(memory_space=pltpu.HBM)],
        {len(inputs) - 2: 0, len(inputs) - 1: 1},
    )[2]
    square, received = lax.optimization_barrier((square, received))
    traces = jnp.sum(merge(parts[:2], received[:2]), axis=1)
    return (square, traces)


def per_device(density, pattern):
    if lax.axis_size("row") == 4 and lax.axis_size("col") == 8 and density.shape[0] == 2 * density.shape[1]:
        return chip_grid(density, pattern)
    return any_mesh(density, pattern)


def solution(mesh):
    placed = (P("row", "col"), P())
    return jax.shard_map(
        per_device, mesh=mesh, in_specs=placed, out_specs=(P("row", "col"), P()), check_vma=False
    )
```
